256 devices in a mesh: grp: 8 (over y, core), dev: 32 (over z, x).
Axes of the slice: x: 4, y: 4, z: 8, core: 2. Of those that a mesh axis runs over, the one named last changes fastest.
Arguments:
- segments: float32 [9, 524288], P(None, ('grp', 'dev')), may hold values from -6 to 6
- pair_blocks: int32 [8192, 2], P(('grp', 'dev')), may hold values from -1 to 511, as said below
- block_cells: int32 [4096], P(('grp', 'dev')), may hold values from 0 to 255, as said below
- mobility: float32 [524288], P(('grp', 'dev')), may hold values from 0.5 to 3
- cell_centers: float32 [3, 256], replicated, may hold values from -2 to 2
Outputs:
- forces: float32 [3, 524288], P(None, ('grp', 'dev'))
- displacement: float32 [3, 524288], P(None, ('grp', 'dev'))
The draws below stay inside these ranges and needn't reach their ends.
Inputs may be any that keep to these rules, and one draw needn't show every extreme that they name: `pair_blocks`: A device's 32 slots list its valid pairs first, each of two different group-local blocks, and then rows of -1 in both columns; every device has one valid pair or more, and in each group one device's slots are all valid. `block_cells`: block k lies in a cell of its own group: from (k // 512) * 32 to (k // 512 + 1) * 32 - 1.
All inputs are finite; a program needn't handle non-finite values.
Results may differ from the reference program's by a relative error of at most 0.0003.
Values sent between devices are 32-bit elements; how exact they have to be, the bound alone decides.
No kernel may reach another device: no remote copies, remote signals or barrier semaphores. Data moves between devices by JAX's collectives and lax.ppermute only.
A program may use at most 128 MiB of HBM per device.

```python
import jax
import jax.numpy as jnp
from jax import lax

BLK = 128
PAIR_DEV = 32
CELL_GRP = 32
BLK_GRP = 512
SEG_GRP = 65536
PAIR_GRP = 1024
NBLOCKS = 4096
SEGS = 524288
NCELL = 256
N_GRP = 8
N_DEV = 32
DEVICES = 256


def draw_pair_blocks(key, part):
    key = jax.random.fold_in(key, 11)
    keys = jax.random.split(key, 4)
    raw = jax.random.randint(keys[0], (DEVICES,), 0, PAIR_DEV)
    counts = raw * raw // PAIR_DEV + 1
    fullest = jax.random.randint(keys[1], (N_GRP,), 0, N_DEV)
    dev_ids = jnp.arange(DEVICES) % N_DEV
    grp_ids = jnp.arange(DEVICES) // N_DEV
    counts = jnp.where(dev_ids == fullest[grp_ids], PAIR_DEV, counts)
    first = jax.random.randint(keys[2], (DEVICES, PAIR_DEV), 0, BLK_GRP)
    second = (first + 1 + jax.random.randint(keys[3], (DEVICES, PAIR_DEV), 0, BLK_GRP - 1)) % BLK_GRP
    live = jnp.arange(PAIR_DEV)[None, :] < counts[:, None]
    pairs = jnp.stack([jnp.where(live, first, -1), jnp.where(live, second, -1)], axis=-1)
    return pairs.reshape(DEVICES * PAIR_DEV, 2).astype(jnp.int32)


def draw_block_cells(key, part):
    key = jax.random.fold_in(key, 23)
    groups = jnp.arange(NBLOCKS) // BLK_GRP
    local = jax.random.randint(key, (NBLOCKS,), 0, CELL_GRP)
    return (groups * CELL_GRP + local).astype(jnp.int32)


def draw_mobility(key, part):
    key = jax.random.fold_in(key, 37)
    ramp = 1.0 + 2.0 * jnp.arange(SEGS, dtype=jnp.float32) / SEGS
    base = jnp.exp(jax.random.uniform(key, (SEGS,), jnp.float32, jnp.log(0.5), 0.0))
    return (base * ramp).astype(jnp.float32)


def levels(rng, shape, cuts, low, top_value):
    def one(dim, shards_of):
        steps = jax.random.uniform(jax.random.fold_in(jax.random.fold_in(rng, 6), dim), (shards_of,), jnp.float32, low / len(cuts), top_value / len(cuts))
        return jnp.repeat(jnp.exp(steps), shape[dim] // shards_of).reshape((-1,) + (1,) * (len(shape) - dim - 1))

    factor_of = one(*cuts[0])
    for cut in cuts[1:]:
        factor_of = factor_of * one(*cut)
    return factor_of


def normal_values(rng, dims, scale, reach, cuts=(), kind=jnp.bfloat16):
    array = jax.random.normal(rng, dims, jnp.float32) * scale
    if len(cuts) > 0:
        array = levels(rng, dims, cuts, -0.22, 0.18) * array
    return jnp.clip(array, min=-reach, max=reach).astype(kind)


def setup_inputs(seed: int = 0) -> dict:
    streams_of = jax.random.split(jax.random.key(seed), 6)
    return {
        "segments": normal_values(streams_of[0], (9, SEGS), 1.0, 6.0, ((1, 256),), jnp.float32),
        "pair_blocks": draw_pair_blocks(jax.random.fold_in(streams_of[5], 71), 0),
        "block_cells": draw_block_cells(jax.random.fold_in(streams_of[5], 71), 0),
        "mobility": draw_mobility(jax.random.fold_in(streams_of[5], 71), 0),
        "cell_centers": jnp.clip(jax.random.uniform(streams_of[4], (3, NCELL), jnp.float32, -2.0, 2.0), -2.0, 2.0),
    }


NEAR_CORE = 0.25
FAR_CORE = 1.0
STEP_LIMIT = 0.5

def pair_weights(first, second, core):
    offset = first[0:3, :, None] - second[0:3, None, :]
    dist_sq = lax.optimization_barrier(jnp.sum(offset * offset, axis=0)) + core
    high = lax.Precision.HIGHEST
    burgers = jnp.dot(first[6:9].T, second[6:9], precision=high)
    lines = jnp.dot(first[3:6].T, second[3:6], precision=high)
    cross_one = jnp.dot(first[6:9].T, second[3:6], precision=high)
    cross_two = jnp.dot(first[3:6].T, second[6:9], precision=high)
    coupling = burgers * lines + 0.5 * cross_one * cross_two
    return (coupling / (dist_sq * jnp.sqrt(dist_sq)), offset)

def pair_forces(first, second):
    weights, offset = pair_weights(first, second, NEAR_CORE)
    pulled = weights[None] * offset
    return (lax.optimization_barrier(jnp.sum(pulled, axis=2)), -lax.optimization_barrier(jnp.sum(pulled, axis=1)))

def self_force(block):
    return pair_forces(block, block)[0]

def add_pair(buffer, blocks, pair_row):
    first = pair_row[0]
    second = pair_row[1]
    usable = (first >= 0).astype(buffer.dtype)
    first_c = jnp.maximum(first, 0).astype(jnp.int32)
    second_c = jnp.maximum(second, 0).astype(jnp.int32)
    zero = jnp.zeros((), jnp.int32)
    length = blocks.shape[2]
    seg_one = lax.dynamic_slice(blocks, (zero, first_c, zero), (9, 1, length))[:, 0, :]
    seg_two = lax.dynamic_slice(blocks, (zero, second_c, zero), (9, 1, length))[:, 0, :]
    force_one, force_two = pair_forces(seg_one, seg_two)
    old_one = lax.dynamic_slice(buffer, (zero, first_c, zero), (3, 1, length))
    buffer = lax.dynamic_update_slice(buffer, old_one + usable * force_one[:, None, :], (zero, first_c, zero))
    old_two = lax.dynamic_slice(buffer, (zero, second_c, zero), (3, 1, length))
    buffer = lax.dynamic_update_slice(buffer, old_two + usable * force_two[:, None, :], (zero, second_c, zero))
    return buffer

def block_outer(block):
    return (block[6:9, None, :] * block[3:6][None, :, :]).reshape(9, block.shape[1])

def cell_moments(segs, cells, cell_count):
    block_count = cells.shape[0]
    outer = (segs[6:9, None, :] * segs[3:6][None, :, :]).reshape(9, block_count, segs.shape[1] // block_count)
    per_block = lax.optimization_barrier(jnp.sum(outer, axis=2))
    onehot = (cells[:, None] == lax.iota(jnp.int32, cell_count)[None, :]).astype(segs.dtype)
    return jnp.dot(per_block, onehot, precision=lax.Precision.HIGHEST)

def far_force(block, cell, moments, centers):
    coupling = jnp.dot(block_outer(block).T, moments, precision=lax.Precision.HIGHEST)
    offset = block[0:3, :, None] - centers[:, None, :]
    dist_sq = lax.optimization_barrier(jnp.sum(offset * offset, axis=0)) + FAR_CORE
    keep = (lax.iota(jnp.int32, centers.shape[1]) != cell).astype(block.dtype)
    weights = coupling * keep[None, :] / (dist_sq * jnp.sqrt(dist_sq))
    return lax.optimization_barrier(jnp.sum(weights[None] * offset, axis=2))

def scan_step(carry, pair_row):
    buffer, group_blocks = carry
    return ((add_pair(buffer, group_blocks, pair_row), group_blocks), None)

def reference(segments, pair_blocks, block_cells, mobility, cell_centers):
    blocks_all = segments.reshape(9, NBLOCKS, BLK)
    pieces = []
    for group in range(N_GRP):
        group_blocks = blocks_all[:, group * BLK_GRP:(group + 1) * BLK_GRP]
        group_pairs = pair_blocks[group * PAIR_GRP:(group + 1) * PAIR_GRP]
        buffer = jnp.zeros((3, BLK_GRP, BLK), jnp.float32)
        carry, unused = lax.scan(scan_step, (buffer, group_blocks), group_pairs)
        pieces.append(carry[0].reshape(3, SEG_GRP))
    near = jnp.concatenate(pieces, axis=1)
    by_block = jnp.moveaxis(blocks_all, 1, 0)
    own = jnp.moveaxis(lax.map(self_force, by_block), 0, 1).reshape(3, SEGS)
    moments = cell_moments(segments, block_cells, NCELL)

    def far_one(item):
        return far_force(item[0], item[1], moments, cell_centers)
    far = jnp.moveaxis(lax.map(far_one, (by_block, block_cells)), 0, 1).reshape(3, SEGS)
    forces = near + own + far
    velocity = mobility[None, :] * forces
    fastest = jnp.max(jnp.sqrt(lax.optimization_barrier(jnp.sum(velocity * velocity, axis=0))))
    return (forces, STEP_LIMIT / (fastest + 1e-06) * velocity)
```

```python
import jax
import jax.numpy as jnp
from jax import lax
from jax.experimental import pallas as pl
from jax.experimental.pallas import tpu as pltpu
from jax.sharding import PartitionSpec as P

NEAR_CORE = 0.25
FAR_CORE = 1.0
STEP_LIMIT = 0.5
BLK = 128
NB = 16
ND = 32
NG = 8
ROWS = 9 * NB + 8
EXTRA = 9 * NB
DUMMY = NB * ND
F32 = jnp.float32
BF16 = jnp.bfloat16
VMEM = pl.BlockSpec(memory_space=pltpu.VMEM)
SMEM = pl.BlockSpec(memory_space=pltpu.SMEM)


def lanes(rows):
    return lax.broadcasted_iota(jnp.int32, (rows, BLK), 1)


def split(x):
    one = x.astype(BF16)
    rest = x - one.astype(F32)
    two = rest.astype(BF16)
    three = (rest - two.astype(F32)).astype(BF16)
    return one, two, three


def pack_kernel(seg, cells, pairs, out):
    for k in range(NB):
        cols = slice(k * BLK, (k + 1) * BLK)
        out[pl.ds(k, 8, stride=NB), :] = seg[0:8, cols]
        out[8 * NB + k : 8 * NB + k + 1, :] = seg[8:9, cols]
    row = lax.broadcasted_iota(jnp.int32, (NB, BLK), 0)
    cell = jnp.zeros((NB, BLK), jnp.int32)
    for k in range(NB):
        cell = jnp.where(row == k, cells[k] & 31, cell)
    hot = (lanes(NB) == cell).astype(F32)
    hot_last = (lanes(NB) == cell + 32).astype(F32)
    rows = []
    for q in range(3):
        for r in range(3):
            outer = out[(6 + q) * NB : (7 + q) * NB, :] * out[(3 + r) * NB : (4 + r) * NB, :]
            total = jnp.sum(outer, axis=1, keepdims=True)
            rows.append(jnp.sum(total * (hot_last if q + r == 4 else hot), axis=0, keepdims=True))
    out[EXTRA : EXTRA + 1, :] = rows[0] + rows[8] + pairs[...]
    for r in range(1, 8):
        out[EXTRA + r : EXTRA + r + 1, :] = rows[r]


def outer_rows(get):
    t = [get(3 + r) for r in range(3)]
    b = [get(6 + q) for q in range(3)]
    return [[b[q] * t[r] for r in range(3)] for q in range(3)]


def main_kernel(rec, mom, cells, centers, mobility, forces, top, gbuf, obuf, lhs, pos, acc, rbuf, lst, smem, sem):
    me = lax.axis_index("dev")

    def couplings(s, carry):
        o = outer_rows(lambda r: rec[s, r * NB : (r + 1) * NB, :])
        for q in range(3):
            for r in range(3):
                gbuf[pl.ds(s * NB * 16 + 3 * q + r, NB, stride=16), :] = o[q][r] + 0.5 * o[r][q]
        return carry

    lax.fori_loop(0, ND, couplings, 0)
    gbuf[pl.ds(DUMMY * 16, 16), :] = jnp.zeros((16, BLK), F32)
    o = outer_rows(lambda r: rec[me, r * NB : (r + 1) * NB, :])
    for q in range(3):
        for r in range(3):
            obuf[pl.ds(3 * q + r, NB, stride=16), :] = o[q][r]

    for s in range(ND):
        rbuf[s : s + 1, :] = rec[s, EXTRA : EXTRA + 1, :]
    lane = lanes(NB)
    cand = jnp.where(lane < 64, pltpu.roll(rbuf[0:16, :], 64, 1), rbuf[16:32, :])
    other = jnp.where((lane & 32) == 0, pltpu.roll(cand, 96, 1), pltpu.roll(cand, 32, 1))
    ci = cand.astype(jnp.int32)
    hit = (ci >> 4) == me
    code = ((ci & 15) * 1024).astype(F32) + other - float(DUMMY)
    hits = hit.astype(F32)
    sq_row = lax.broadcasted_iota(jnp.int32, (BLK, BLK), 0)
    sq_lane = lanes(BLK)
    below = (sq_row < sq_lane).astype(BF16)
    inside = jnp.dot(hits.astype(BF16), below, preferred_element_type=F32)
    totals = jnp.dot(hits.astype(BF16), jnp.ones((BLK, BLK), BF16), preferred_element_type=F32)
    before = jnp.zeros((NB, BLK), F32)
    running = jnp.zeros((1, BLK), F32)
    row16 = lax.broadcasted_iota(jnp.int32, (NB, BLK), 0)
    for s in range(NB):
        before = jnp.where(row16 == s, running, before)
        running = running + totals[s : s + 1, :]
    count = jnp.sum(hits).astype(jnp.int32)
    rank = jnp.where(hit, inside + before, -1.0)
    turned = jnp.concatenate([rank, code, jnp.zeros((BLK - 32, BLK), F32)], axis=0).T

    def listing(chunk, carry):
        slot = (sq_lane + chunk * BLK).astype(F32)
        found = jnp.zeros((BLK, BLK), F32)
        for c in range(NB):
            found = found + jnp.where(turned[:, c : c + 1] == slot, turned[:, NB + c : NB + c + 1], 0.0)
        codes = jnp.sum(found, axis=0, keepdims=True) + float(DUMMY)
        lst[pl.ds(chunk, 1), :] = codes.astype(jnp.int32)
        return carry

    lax.fori_loop(0, (count + BLK - 1) // BLK, listing, 0)
    copy = pltpu.make_async_copy(lst, smem, sem)
    copy.start()

    far_rhs = []
    for half in range(2):
        rows = jnp.zeros((8, BLK), F32)
        last = jnp.zeros((1, BLK), F32)
        for g in range(4):
            tile = mom[half * 4 + g]
            low = jnp.where(lanes(8) < 32, tile, 0.0)
            high = jnp.where((lanes(8) >= 32) & (lanes(8) < 64), tile, 0.0)
            rows = rows + (pltpu.roll(low, 32 * g, 1) if g else low)
            shifted = pltpu.roll(high, (32 * g + 96) % 128, 1)
            last = last + shifted[0:1, :]
        full = jnp.concatenate([rows, last, jnp.zeros((7, BLK), F32)], axis=0)
        m1, m2, m3 = split(full)
        zero = jnp.zeros((32, BLK), BF16)
        far_rhs.append(jnp.concatenate([m1, m2, m1, m3, m2, m1, zero], axis=0))

    def pull(k, rhs, points, core, drop=None):
        c = jnp.dot(lhs[k], rhs, preferred_element_type=F32)
        if drop is not None:
            c = jnp.where(sq_lane == drop, 0.0, c)
        d = [pos[k, a] - points[a] for a in range(3)]
        inv = lax.rsqrt(d[0] * d[0] + d[1] * d[1] + (d[2] * d[2] + core))
        w = c * (inv * inv * inv)
        return [w * d[a] for a in range(3)]

    def block_rhs(f):
        g = gbuf[pl.ds(pl.multiple_of(f * 16, 16), 16), :]
        g = jnp.where(row16 < 9, g, 0.0)
        g1, g2, g3 = split(g)
        return jnp.concatenate([g1, g2, g1, g3, g2, g1, jnp.zeros((32, BLK), BF16)], axis=0)

    def block_points(f):
        return [rec[f >> 4, pl.ds(a * NB + (f & 15), 1), :] for a in range(3)]

    def home(k, carry):
        own = block_points(me * NB + k)
        ob = jnp.where(row16 < 9, obuf[pl.ds(pl.multiple_of(k * 16, 16), 16), :], 0.0)
        o1, o2, o3 = [x.astype(F32) for x in split(ob)]
        points = jnp.concatenate(own + [jnp.zeros((13, BLK), F32)], axis=0)
        turn = jnp.concatenate([o1, o1, o2, o1, o2, o3, points, jnp.zeros((16, BLK), F32)], axis=0).T
        lhs[k] = turn.astype(BF16)
        for a in range(3):
            pos[k, a] = jnp.broadcast_to(turn[:, 96 + a : 97 + a], (BLK, BLK))
        cell = cells[k]
        one = pull(k, far_rhs[0], [centers[a : a + 1, 0:BLK] for a in range(3)], FAR_CORE, cell)
        two = pull(k, far_rhs[1], [centers[a : a + 1, BLK : 2 * BLK] for a in range(3)], FAR_CORE, cell - BLK)
        self_pull = pull(k, block_rhs(me * NB + k), own, NEAR_CORE)
        for a in range(3):
            acc[k, a] = one[a] + two[a] + self_pull[a]
        return carry

    lax.fori_loop(0, NB, home, 0)
    copy.wait()

    def pair_step(i, carry):
        for u in range(2):
            at = 2 * i + u
            entry = smem[at >> 7, at & 127]
            k = entry >> 10
            f = entry & 1023
            near = pull(k, block_rhs(f), block_points(jnp.minimum(f, DUMMY - 1)), NEAR_CORE)
            for a in range(3):
                acc[k, a] = acc[k, a] + near[a]
        return carry

    lax.fori_loop(0, (count + 1) // 2, pair_step, 0)

    for k in range(NB):
        sums = [jnp.sum(acc[k, a], axis=1, keepdims=True) for a in range(3)]
        cols = jnp.where(sq_lane == 0, sums[0], jnp.where(sq_lane == 1, sums[1], sums[2]))
        forces[:, k * BLK : (k + 1) * BLK] = cols.T[0:3, :]
    v = mobility[...] * forces[...]
    speed = jnp.sum(v * v, axis=0, keepdims=True)
    top[...] = jnp.broadcast_to(jnp.max(speed, axis=1, keepdims=True), (1, BLK))


def step_kernel(tops, forces, mobility, out):
    best = jnp.max(jnp.max(tops[...], axis=0, keepdims=True), axis=1, keepdims=True)
    scale = STEP_LIMIT / (jnp.sqrt(best) + 1e-06)
    out[...] = scale * (mobility[...] * forces[...])


def body(segments, pair_blocks, block_cells, mobility, cell_centers):
    params = pltpu.CompilerParams(vmem_limit_bytes=40 * 1024 * 1024)
    listed = jnp.concatenate([jnp.zeros((64,), jnp.int32), pair_blocks[:, 0], pair_blocks[:, 1]])
    payload = pl.pallas_call(
        pack_kernel,
        out_shape=jax.ShapeDtypeStruct((ROWS, BLK), F32),
        in_specs=[VMEM, SMEM, VMEM],
        out_specs=VMEM,
        name="pack",
    )(segments, block_cells, listed.astype(F32)[None, :])
    rec = lax.all_to_all(jnp.broadcast_to(payload[None], (ND, ROWS, BLK)), "dev", 0, 0, tiled=True)
    group = jnp.sum(rec[:, EXTRA:, :], axis=0)
    mom = lax.all_to_all(jnp.broadcast_to(group[None], (NG, 8, BLK)), "grp", 0, 0, tiled=True)
    mob = mobility[None, :]
    forces, top = pl.pallas_call(
        main_kernel,
        out_shape=(jax.ShapeDtypeStruct((3, NB * BLK), F32), jax.ShapeDtypeStruct((1, BLK), F32)),
        in_specs=[VMEM, VMEM, SMEM, VMEM, VMEM],
        out_specs=(VMEM, VMEM),
        scratch_shapes=[
            pltpu.VMEM(((DUMMY + 1) * 16, BLK), F32),
            pltpu.VMEM((NB * 16, BLK), F32),
            pltpu.VMEM((NB, BLK, BLK), BF16),
            pltpu.VMEM((NB, 3, BLK, BLK), F32),
            pltpu.VMEM((NB, 3, BLK, BLK), F32),
            pltpu.VMEM((ND, BLK), F32),
            pltpu.VMEM((NB, BLK), jnp.int32),
            pltpu.SMEM((NB, BLK), jnp.int32),
            pltpu.SemaphoreType.DMA,
        ],
        compiler_params=params,
        name="forces",
    )(rec, mom, block_cells, cell_centers, mob)
    tops = lax.all_to_all(jnp.broadcast_to(top, (ND * NG, BLK)), ("grp", "dev"), 0, 0, tiled=True)
    displacement = pl.pallas_call(
        step_kernel,
        out_shape=jax.ShapeDtypeStruct((3, NB * BLK), F32),
        in_specs=[VMEM, VMEM, VMEM],
        out_specs=VMEM,
        name="step",
    )(tops, forces, mob)
    return forces, displacement


def solution(mesh):
    both = ("grp", "dev")
    in_specs = (P(None, both), P(both, None), P(both), P(both), P())
    out_specs = (P(None, both), P(None, both))
    return jax.shard_map(body, mesh=mesh, in_specs=in_specs, out_specs=out_specs, check_vma=False)
```

```python
import jax
import jax.numpy as jnp
from jax import lax
from jax.experimental import pallas as pl
from jax.experimental.pallas import tpu as pltpu
from jax.sharding import Mesh
from jax.sharding import PartitionSpec as P

NEAR_CORE = 0.25
FAR_CORE = 1.0
STEP_LIMIT = 0.5
BLK = 128
NB = 16
NZ = 8
NX = 4
NG = 8
EXTRA = 9 * NB
ROWS = EXTRA + 8
CAP = 24
SECT = 9 * CAP
TASKS = 2048
COUNT, ROUNDS = TASKS + 64, TASKS + 65
PAD = 1 << 16
F32 = jnp.float32
BF16 = jnp.bfloat16
VMEM = pl.BlockSpec(memory_space=pltpu.VMEM)
SMEM = pl.BlockSpec(memory_space=pltpu.SMEM)
NT = (((1,), (1,)), ((), ()))


def lanes(rows):
    return lax.broadcasted_iota(jnp.int32, (rows, BLK), 1)


def subs(rows):
    return lax.broadcasted_iota(jnp.int32, (rows, BLK), 0)


def split(x):
    one = x.astype(BF16)
    rest = x - one.astype(F32)
    two = rest.astype(BF16)
    three = (rest - two.astype(F32)).astype(BF16)
    return one, two, three


def pack_kernel(seg, cells, pairs, out):
    for k in range(NB):
        cols = slice(k * BLK, (k + 1) * BLK)
        out[pl.ds(k, 8, stride=NB), :] = seg[0:8, cols]
        out[8 * NB + k : 8 * NB + k + 1, :] = seg[8:9, cols]
    row = subs(NB)
    cell = jnp.zeros((NB, BLK), jnp.int32)
    for k in range(NB):
        cell = jnp.where(row == k, cells[k] & 31, cell)
    hot = (lanes(NB) == cell + 64).astype(F32)
    hot_last = (lanes(NB) == cell + 96).astype(F32)
    rows = []
    for q in range(3):
        for r in range(3):
            outer = out[(6 + q) * NB : (7 + q) * NB, :] * out[(3 + r) * NB : (4 + r) * NB, :]
            total = jnp.sum(outer, axis=1, keepdims=True)
            rows.append(jnp.sum(total * (hot_last if q + r == 4 else hot), axis=0, keepdims=True))
    out[EXTRA : EXTRA + 1, :] = rows[0] + rows[8]
    for r in range(1, 8):
        out[EXTRA + r : EXTRA + r + 1, :] = rows[r]
    out[EXTRA : EXTRA + 2, 0:32] = pairs[...].astype(F32)


def column_kernel(rec_z, out):
    lane = lanes(8)
    first = rec_z[pl.ds(EXTRA, NZ, stride=ROWS), :]
    second = rec_z[pl.ds(EXTRA + 1, NZ, stride=ROWS), :]
    total = rec_z[EXTRA : EXTRA + 8, :]
    for s in range(1, NZ):
        total = total + rec_z[s * ROWS + EXTRA : s * ROWS + EXTRA + 8, :]
    out[...] = jnp.where(lane < 32, first, jnp.where(lane < 64, pltpu.roll(second, 32, 1), total))


def route_kernel(turn_no, rec_t, rec_z, send, tasks, lst, smem, cnt, sem):
    g = lax.axis_index("y") * 2 + lax.axis_index("c")
    zz = lax.axis_index("z")
    xx = lax.axis_index("x")
    rnd = turn_no[0]
    lane = lanes(8)
    a = jnp.zeros((8, BLK), F32)
    b = jnp.zeros((8, BLK), F32)
    for x in range(NX):
        part = rec_t[pl.ds(pl.multiple_of(g * 32 + x * 8, 8), 8), :]
        one = jnp.where(lane < 32, part, 0.0)
        two = jnp.where((lane >= 32) & (lane < 64), part, 0.0)
        a = a + (pltpu.roll(one, 32 * x, 1) if x else one)
        b = b + (pltpu.roll(two, (32 * x + 96) % 128, 1) if x != 1 else two)
    ai = a.astype(jnp.int32)
    bi = b.astype(jnp.int32)
    own_a = ai >> 4
    own_b = bi >> 4

    need = jnp.zeros((32, 16), F32)
    for i in range(8):
        ra, rb = own_a[i : i + 1, :], own_b[i : i + 1, :]
        for here, there in ((ra, rb), (rb, ra)):
            owner = (subs(32) == here).astype(BF16)
            column = (subs(16) == (there & 3)).astype(BF16)
            need = need + lax.dot_general(owner, column, NT, preferred_element_type=F32)
    r32 = lax.broadcasted_iota(jnp.int32, (32, 16), 0)
    c32 = lax.broadcasted_iota(jnp.int32, (32, 16), 1)
    longest = jnp.max(jnp.where((r32 & 3) == c32, 0.0, need)).astype(jnp.int32)

    hits, codes = [], []
    for x in range(NX):
        d = zz * NX + x
        fa = own_a == d
        fb = own_b == d
        swapped = (bi & 15) * 512 + ai
        hits += [fa | fb, fa & fb]
        codes += [jnp.where(fa, (ai & 15) * 512 + bi, swapped), swapped]
    hit = jnp.concatenate([h.astype(F32) for h in hits], axis=0)
    code = jnp.concatenate(codes, axis=0).astype(F32)
    hot = hit.astype(BF16)
    sq_row, sq_lane = subs(BLK), lanes(BLK)
    inside = jnp.dot(hot, (sq_row < sq_lane).astype(BF16), preferred_element_type=F32)
    totals = jnp.dot(hot, jnp.ones((BLK, BLK), BF16), preferred_element_type=F32)
    r64 = lax.broadcasted_iota(jnp.int32, (64, 64), 0)
    c64 = lax.broadcasted_iota(jnp.int32, (64, 64), 1)
    earlier = ((c64 < r64) & ((c64 >> 4) == (r64 >> 4))).astype(BF16)
    before = jnp.dot(earlier, totals.astype(BF16), preferred_element_type=F32)
    rank = jnp.where(hit > 0.0, inside + before, -1.0)
    turned = jnp.concatenate([rank, code], axis=0).T
    counts = [jnp.sum(hit[16 * x : 16 * x + 16]).astype(jnp.int32) for x in range(NX)]
    for x in range(NX):

        def listing(chunk, carry):
            slot = (sq_lane + chunk * BLK).astype(F32)
            found = jnp.zeros((BLK, BLK), F32)
            for c in range(16 * x, 16 * x + 16):
                found = found + jnp.where(turned[:, c : c + 1] == slot, turned[:, 64 + c : 65 + c], 0.0)
            lst[pl.ds(16 * x + chunk, 1), :] = jnp.sum(found, axis=0, keepdims=True).astype(jnp.int32)
            return carry

        lax.fori_loop(0, (counts[x] + BLK - 1) // BLK, listing, 0)
    copy = pltpu.make_async_copy(lst, smem, sem)
    copy.start()
    send[...] = jnp.zeros_like(send)
    for x in range(2 * NX):
        cnt[x] = 0
    copy.wait()

    def receive(i, at):
        entry = smem[xx * 16 + (i >> 7), i & 127]
        f = entry & 511
        column = (f >> 4) & 3
        here = column == xx
        slot = cnt[column] - rnd * CAP
        cnt[column] = cnt[column] + 1
        base = jnp.where(here, (NX + (f >> 6)) * SECT + (f & 15), column * SECT + slot)
        use = jnp.where(here, rnd == 0, (slot >= 0) & (slot < CAP))
        tasks[at] = base | ((entry >> 9) << 12)
        return at + use.astype(jnp.int32)

    mine = jnp.where(xx == 0, counts[0], jnp.where(xx == 1, counts[1], jnp.where(xx == 2, counts[2], counts[3])))
    used = lax.fori_loop(0, mine, receive, 0)
    for u in range(4):
        tasks[used + u] = PAD
    tasks[COUNT] = used
    tasks[ROUNDS] = (longest + CAP - 1) // CAP

    for x in range(NX):

        def deliver(i, carry):
            f = smem[16 * x + (i >> 7), i & 127] & 511

            @pl.when(((f >> 4) & 3) == xx)
            def _():
                slot = cnt[NX + x] - rnd * CAP
                cnt[NX + x] = cnt[NX + x] + 1

                @pl.when((slot >= 0) & (slot < CAP))
                def _():
                    source = (f >> 6) * ROWS + (f & 15)
                    target = x * SECT + slot
                    send[pl.ds(target, 8, stride=CAP), :] = rec_z[pl.ds(source, 8, stride=NB), :]
                    send[pl.ds(target + 8 * CAP, 1), :] = rec_z[pl.ds(source + 8 * NB, 1), :]

            return carry

        lax.fori_loop(0, jnp.where(xx == x, 0, counts[x]), deliver, 0)


def outer_rows(row, symmetric):
    s = subs(16)
    t = [jnp.broadcast_to(row(3 + r), (16, BLK)) for r in range(3)]
    b = [jnp.broadcast_to(row(6 + q), (16, BLK)) for q in range(3)]

    def slow(v):
        return jnp.where(s < 3, v[0], jnp.where(s < 6, v[1], v[2]))

    def fast(v):
        first = (s == 0) | (s == 3) | (s == 6)
        return jnp.where(first, v[0], jnp.where((s == 1) | (s == 4) | (s == 7), v[1], v[2]))

    o = slow(b) * fast(t)
    return o + 0.5 * (fast(b) * slow(t)) if symmetric else o


def right_side(rows):
    one, two, three = split(rows)
    return jnp.concatenate([one, two, one, three, two, one, jnp.zeros((32, BLK), BF16)], axis=0)


def prepare(k, row, lhs, pos):
    o = jnp.where(subs(16) < 9, outer_rows(row, False), 0.0)
    o1, o2, o3 = [x.astype(F32) for x in split(o)]
    points = jnp.concatenate([row(a) for a in range(3)] + [jnp.zeros((13, BLK), F32)], axis=0)
    turn = jnp.concatenate([o1, o1, o2, o1, o2, o3, points, jnp.zeros((16, BLK), F32)], axis=0).T
    lhs[k] = turn.astype(BF16)
    for a in range(3):
        pos[k, a] = jnp.broadcast_to(turn[:, 96 + a : 97 + a], (BLK, BLK))


def pull(k, lhs, pos, rhs, points, core, drop=None):
    c = jnp.dot(lhs[k], rhs, preferred_element_type=F32)
    if drop is not None:
        c = jnp.where(lanes(BLK) == drop, 0.0, c)
    d = [pos[k, a] - points[a] for a in range(3)]
    inv = lax.rsqrt(d[0] * d[0] + d[1] * d[1] + (d[2] * d[2] + core))
    w = c * (inv * inv * inv)
    return [w * d[a] for a in range(3)]


def total_rows(acc, k):
    sums = [jnp.sum(acc[k, a], axis=1, keepdims=True) for a in range(3)]
    lane = lanes(BLK)
    return jnp.where(lane == 0, sums[0], jnp.where(lane == 1, sums[1], sums[2])).T[0:3, :]


def home_kernel(own, rec_t, cells, centers, forces, lhs, pos, acc):
    far_rhs = []
    for half in range(2):
        rows = jnp.zeros((8, BLK), F32)
        last = jnp.zeros((8, BLK), F32)
        for i in range(4):
            at = (half * 4 + i) * 32
            tile = rec_t[at : at + 8, :]
            for x in range(1, NX):
                tile = tile + rec_t[at + 8 * x : at + 8 * x + 8, :]
            low = jnp.where((lanes(8) >= 64) & (lanes(8) < 96), tile, 0.0)
            high = jnp.where(lanes(8) >= 96, tile, 0.0)
            rows = rows + (pltpu.roll(low, (32 * i + 64) % 128, 1) if i != 2 else low)
            last = last + (pltpu.roll(high, (32 * i + 32) % 128, 1) if i != 3 else high)
        far_rhs.append(right_side(jnp.concatenate([rows, last[0:1, :], jnp.zeros((7, BLK), F32)], axis=0)))

    def step(k, carry):
        def row(r):
            return own[pl.ds(r * NB + k, 1), :]

        prepare(k, row, lhs, pos)
        cell = cells[k]
        self_rhs = right_side(jnp.where(subs(16) < 9, outer_rows(row, True), 0.0))
        one = pull(k, lhs, pos, far_rhs[0], [centers[a : a + 1, 0:BLK] for a in range(3)], FAR_CORE, cell)
        two = pull(k, lhs, pos, far_rhs[1], [centers[a : a + 1, BLK:] for a in range(3)], FAR_CORE, cell - BLK)
        same = pull(k, lhs, pos, self_rhs, [row(a) for a in range(3)], NEAR_CORE)
        for a in range(3):
            acc[k, a] = one[a] + two[a] + same[a]
        return carry

    lax.fori_loop(0, NB, step, 0)
    for k in range(NB):
        forces[:, k * BLK : (k + 1) * BLK] = total_rows(acc, k)


def near_kernel(rec_x, rec_z, tasks, so_far, mobility, forces, top, blocks, lhs, pos, acc):
    zz = lax.axis_index("z")
    blocks[0 : NX * SECT, :] = rec_x[...]
    for s in range(NZ):
        for r in range(9):
            at = (NX + s) * SECT + r * CAP
            blocks[at : at + NB, :] = rec_z[s * ROWS + r * NB : s * ROWS + (r + 1) * NB, :]

    def ready(k, carry):
        prepare(k, lambda r: blocks[pl.ds((NX + zz) * SECT + r * CAP + k, 1), :], lhs, pos)
        for a in range(3):
            acc[k, a] = jnp.zeros((BLK, BLK), F32)
        return carry

    lax.fori_loop(0, NB, ready, 0)

    def pair_step(i, carry):
        for u in range(2):
            entry = tasks[2 * i + u]
            base = entry & 4095
            k = (entry >> 12) & 15
            limit = jnp.where(entry >= PAD, 0, 9)

            def row(r):
                return blocks[pl.ds(base + r * CAP, 1), :]

            rhs = right_side(jnp.where(subs(16) < limit, outer_rows(row, True), 0.0))
            near = pull(k, lhs, pos, rhs, [row(a) for a in range(3)], NEAR_CORE)
            for a in range(3):
                acc[k, a] = acc[k, a] + near[a]
        return carry

    lax.fori_loop(0, (tasks[COUNT] + 1) // 2, pair_step, 0)
    for k in range(NB):
        cols = slice(k * BLK, (k + 1) * BLK)
        forces[:, cols] = so_far[:, cols] + total_rows(acc, k)
    v = mobility[...] * forces[...]
    speed = jnp.sum(v * v, axis=0, keepdims=True)
    top[...] = jnp.broadcast_to(jnp.max(speed, axis=1, keepdims=True), (1, BLK))


def step_kernel(tops, forces, mobility, out):
    best = jnp.max(jnp.max(tops[...], axis=0, keepdims=True), axis=1, keepdims=True)
    scale = STEP_LIMIT / (jnp.sqrt(best) + 1e-06)
    out[...] = scale * (mobility[...] * forces[...])


def shape(*dims, kind=F32):
    return jax.ShapeDtypeStruct(dims, kind)


def work_scratch():
    return [
        pltpu.VMEM((NB, BLK, BLK), BF16),
        pltpu.VMEM((NB, 3, BLK, BLK), F32),
        pltpu.VMEM((NB, 3, BLK, BLK), F32),
    ]


def body(segments, pair_blocks, block_cells, mobility, cell_centers):
    params = pltpu.CompilerParams(vmem_limit_bytes=24 * 1024 * 1024)
    seg_count = segments.shape[1]
    own = pl.pallas_call(
        pack_kernel,
        out_shape=shape(ROWS, BLK),
        in_specs=[VMEM, SMEM, VMEM],
        out_specs=VMEM,
        name="pack",
    )(segments, block_cells, pair_blocks.T)
    rec_z = lax.all_to_all(jnp.broadcast_to(own[None], (NZ, ROWS, BLK)), "z", 0, 0, tiled=True)
    rec_z = rec_z.reshape(NZ * ROWS, BLK)
    column = pl.pallas_call(
        column_kernel, out_shape=shape(8, BLK), in_specs=[VMEM], out_specs=VMEM, name="column"
    )(rec_z)
    rec_t = lax.all_to_all(jnp.broadcast_to(column[None], (NG * NX, 8, BLK)), ("y", "c", "x"), 0, 0, tiled=True)
    rec_t = rec_t.reshape(NG * NX * 8, BLK)

    def exchange(number):
        send, tasks = pl.pallas_call(
            route_kernel,
            out_shape=(shape(NX * SECT, BLK), shape(TASKS + 128, kind=jnp.int32)),
            in_specs=[SMEM, VMEM, VMEM],
            out_specs=(VMEM, SMEM),
            scratch_shapes=[
                pltpu.VMEM((NX * 16, BLK), jnp.int32),
                pltpu.SMEM((NX * 16, BLK), jnp.int32),
                pltpu.SMEM((2 * NX,), jnp.int32),
                pltpu.SemaphoreType.DMA,
            ],
            compiler_params=params,
            name="route",
        )(number, rec_t, rec_z)
        rec_x = lax.all_to_all(send.reshape(NX, SECT, BLK), "x", 0, 0, tiled=True)
        return rec_x.reshape(NX * SECT, BLK), tasks

    def add_near(rec_x, tasks, so_far):
        return pl.pallas_call(
            near_kernel,
            out_shape=(shape(3, seg_count), shape(1, BLK)),
            in_specs=[VMEM, VMEM, SMEM, VMEM, VMEM],
            out_specs=(VMEM, VMEM),
            scratch_shapes=[pltpu.VMEM(((NX + NZ) * SECT, BLK), F32)] + work_scratch(),
            compiler_params=params,
            name="near",
        )(rec_x, rec_z, tasks, so_far, mob)

    mob = mobility[None, :]
    rec_x, tasks = exchange(jnp.zeros((1,), jnp.int32))
    home = pl.pallas_call(
        home_kernel,
        out_shape=shape(3, seg_count),
        in_specs=[VMEM, VMEM, SMEM, VMEM],
        out_specs=VMEM,
        scratch_shapes=work_scratch(),
        compiler_params=params,
        cost_estimate=pl.CostEstimate(flops=6 * 10**9, bytes_accessed=10**6, transcendentals=0),
        name="home",
    )(own, rec_t, block_cells, cell_centers)
    forces, top = add_near(rec_x, tasks, home)

    def more(carry):
        number, so_far, _ = carry
        rec_x, tasks = exchange(number[None])
        forces, top = add_near(rec_x, tasks, so_far)
        return number + 1, forces, top

    rounds = tasks[ROUNDS]
    _, forces, top = lax.while_loop(lambda c: c[0] < rounds, more, (jnp.ones((), jnp.int32), forces, top))
    tops = lax.all_to_all(jnp.broadcast_to(top, (8 * NG * NX, BLK)), ("y", "c", "z", "x"), 0, 0, tiled=True)
    displacement = pl.pallas_call(
        step_kernel, out_shape=shape(3, seg_count), in_specs=[VMEM, VMEM, VMEM], out_specs=VMEM, name="step"
    )(tops, forces, mob)
    return forces, displacement


def solution(mesh):
    names = ("y", "c", "z", "x")
    fine = Mesh(mesh.devices.reshape(NG // 2, 2, NZ, NX), names)
    in_specs = (P(None, names), P(names, None), P(names), P(names), P())
    out_specs = (P(None, names), P(None, names))
    return jax.shard_map(body, mesh=fine, in_specs=in_specs, out_specs=out_specs, check_vma=False)
```

```python
import jax
import jax.numpy as jnp
from jax import lax
from jax.experimental import pallas as pl
from jax.experimental.pallas import tpu as pltpu
from jax.sharding import Mesh
from jax.sharding import PartitionSpec as P

NEAR_CORE = 0.25
FAR_CORE = 1.0
STEP_LIMIT = 0.5
BLK = 128
NB = 16
NZ = 8
NX = 4
NG = 8
EXTRA = 9 * NB
ROWS = EXTRA + 8
CAP = 24
SECT = 9 * CAP
LOCAL = NX * SECT
TASKS = 2048
COUNT = TASKS + 64
UNROLL = 2
PAD = 1 << 16
F32 = jnp.float32
BF16 = jnp.bfloat16
VMEM = pl.BlockSpec(memory_space=pltpu.VMEM)
SMEM = pl.BlockSpec(memory_space=pltpu.SMEM)
ANY = pl.BlockSpec(memory_space=pl.ANY)
NT = (((1,), (1,)), ((), ()))


def lanes(rows):
    return lax.broadcasted_iota(jnp.int32, (rows, BLK), 1)


def subs(rows):
    return lax.broadcasted_iota(jnp.int32, (rows, BLK), 0)


def split(x):
    one = x.astype(BF16)
    rest = x - one.astype(F32)
    two = rest.astype(BF16)
    three = (rest - two.astype(F32)).astype(BF16)
    return one, two, three


def pack_kernel(seg, cells, pairs, packed, out):
    for k in range(NB):
        cols = slice(k * BLK, (k + 1) * BLK)
        out[pl.ds(k, 8, stride=NB), :] = seg[0:8, cols]
        out[8 * NB + k : 8 * NB + k + 1, :] = seg[8:9, cols]
    row = subs(NB)
    cell = jnp.zeros((NB, BLK), jnp.int32)
    for k in range(NB):
        cell = jnp.where(row == k, cells[k] & 31, cell)
    hot = (lanes(NB) == cell + 64).astype(F32)
    hot_last = (lanes(NB) == cell + 96).astype(F32)
    rows = []
    for q in range(3):
        for r in range(3):
            outer = out[(6 + q) * NB : (7 + q) * NB, :] * out[(3 + r) * NB : (4 + r) * NB, :]
            total = jnp.sum(outer, axis=1, keepdims=True)
            rows.append(jnp.sum(total * (hot_last if q + r == 4 else hot), axis=0, keepdims=True))
    out[EXTRA : EXTRA + 1, :] = rows[0] + rows[8]
    for r in range(1, 8):
        out[EXTRA + r : EXTRA + r + 1, :] = rows[r]
    out[EXTRA : EXTRA + 2, 0:32] = pairs[...].astype(F32)
    whole = out[...]
    for copy in range(NZ):
        packed[copy * ROWS : (copy + 1) * ROWS, :] = whole


def column_kernel(*refs):
    out = refs[NZ]
    lane = lanes(8)
    first = jnp.concatenate([ref[0:1, :] for ref in refs[:NZ]], axis=0)
    second = jnp.concatenate([ref[1:2, :] for ref in refs[:NZ]], axis=0)
    total = refs[0][...]
    for ref in refs[1:NZ]:
        total = total + ref[...]
    tile = jnp.where(lane < 32, first, jnp.where(lane < 64, pltpu.roll(second, 32, 1), total))
    for copy in range(NG * NX):
        out[8 * copy : 8 * copy + 8, :] = tile


def group_pairs(rec_t):
    g = lax.axis_index("y") * 2 + lax.axis_index("c")
    lane = lanes(8)
    a = jnp.zeros((8, BLK), F32)
    b = jnp.zeros((8, BLK), F32)
    for x in range(NX):
        part = rec_t[pl.ds(pl.multiple_of(g * 32 + x * 8, 8), 8), :]
        one = jnp.where(lane < 32, part, 0.0)
        two = jnp.where((lane >= 32) & (lane < 64), part, 0.0)
        a = a + (pltpu.roll(one, 32 * x, 1) if x else one)
        b = b + (pltpu.roll(two, (32 * x + 96) % 128, 1) if x != 1 else two)
    return a.astype(jnp.int32), b.astype(jnp.int32)


def list_hits(hit, code, lst, smem, sem):
    rows = hit.shape[0]
    hits = hit.astype(F32)
    hot = jnp.concatenate([hits, jnp.zeros((16 - rows, BLK), F32)], axis=0) if rows < 16 else hits
    hot = hot.astype(BF16)
    sq_row, sq_lane = subs(BLK), lanes(BLK)
    inside = jnp.dot(hot, (sq_row < sq_lane).astype(BF16), preferred_element_type=F32)
    totals = jnp.dot(hot, jnp.ones((BLK, BLK), BF16), preferred_element_type=F32)
    before = jnp.zeros((16, BLK), F32)
    running = jnp.zeros((1, BLK), F32)
    for s in range(rows):
        before = jnp.where(subs(16) == s, running, before)
        running = running + totals[s : s + 1, :]
    count = jnp.max(running).astype(jnp.int32)
    rank = jnp.where(hits > 0.0, (inside + before)[0:rows, :], -1.0)
    code = code.astype(F32)

    def listing(chunk, carry):
        slot = (sq_row + chunk * BLK).astype(F32)
        found = jnp.zeros((BLK, BLK), F32)
        for c in range(rows):
            found = found + jnp.where(rank[c : c + 1, :] == slot, code[c : c + 1, :], 0.0)
        lst[pl.ds(chunk, 1), :] = jnp.sum(found.T, axis=0, keepdims=True).astype(jnp.int32)
        return carry

    listing(0, 0)
    lax.fori_loop(1, (count + BLK - 1) // BLK, listing, 0)
    copy = pltpu.make_async_copy(lst, smem, sem)
    copy.start()
    return copy, count


def send_kernel(turn_no, rec_t, rec_z_ref, send, lst, smem, cnt, sem, rec_z, sem_z):
    bring = pltpu.make_async_copy(rec_z_ref, rec_z, sem_z)
    bring.start()
    zz = lax.axis_index("z")
    xx = lax.axis_index("x")
    rnd = turn_no[0]
    ai, bi = group_pairs(rec_t)
    own_a, own_b = ai >> 4, bi >> 4
    xa, xb = own_a & 3, own_b & 3
    to_a = ((own_a >> 2) == zz) & (xa != xx) & (xb == xx)
    to_b = ((own_b >> 2) == zz) & (xb != xx) & (xa == xx)
    code = jnp.where(to_a, xa * 512 + bi, xb * 512 + ai)
    copy, count = list_hits(to_a | to_b, code, lst, smem, sem)
    send[...] = jnp.zeros_like(send)
    for x in range(NX):
        cnt[x] = 0
    copy.wait()
    bring.wait()

    def deliver(i, carry):
        entry = smem[i >> 7, i & 127]
        f = entry & 511
        x = entry >> 9
        slot = cnt[x] - rnd * CAP
        cnt[x] = cnt[x] + 1

        @pl.when((slot >= 0) & (slot < CAP))
        def _():
            source = (f >> 6) * ROWS + (f & 15)
            target = x * SECT + slot
            send[pl.ds(target, 8, stride=CAP), :] = rec_z[pl.ds(source, 8, stride=NB), :]
            send[pl.ds(target + 8 * CAP, 1), :] = rec_z[pl.ds(source + 8 * NB, 1), :]

        return carry

    lax.fori_loop(0, count, deliver, 0)


def tasks_kernel(turn_no, rec_t, tasks, rounds, lst, smem, cnt, sem):
    zz = lax.axis_index("z")
    xx = lax.axis_index("x")
    rnd = turn_no[0]
    ai, bi = group_pairs(rec_t)
    own_a, own_b = ai >> 4, bi >> 4
    me = zz * NX + xx
    fa, fb = own_a == me, own_b == me
    swapped = (bi & 15) * 512 + ai
    hits = jnp.concatenate([(fa | fb).astype(F32), (fa & fb).astype(F32)], axis=0)
    code = jnp.concatenate([jnp.where(fa, (ai & 15) * 512 + bi, swapped), swapped], axis=0)
    copy, count = list_hits(hits > 0.0, code, lst, smem, sem)

    owner, column = [], []
    for here, there in ((own_a, own_b), (own_b, own_a)):
        for i in range(8):
            owner.append((subs(32) == here[i : i + 1, :]).astype(BF16))
            column.append((subs(16) == (there[i : i + 1, :] & 3)).astype(BF16))
    owner, column = jnp.concatenate(owner, axis=1), jnp.concatenate(column, axis=1)
    need = lax.dot_general(owner, column, NT, preferred_element_type=F32)
    r32 = lax.broadcasted_iota(jnp.int32, (32, 16), 0)
    c32 = lax.broadcasted_iota(jnp.int32, (32, 16), 1)
    longest = jnp.max(jnp.where((r32 & 3) == c32, 0.0, need)).astype(jnp.int32)
    rounds[0] = (longest + CAP - 1) // CAP
    for x in range(NX):
        cnt[x] = 0
    copy.wait()

    def receive(i, at):
        entry = smem[i >> 7, i & 127]
        f = entry & 511
        column = (f >> 4) & 3
        here = column == xx
        slot = cnt[column] - rnd * CAP
        cnt[column] = cnt[column] + 1
        base = jnp.where(here, LOCAL + (f >> 6) * ROWS + (f & 15), column * SECT + slot)
        use = jnp.where(here, rnd == 0, (slot >= 0) & (slot < CAP))
        tasks[at] = base | ((entry >> 9) << 12)
        return at + use.astype(jnp.int32)

    used = lax.fori_loop(0, count, receive, 0)
    for u in range(8):
        tasks[used + u] = PAD
    tasks[COUNT] = used


def outer_rows(row, symmetric):
    s = subs(16)
    t = [jnp.broadcast_to(row(3 + r), (16, BLK)) for r in range(3)]
    b = [jnp.broadcast_to(row(6 + q), (16, BLK)) for q in range(3)]

    def slow(v):
        return jnp.where(s < 3, v[0], jnp.where(s < 6, v[1], v[2]))

    def fast(v):
        first = (s == 0) | (s == 3) | (s == 6)
        return jnp.where(first, v[0], jnp.where((s == 1) | (s == 4) | (s == 7), v[1], v[2]))

    o = slow(b) * fast(t)
    return o + 0.5 * (fast(b) * slow(t)) if symmetric else o


def right_side(rows):
    one, two, three = split(rows)
    return jnp.concatenate([one, two, one, three, two, one, jnp.zeros((32, BLK), BF16)], axis=0)


def prepare(k, row, left):
    o = jnp.where(subs(16) < 9, outer_rows(row, False), 0.0)
    o1, o2, o3 = [x.astype(F32) for x in split(o)]
    points = jnp.concatenate([row(a) for a in range(3)] + [jnp.zeros((13, BLK), F32)], axis=0)
    left[k] = jnp.concatenate([o1, o1, o2, o1, o2, o3, points, jnp.zeros((16, BLK), F32)], axis=0).T


def spread(left):
    return [jnp.broadcast_to(left[:, 96 + a : 97 + a], (BLK, BLK)) for a in range(3)]


def pull(left, here, rhs, there, core, drop=None):
    c = jnp.dot(left, rhs, preferred_element_type=F32)
    if drop is not None:
        c = jnp.where(lanes(BLK) == drop, 0.0, c)
    d = [here[a] - there[a] for a in range(3)]
    inv = lax.rsqrt(d[0] * d[0] + d[1] * d[1] + (d[2] * d[2] + core))
    w = c * (inv * inv * inv)
    return [w * d[a] for a in range(3)]


def total_rows(acc, k):
    return jnp.concatenate([jnp.sum(acc[k, a].T, axis=0, keepdims=True) for a in range(3)], axis=0)


def own_kernel(own, left, forces, acc):
    def step(k, carry):
        def row(r):
            return own[pl.ds(r * NB + k, 1), :]

        prepare(k, row, left)
        rhs = right_side(jnp.where(subs(16) < 9, outer_rows(row, True), 0.0))
        mine = left[k]
        same = pull(mine.astype(BF16), spread(mine), rhs, [row(a) for a in range(3)], NEAR_CORE)
        for a in range(3):
            acc[k, a] = same[a]
        return carry

    lax.fori_loop(0, NB, step, 0)
    for k in range(NB):
        forces[:, k * BLK : (k + 1) * BLK] = total_rows(acc, k)


def far_kernel(rec_t, cells, centers, left_ref, so_far, forces, left, acc, sem):
    bring = pltpu.make_async_copy(left_ref, left, sem)
    bring.start()
    far_rhs = []
    for half in range(2):
        rows = jnp.zeros((8, BLK), F32)
        last = jnp.zeros((8, BLK), F32)
        for i in range(4):
            at = (half * 4 + i) * 32
            tile = rec_t[at : at + 8, :]
            for x in range(1, NX):
                tile = tile + rec_t[at + 8 * x : at + 8 * x + 8, :]
            low = jnp.where((lanes(8) >= 64) & (lanes(8) < 96), tile, 0.0)
            high = jnp.where(lanes(8) >= 96, tile, 0.0)
            rows = rows + (pltpu.roll(low, (32 * i + 64) % 128, 1) if i != 2 else low)
            last = last + (pltpu.roll(high, (32 * i + 32) % 128, 1) if i != 3 else high)
        far_rhs.append(right_side(jnp.concatenate([rows, last[0:1, :], jnp.zeros((7, BLK), F32)], axis=0)))

    bring.wait()

    def step(k, carry):
        cell = cells[k]
        mine = left[k]
        side, here = mine.astype(BF16), spread(mine)
        one = pull(side, here, far_rhs[0], [centers[a : a + 1, 0:BLK] for a in range(3)], FAR_CORE, cell)
        two = pull(side, here, far_rhs[1], [centers[a : a + 1, BLK:] for a in range(3)], FAR_CORE, cell - BLK)
        for a in range(3):
            acc[k, a] = one[a] + two[a]
        return carry

    lax.fori_loop(0, NB, step, 0)
    for k in range(NB):
        cols = slice(k * BLK, (k + 1) * BLK)
        forces[:, cols] = so_far[:, cols] + total_rows(acc, k)


def gather_blocks(rec_x, rec_z, blocks, sems):
    copies = [
        pltpu.make_async_copy(rec_x, blocks.at[pl.ds(0, LOCAL)], sems.at[0]),
        pltpu.make_async_copy(rec_z, blocks.at[pl.ds(LOCAL, NZ * ROWS)], sems.at[1]),
    ]
    for copy in copies:
        copy.start()
    return copies


def add_pairs(tasks, blocks, left, acc):
    def pair_step(i, carry):
        for u in range(UNROLL):
            entry = tasks[UNROLL * i + u]
            base = entry & 4095
            k = (entry >> 12) & 15
            limit = jnp.where(entry >= PAD, 0, 9)
            apart = jnp.where(base >= LOCAL, NB, CAP)

            def row(r):
                return blocks[pl.ds(base + r * apart, 1), :]

            rhs = right_side(jnp.where(subs(16) < limit, outer_rows(row, True), 0.0))
            mine = left[k]
            near = pull(mine.astype(BF16), spread(mine), rhs, [row(a) for a in range(3)], NEAR_CORE)
            for a in range(3):
                acc[k, a] = acc[k, a] + near[a]
        return carry

    lax.fori_loop(0, (tasks[COUNT] + UNROLL - 1) // UNROLL, pair_step, 0)


def speeds(mobility, forces, tops):
    v = mobility[...] * forces[...]
    speed = jnp.sum(v * v, axis=0, keepdims=True)
    tops[...] = jnp.broadcast_to(jnp.max(speed, axis=1, keepdims=True), tops.shape)


def near_kernel(rec_x, rec_z, tasks, left_ref, so_far, mobility, forces, tops, blocks, left, acc, sems):
    copies = gather_blocks(rec_x, rec_z, blocks, sems)
    copies.append(pltpu.make_async_copy(left_ref, left, sems.at[2]))
    copies[2].start()
    acc[...] = jnp.zeros_like(acc)
    for copy in copies:
        copy.wait()
    add_pairs(tasks, blocks, left, acc)
    for k in range(NB):
        cols = slice(k * BLK, (k + 1) * BLK)
        forces[:, cols] = so_far[:, cols] + total_rows(acc, k)
    speeds(mobility, forces, tops)


def late_kernel(rec_x, rec_z, tasks, so_far, mobility, forces, tops, blocks, left, acc, sems):
    zz = lax.axis_index("z")
    for copy in gather_blocks(rec_x, rec_z, blocks, sems):
        copy.wait()

    def ready(k, carry):
        prepare(k, lambda r: blocks[pl.ds(LOCAL + zz * ROWS + r * NB + k, 1), :], left)
        for a in range(3):
            acc[k, a] = jnp.zeros((BLK, BLK), F32)
        return carry

    lax.fori_loop(0, NB, ready, 0)
    add_pairs(tasks, blocks, left, acc)
    for k in range(NB):
        cols = slice(k * BLK, (k + 1) * BLK)
        forces[:, cols] = so_far[:, cols] + total_rows(acc, k)
    speeds(mobility, forces, tops)


def step_kernel(tops, forces, mobility, out):
    best = jnp.max(jnp.max(tops[...], axis=0, keepdims=True), axis=1, keepdims=True)
    scale = STEP_LIMIT / (jnp.sqrt(best) + 1e-06)
    out[...] = scale * (mobility[...] * forces[...])


def shape(*dims, kind=F32):
    return jax.ShapeDtypeStruct(dims, kind)


def cost(flops):
    return pl.CostEstimate(flops=flops, bytes_accessed=10**6, transcendentals=0)


LEFT = (NB, BLK, BLK)
PARTS = (NB, 3, BLK, BLK)


def body(segments, pair_blocks, block_cells, mobility, cell_centers):
    params = pltpu.CompilerParams(vmem_limit_bytes=8 * 1024 * 1024)
    small = pltpu.CompilerParams(vmem_limit_bytes=4 * 1024 * 1024)
    seg_count = segments.shape[1]
    devices = 8 * NG * NX
    mob = mobility[None, :]
    packed, own = pl.pallas_call(
        pack_kernel,
        out_shape=(shape(NZ * ROWS, BLK), shape(ROWS, BLK)),
        in_specs=[VMEM, SMEM, VMEM],
        out_specs=(VMEM, VMEM),
        name="pack",
    )(segments, block_cells, pair_blocks.T)
    rec_z = lax.all_to_all(packed.reshape(NZ, ROWS, BLK), "z", 0, 0, tiled=True).reshape(NZ * ROWS, BLK)
    left, same = pl.pallas_call(
        own_kernel,
        out_shape=(shape(*LEFT), shape(3, seg_count)),
        in_specs=[VMEM],
        out_specs=(VMEM, VMEM),
        scratch_shapes=[pltpu.VMEM(PARTS, F32)],
        compiler_params=params,
        cost_estimate=cost(10**9),
        name="own",
    )(own)
    rec_z, left, same = lax.optimization_barrier((rec_z, left, same))
    column = pl.pallas_call(
        column_kernel,
        out_shape=shape(NG * NX * 8, BLK),
        grid=(1,),
        in_specs=[pl.BlockSpec((8, BLK), lambda i, s=s: ((s * ROWS + EXTRA) // 8, 0)) for s in range(NZ)],
        out_specs=pl.BlockSpec((NG * NX * 8, BLK), lambda i: (0, 0)),
        compiler_params=small,
        name="column",
    )(*([rec_z] * NZ))
    rec_t = lax.all_to_all(column.reshape(NG * NX, 8, BLK), ("y", "c", "x"), 0, 0, tiled=True)
    rec_t = rec_t.reshape(NG * NX * 8, BLK)

    def lists(rows):
        return [
            pltpu.VMEM((rows, BLK), jnp.int32),
            pltpu.SMEM((rows, BLK), jnp.int32),
            pltpu.SMEM((NX,), jnp.int32),
            pltpu.SemaphoreType.DMA,
        ]

    def exchange(number):
        send = pl.pallas_call(
            send_kernel,
            out_shape=shape(NX * SECT, BLK),
            in_specs=[SMEM, VMEM, ANY],
            out_specs=VMEM,
            scratch_shapes=lists(8) + [pltpu.VMEM((NZ * ROWS, BLK), F32), pltpu.SemaphoreType.DMA],
            compiler_params=small,
            name="send",
        )(number, rec_t, rec_z)
        rec_x = lax.all_to_all(send.reshape(NX, SECT, BLK), "x", 0, 0, tiled=True)
        tasks, rounds = pl.pallas_call(
            tasks_kernel,
            out_shape=(shape(TASKS + 128, kind=jnp.int32), shape(1, kind=jnp.int32)),
            in_specs=[SMEM, VMEM],
            out_specs=(SMEM, SMEM),
            scratch_shapes=lists(16),
            compiler_params=small,
            cost_estimate=cost(10**8),
            name="tasks",
        )(number, rec_t)
        return rec_x.reshape(NX * SECT, BLK), tasks, rounds

    blocks = pltpu.VMEM((LOCAL + NZ * ROWS, BLK), F32)
    sems = pltpu.SemaphoreType.DMA((3,))
    results = (shape(3, seg_count), shape(devices, BLK))
    rec_x, tasks, rounds = exchange(jnp.zeros((1,), jnp.int32))
    home = pl.pallas_call(
        far_kernel,
        out_shape=shape(3, seg_count),
        in_specs=[VMEM, SMEM, VMEM, ANY, VMEM],
        out_specs=VMEM,
        scratch_shapes=[pltpu.VMEM(LEFT, F32), pltpu.VMEM(PARTS, F32), pltpu.SemaphoreType.DMA],
        compiler_params=params,
        cost_estimate=cost(10**8),
        name="far",
    )(rec_t, block_cells, cell_centers, left, same)
    forces, tops = pl.pallas_call(
        near_kernel,
        out_shape=results,
        in_specs=[ANY, ANY, SMEM, ANY, VMEM, VMEM],
        out_specs=(VMEM, VMEM),
        scratch_shapes=[blocks, pltpu.VMEM(LEFT, F32), pltpu.VMEM(PARTS, F32), sems],
        compiler_params=params,
        name="near",
    )(rec_x, rec_z, tasks, left, home, mob)

    def more(carry):
        number, so_far, _ = carry
        rec_x, tasks, _ = exchange(number[None])
        forces, tops = pl.pallas_call(
            late_kernel,
            out_shape=results,
            in_specs=[ANY, ANY, SMEM, VMEM, VMEM],
            out_specs=(VMEM, VMEM),
            scratch_shapes=[blocks, pltpu.VMEM(LEFT, F32), pltpu.VMEM(PARTS, F32), sems],
            compiler_params=params,
            name="late",
        )(rec_x, rec_z, tasks, so_far, mob)
        return number + 1, forces, tops

    _, forces, tops = lax.while_loop(lambda c: c[0] < rounds[0], more, (jnp.ones((), jnp.int32), forces, tops))
    tops = lax.all_to_all(tops.reshape(devices, 1, BLK), ("y", "c", "z", "x"), 0, 0, tiled=True)
    displacement = pl.pallas_call(
        step_kernel,
        out_shape=shape(3, seg_count),
        in_specs=[VMEM, VMEM, VMEM],
        out_specs=VMEM,
        compiler_params=small,
        name="step",
    )(tops.reshape(devices, BLK), forces, mob)
    return forces, displacement


def solution(mesh):
    names = ("y", "c", "z", "x")
    fine = Mesh(mesh.devices.reshape(NG // 2, 2, NZ, NX), names)
    in_specs = (P(None, names), P(names, None), P(names), P(names), P())
    out_specs = (P(None, names), P(None, names))
    return jax.shard_map(body, mesh=fine, in_specs=in_specs, out_specs=out_specs, check_vma=False)
```

```python
import jax
import jax.numpy as jnp
from jax import lax
from jax.experimental import pallas as pl
from jax.experimental.pallas import tpu as pltpu
from jax.sharding import Mesh
from jax.sharding import PartitionSpec as P

NEAR_CORE = 0.25
FAR_CORE = 1.0
STEP_LIMIT = 0.5
BLK = 128
NB = 16
NZ = 8
NX = 4
NG = 8
EXTRA = 9 * NB
ROWS = EXTRA + 8
CAP = 24
SECT = 9 * CAP
LOCAL = NX * SECT
TASKS = 2048
COUNT = TASKS + 64
UNROLL = 4
PAD = 1 << 16
F32 = jnp.float32
BF16 = jnp.bfloat16
VMEM = pl.BlockSpec(memory_space=pltpu.VMEM)
SMEM = pl.BlockSpec(memory_space=pltpu.SMEM)
NT = (((1,), (1,)), ((), ()))


def lanes(rows):
    return lax.broadcasted_iota(jnp.int32, (rows, BLK), 1)


def subs(rows):
    return lax.broadcasted_iota(jnp.int32, (rows, BLK), 0)


def split(x):
    one = x.astype(BF16)
    rest = x - one.astype(F32)
    two = rest.astype(BF16)
    three = (rest - two.astype(F32)).astype(BF16)
    return one, two, three


def pack_kernel(seg, cells, pairs, packed, out):
    for k in range(NB):
        cols = slice(k * BLK, (k + 1) * BLK)
        out[pl.ds(k, 8, stride=NB), :] = seg[0:8, cols]
        out[8 * NB + k : 8 * NB + k + 1, :] = seg[8:9, cols]
    row = subs(NB)
    cell = jnp.zeros((NB, BLK), jnp.int32)
    for k in range(NB):
        cell = jnp.where(row == k, cells[k] & 31, cell)
    hot = (lanes(NB) == cell + 64).astype(F32)
    hot_last = (lanes(NB) == cell + 96).astype(F32)
    rows = []
    for q in range(3):
        for r in range(3):
            outer = out[(6 + q) * NB : (7 + q) * NB, :] * out[(3 + r) * NB : (4 + r) * NB, :]
            total = jnp.sum(outer, axis=1, keepdims=True)
            rows.append(jnp.sum(total * (hot_last if q + r == 4 else hot), axis=0, keepdims=True))
    out[EXTRA : EXTRA + 1, :] = rows[0] + rows[8]
    for r in range(1, 8):
        out[EXTRA + r : EXTRA + r + 1, :] = rows[r]
    out[EXTRA : EXTRA + 2, 0:32] = pairs[...].astype(F32)
    whole = out[...]
    for copy in range(NZ):
        packed[copy * ROWS : (copy + 1) * ROWS, :] = whole


def column_kernel(*refs):
    out = refs[NZ]
    lane = lanes(8)
    first = jnp.concatenate([ref[0:1, :] for ref in refs[:NZ]], axis=0)
    second = jnp.concatenate([ref[1:2, :] for ref in refs[:NZ]], axis=0)
    total = refs[0][...]
    for ref in refs[1:NZ]:
        total = total + ref[...]
    tile = jnp.where(lane < 32, first, jnp.where(lane < 64, pltpu.roll(second, 32, 1), total))
    for copy in range(NG * NX):
        out[8 * copy : 8 * copy + 8, :] = tile


def group_pairs(rec_t):
    g = lax.axis_index("y") * 2 + lax.axis_index("c")
    lane = lanes(8)
    a = jnp.zeros((8, BLK), F32)
    b = jnp.zeros((8, BLK), F32)
    for x in range(NX):
        part = rec_t[pl.ds(pl.multiple_of(g * 32 + x * 8, 8), 8), :]
        one = jnp.where(lane < 32, part, 0.0)
        two = jnp.where((lane >= 32) & (lane < 64), part, 0.0)
        a = a + (pltpu.roll(one, 32 * x, 1) if x else one)
        b = b + (pltpu.roll(two, (32 * x + 96) % 128, 1) if x != 1 else two)
    return a.astype(jnp.int32), b.astype(jnp.int32)


def list_hits(hit, code, lst, smem, sem):
    rows = hit.shape[0]
    hits = hit.astype(F32)
    hot = jnp.concatenate([hits, jnp.zeros((16 - rows, BLK), F32)], axis=0) if rows < 16 else hits
    hot = hot.astype(BF16)
    sq_row, sq_lane = subs(BLK), lanes(BLK)
    inside = jnp.dot(hot, (sq_row < sq_lane).astype(BF16), preferred_element_type=F32)
    totals = jnp.dot(hot, jnp.ones((BLK, BLK), BF16), preferred_element_type=F32)
    before = jnp.zeros((16, BLK), F32)
    running = jnp.zeros((1, BLK), F32)
    for s in range(rows):
        before = jnp.where(subs(16) == s, running, before)
        running = running + totals[s : s + 1, :]
    count = jnp.max(running).astype(jnp.int32)
    rank = jnp.where(hits > 0.0, (inside + before)[0:rows, :], -1.0)
    code = code.astype(F32)

    def listing(chunk, carry):
        slot = (sq_row + chunk * BLK).astype(F32)
        found = jnp.zeros((BLK, BLK), F32)
        for c in range(rows):
            found = found + jnp.where(rank[c : c + 1, :] == slot, code[c : c + 1, :], 0.0)
        lst[pl.ds(chunk, 1), :] = jnp.sum(found.T, axis=0, keepdims=True).astype(jnp.int32)
        return carry

    listing(0, 0)
    lax.fori_loop(1, (count + BLK - 1) // BLK, listing, 0)
    copy = pltpu.make_async_copy(lst, smem, sem)
    copy.start()
    return copy, count


def send_kernel(turn_no, rec_t, rec_z, send, lst, smem, cnt, sem):
    zz = lax.axis_index("z")
    xx = lax.axis_index("x")
    rnd = turn_no[0]
    ai, bi = group_pairs(rec_t)
    own_a, own_b = ai >> 4, bi >> 4
    xa, xb = own_a & 3, own_b & 3
    to_a = ((own_a >> 2) == zz) & (xa != xx) & (xb == xx)
    to_b = ((own_b >> 2) == zz) & (xb != xx) & (xa == xx)
    code = jnp.where(to_a, xa * 512 + bi, xb * 512 + ai)
    copy, count = list_hits(to_a | to_b, code, lst, smem, sem)
    send[...] = jnp.zeros_like(send)
    for x in range(NX):
        cnt[x] = 0
    copy.wait()

    def deliver(i, carry):
        entry = smem[i >> 7, i & 127]
        f = entry & 511
        x = entry >> 9
        slot = cnt[x] - rnd * CAP
        cnt[x] = cnt[x] + 1

        @pl.when((slot >= 0) & (slot < CAP))
        def _():
            source = (f >> 6) * ROWS + (f & 15)
            target = x * SECT + slot
            send[pl.ds(target, 8, stride=CAP), :] = rec_z[pl.ds(source, 8, stride=NB), :]
            send[pl.ds(target + 8 * CAP, 1), :] = rec_z[pl.ds(source + 8 * NB, 1), :]

        return carry

    lax.fori_loop(0, count, deliver, 0)


def rounds_needed(ai, bi):
    own_a, own_b = ai >> 4, bi >> 4
    owner, column = [], []
    for here, there in ((own_a, own_b), (own_b, own_a)):
        for i in range(8):
            owner.append((subs(32) == here[i : i + 1, :]).astype(BF16))
            column.append((subs(16) == (there[i : i + 1, :] & 3)).astype(BF16))
    owner, column = jnp.concatenate(owner, axis=1), jnp.concatenate(column, axis=1)
    need = lax.dot_general(owner, column, NT, preferred_element_type=F32)
    r32 = lax.broadcasted_iota(jnp.int32, (32, 16), 0)
    c32 = lax.broadcasted_iota(jnp.int32, (32, 16), 1)
    longest = jnp.max(jnp.where((r32 & 3) == c32, 0.0, need)).astype(jnp.int32)
    return (longest + CAP - 1) // CAP


def list_tasks(rec_t, lst, smem, sem):
    me = lax.axis_index("z") * NX + lax.axis_index("x")
    ai, bi = group_pairs(rec_t)
    fa, fb = (ai >> 4) == me, (bi >> 4) == me
    swapped = (bi & 15) * 512 + ai
    hits = jnp.concatenate([(fa | fb).astype(F32), (fa & fb).astype(F32)], axis=0)
    code = jnp.concatenate([jnp.where(fa, (ai & 15) * 512 + bi, swapped), swapped], axis=0)
    return list_hits(hits > 0.0, code, lst, smem, sem)


def place_tasks(rnd, count, tasks, smem, cnt):
    xx = lax.axis_index("x")
    for x in range(NX):
        cnt[x] = 0

    def receive(i, at):
        entry = smem[i >> 7, i & 127]
        f = entry & 511
        column = (f >> 4) & 3
        here = column == xx
        slot = cnt[column] - rnd * CAP
        cnt[column] = cnt[column] + 1
        base = jnp.where(here, LOCAL + (f >> 6) * ROWS + (f & 15), column * SECT + slot)
        use = jnp.where(here, rnd == 0, (slot >= 0) & (slot < CAP))
        tasks[at] = base | ((entry >> 9) << 12)
        return at + use.astype(jnp.int32)

    used = lax.fori_loop(0, count, receive, 0)
    for u in range(8):
        tasks[used + u] = PAD
    tasks[COUNT] = used


def tasks_kernel(turn_no, rec_t, tasks, lst, smem, cnt, sem):
    copy, count = list_tasks(rec_t, lst, smem, sem)
    copy.wait()
    place_tasks(turn_no[0], count, tasks, smem, cnt)


def outer_rows(row, symmetric):
    s = subs(16)
    t = [jnp.broadcast_to(row(3 + r), (16, BLK)) for r in range(3)]
    b = [jnp.broadcast_to(row(6 + q), (16, BLK)) for q in range(3)]

    def slow(v):
        return jnp.where(s < 3, v[0], jnp.where(s < 6, v[1], v[2]))

    def fast(v):
        first = (s == 0) | (s == 3) | (s == 6)
        return jnp.where(first, v[0], jnp.where((s == 1) | (s == 4) | (s == 7), v[1], v[2]))

    o = slow(b) * fast(t)
    return o + 0.5 * (fast(b) * slow(t)) if symmetric else o


def other_side(rows, points):
    one, two, three = [x.astype(F32) for x in split(rows)]
    points = jnp.concatenate(points + [jnp.zeros((29, BLK), F32)], axis=0)
    return jnp.concatenate([one, two, one, three, two, one, points], axis=0).T


def own_side(row):
    o = jnp.where(subs(16) < 9, outer_rows(row, False), 0.0)
    one, two, three = split(o)
    return jnp.concatenate([one, one, two, one, two, three, jnp.zeros((32, BLK), BF16)], axis=0)


def own_sides(own, sides):
    for k in range(NB):
        sides[k] = own_side(lambda r: own[r * NB + k : r * NB + k + 1, :])


def spread(turned):
    return [jnp.broadcast_to(turned[:, 96 + a : 97 + a], (BLK, BLK)) for a in range(3)]


def fold(v):
    total = v[0:8, :]
    for i in range(1, BLK // 8):
        total = total + v[8 * i : 8 * i + 8, :]
    return total


def pull(other, there, mine, here, core, drop=None):
    c = jnp.dot(other, mine, preferred_element_type=F32)
    if drop is not None:
        c = jnp.where(subs(BLK) == drop, 0.0, c)
    d = [here[a] - there[a] for a in range(3)]
    inv = lax.rsqrt(d[0] * d[0] + d[1] * d[1] + (d[2] * d[2] + core))
    w = c * (inv * inv * inv)
    return [fold(w * d[a]) for a in range(3)]


def point_columns():
    row = lax.broadcasted_iota(jnp.int32, (BLK, 3 * BLK), 0) - 96
    axis = lax.broadcasted_iota(jnp.int32, (BLK, 3 * BLK), 1) // BLK
    return ((row == axis) | (row == axis + 3) | (row == axis + 6)).astype(BF16)


def source_pull(row, limit, mine, here, columns):
    rows = jnp.where(subs(16) < limit, outer_rows(row, True), 0.0)
    one, two, three = split(rows)
    s = subs(16)
    p = [row(a) for a in range(3)]
    points = jnp.concatenate(p + p + p + [jnp.zeros((7, BLK), F32)], axis=0)
    p1, p2, p3 = [x.astype(F32) for x in split(points)]
    pieces = jnp.where(s < 3, p1, jnp.where(s < 6, p2, p3)).astype(BF16)
    side = jnp.concatenate([one, two, one, three, two, one, pieces, jnp.zeros((16, BLK), BF16)], axis=0).T
    spots = jnp.dot(side, columns, preferred_element_type=F32)
    there = [spots[:, a * BLK : (a + 1) * BLK] for a in range(3)]
    return pull(side, there, mine, here, NEAR_CORE)


def write_forces(acc, forces, so_far=None):
    for k in range(NB):
        cols = slice(k * BLK, (k + 1) * BLK)
        rows = jnp.concatenate([jnp.sum(acc[k, a], axis=0, keepdims=True) for a in range(3)], axis=0)
        forces[:, cols] = rows if so_far is None else so_far[:, cols] + rows


def own_kernel(own, forces, acc):
    columns = point_columns()

    def step(i, carry):
        for u in range(4):
            k = 4 * i + u

            def row(r):
                return own[pl.ds(r * NB + k, 1), :]

            same = source_pull(row, 9, own_side(row), [row(a) for a in range(3)], columns)
            for a in range(3):
                acc[k, a] = same[a]
        return carry

    lax.fori_loop(0, NB // 4, step, 0)
    write_forces(acc, forces)


def far_kernel(own, rec_t, cells, centers, so_far, forces, rounds, tasks, there, sides, acc, lst, smem, cnt, sem):
    copy, count = list_tasks(rec_t, lst, smem, sem)
    rounds[0] = rounds_needed(*group_pairs(rec_t))
    others = []
    for half in range(2):
        rows = jnp.zeros((8, BLK), F32)
        last = jnp.zeros((8, BLK), F32)
        for i in range(4):
            at = (half * 4 + i) * 32
            tile = rec_t[at : at + 8, :]
            for x in range(1, NX):
                tile = tile + rec_t[at + 8 * x : at + 8 * x + 8, :]
            low = jnp.where((lanes(8) >= 64) & (lanes(8) < 96), tile, 0.0)
            high = jnp.where(lanes(8) >= 96, tile, 0.0)
            rows = rows + (pltpu.roll(low, (32 * i + 64) % 128, 1) if i != 2 else low)
            last = last + (pltpu.roll(high, (32 * i + 32) % 128, 1) if i != 3 else high)
        rows = jnp.concatenate([rows, last[0:1, :], jnp.zeros((7, BLK), F32)], axis=0)
        cols = slice(half * BLK, (half + 1) * BLK)
        turned = other_side(rows, [centers[a : a + 1, cols] for a in range(3)])
        others.append(turned.astype(BF16))
        for a, point in enumerate(spread(turned)):
            there[half, a] = point
    own_sides(own, sides)

    def step(i, carry):
        for u in range(2):
            k = 2 * i + u
            here = [own[pl.ds(a * NB + k, 1), :] for a in range(3)]
            parts = [
                pull(others[h], [there[h, a] for a in range(3)], sides[k], here, FAR_CORE, cells[k] - h * BLK)
                for h in range(2)
            ]
            for a in range(3):
                acc[k, a] = parts[0][a] + parts[1][a]
        return carry

    lax.fori_loop(0, NB // 2, step, 0)
    write_forces(acc, forces, so_far)
    copy.wait()
    place_tasks(0, count, tasks, smem, cnt)


def near_kernel(rec_x, rec_z, tasks, own, so_far, mobility, forces, tops, sides, acc):
    acc[...] = jnp.zeros_like(acc)
    own_sides(own, sides)
    columns = point_columns()

    def pair_step(i, carry):
        for u in range(UNROLL):
            entry = tasks[UNROLL * i + u]
            base = entry & 4095
            k = (entry >> 12) & 15
            here = base >= LOCAL
            at_z = jnp.where(here, base - LOCAL, 0)
            at_x = jnp.where(here, 0, base)

            def row(r):
                return jnp.where(here, rec_z[pl.ds(at_z + r * NB, 1), :], rec_x[pl.ds(at_x + r * CAP, 1), :])

            mine = [own[pl.ds(a * NB + k, 1), :] for a in range(3)]
            near = source_pull(row, jnp.where(entry >= PAD, 0, 9), sides[k], mine, columns)
            for a in range(3):
                acc[k, a] = acc[k, a] + near[a]
        return carry

    lax.fori_loop(0, (tasks[COUNT] + UNROLL - 1) // UNROLL, pair_step, 0)
    write_forces(acc, forces, so_far)
    v = mobility[...] * forces[...]
    speed = jnp.sum(v * v, axis=0, keepdims=True)
    tops[...] = jnp.broadcast_to(jnp.max(speed, axis=1, keepdims=True), tops.shape)


def step_kernel(tops, forces, mobility, out):
    best = jnp.max(jnp.max(tops[...], axis=0, keepdims=True), axis=1, keepdims=True)
    scale = STEP_LIMIT / (jnp.sqrt(best) + 1e-06)
    out[...] = scale * (mobility[...] * forces[...])


def shape(*dims, kind=F32):
    return jax.ShapeDtypeStruct(dims, kind)


def cost(flops):
    return pl.CostEstimate(flops=flops, bytes_accessed=1, transcendentals=0)


def body(segments, pair_blocks, block_cells, mobility, cell_centers):
    small = pltpu.CompilerParams(vmem_limit_bytes=6 * 1024 * 1024)
    seg_count = segments.shape[1]
    devices = 8 * NG * NX
    mob = mobility[None, :]
    packed, own = pl.pallas_call(
        pack_kernel,
        out_shape=(shape(NZ * ROWS, BLK), shape(ROWS, BLK)),
        in_specs=[VMEM, SMEM, VMEM],
        out_specs=(VMEM, VMEM),
        name="pack",
    )(segments, block_cells, pair_blocks.T)
    rec_z = lax.all_to_all(packed.reshape(NZ, ROWS, BLK), "z", 0, 0, tiled=True).reshape(NZ * ROWS, BLK)
    sides = pltpu.VMEM((NB, BLK, BLK), BF16)
    sums = pltpu.VMEM((NB, 3, 8, BLK), F32)
    same = pl.pallas_call(
        own_kernel,
        out_shape=shape(3, seg_count),
        in_specs=[VMEM],
        out_specs=VMEM,
        scratch_shapes=[sums],
        compiler_params=small,
        cost_estimate=cost(10**9),
        name="own",
    )(own)
    rec_z, same = lax.optimization_barrier((rec_z, same))
    column = pl.pallas_call(
        column_kernel,
        out_shape=shape(NG * NX * 8, BLK),
        grid=(1,),
        in_specs=[pl.BlockSpec((8, BLK), lambda i, s=s: ((s * ROWS + EXTRA) // 8, 0)) for s in range(NZ)],
        out_specs=pl.BlockSpec((NG * NX * 8, BLK), lambda i: (0, 0)),
        compiler_params=small,
        name="column",
    )(*([rec_z] * NZ))
    rec_t = lax.all_to_all(column.reshape(NG * NX, 8, BLK), ("y", "c", "x"), 0, 0, tiled=True)
    rec_t = rec_t.reshape(NG * NX * 8, BLK)

    def lists(rows):
        return [
            pltpu.VMEM((rows, BLK), jnp.int32),
            pltpu.SMEM((rows, BLK), jnp.int32),
            pltpu.SMEM((NX,), jnp.int32),
            pltpu.SemaphoreType.DMA,
        ]

    def to_send(number):
        return pl.pallas_call(
            send_kernel,
            out_shape=shape(NX * SECT, BLK),
            in_specs=[SMEM, VMEM, VMEM],
            out_specs=VMEM,
            scratch_shapes=lists(8),
            compiler_params=small,
            name="send",
        )(number, rec_t, rec_z).reshape(NX, SECT, BLK)

    def to_do(number):
        return pl.pallas_call(
            tasks_kernel,
            out_shape=shape(TASKS + 128, kind=jnp.int32),
            in_specs=[SMEM, VMEM],
            out_specs=SMEM,
            scratch_shapes=lists(16),
            compiler_params=small,
            cost_estimate=cost(1),
            name="tasks",
        )(number, rec_t)

    def add_near(rec_x, tasks, so_far):
        return pl.pallas_call(
            near_kernel,
            out_shape=(shape(3, seg_count), shape(devices, BLK)),
            in_specs=[VMEM, VMEM, SMEM, VMEM, VMEM, VMEM],
            out_specs=(VMEM, VMEM),
            scratch_shapes=[sides, sums],
            compiler_params=small,
            name="near",
        )(rec_x, rec_z, tasks, own, so_far, mob)

    first = jnp.zeros((1,), jnp.int32)
    rec_x = lax.all_to_all(to_send(first), "x", 0, 0, tiled=True)
    home, rounds, tasks = pl.pallas_call(
        far_kernel,
        out_shape=(shape(3, seg_count), shape(1, kind=jnp.int32), shape(TASKS + 128, kind=jnp.int32)),
        in_specs=[VMEM, VMEM, SMEM, VMEM, VMEM],
        out_specs=(VMEM, SMEM, SMEM),
        scratch_shapes=[pltpu.VMEM((2, 3, BLK, BLK), F32), sides, sums] + lists(16),
        compiler_params=small,
        cost_estimate=cost(1),
        name="far",
    )(own, rec_t, block_cells, cell_centers, same)

    def more(carry):
        left, so_far = carry
        number = left - 1
        send = to_send(number)
        late = to_do(number)
        x = lax.axis_index("x")
        got = jnp.zeros_like(send)
        for k in range(1, NX):
            part = lax.dynamic_index_in_dim(send, (x + k) % NX, 0, keepdims=True)
            part = lax.ppermute(part, "x", [(i, (i + k) % NX) for i in range(NX)])
            got = lax.dynamic_update_slice_in_dim(got, part, (x + NX - k) % NX, 0)
        return number, add_near(got.reshape(NX * SECT, BLK), late, so_far)[0]

    _, home = lax.while_loop(lambda c: c[0][0] > 1, more, (rounds, home))
    forces, tops = add_near(rec_x.reshape(NX * SECT, BLK), tasks, home)
    tops = lax.all_to_all(tops.reshape(devices, 1, BLK), ("y", "c", "z", "x"), 0, 0, tiled=True)
    displacement = pl.pallas_call(
        step_kernel,
        out_shape=shape(3, seg_count),
        in_specs=[VMEM, VMEM, VMEM],
        out_specs=VMEM,
        compiler_params=small,
        name="step",
    )(tops.reshape(devices, BLK), forces, mob)
    return forces, displacement


def solution(mesh):
    names = ("y", "c", "z", "x")
    fine = Mesh(mesh.devices.reshape(NG // 2, 2, NZ, NX), names)
    in_specs = (P(None, names), P(names, None), P(names), P(names), P())
    out_specs = (P(None, names), P(None, names))
    return jax.shard_map(body, mesh=fine, in_specs=in_specs, out_specs=out_specs, check_vma=False)
```

```python
import jax
import jax.numpy as jnp
from jax import lax
from jax.experimental import pallas as pl
from jax.experimental.pallas import tpu as pltpu
from jax.sharding import Mesh
from jax.sharding import PartitionSpec as P

NEAR_CORE = 0.25
FAR_CORE = 1.0
STEP_LIMIT = 0.5
BLK = 128
NB = 16
NZ = 8
NX = 4
NG = 8
EXTRA = 9 * NB
ROWS = EXTRA + 8
CAP = 20
SECT = 9 * CAP + 4
TASKS = 2048
COUNT = TASKS + 64
UNROLL = 4
PAD = 1 << 16
F32 = jnp.float32
BF16 = jnp.bfloat16
VMEM = pl.BlockSpec(memory_space=pltpu.VMEM)
SMEM = pl.BlockSpec(memory_space=pltpu.SMEM)
NT = (((1,), (1,)), ((), ()))


def lanes(rows):
    return lax.broadcasted_iota(jnp.int32, (rows, BLK), 1)


def subs(rows):
    return lax.broadcasted_iota(jnp.int32, (rows, BLK), 0)


def split(x):
    one = x.astype(BF16)
    rest = x - one.astype(F32)
    two = rest.astype(BF16)
    three = (rest - two.astype(F32)).astype(BF16)
    return one, two, three


def pack_kernel(seg, cells, pairs, packed, out):
    for k in range(NB):
        cols = slice(k * BLK, (k + 1) * BLK)
        out[pl.ds(k, 8, stride=NB), :] = seg[0:8, cols]
        out[8 * NB + k : 8 * NB + k + 1, :] = seg[8:9, cols]
    row = subs(NB)
    cell = jnp.zeros((NB, BLK), jnp.int32)
    for k in range(NB):
        cell = jnp.where(row == k, cells[k] & 31, cell)
    hot = (lanes(NB) == cell + 64).astype(F32)
    hot_last = (lanes(NB) == cell + 96).astype(F32)
    rows = []
    for q in range(3):
        for r in range(3):
            outer = out[(6 + q) * NB : (7 + q) * NB, :] * out[(3 + r) * NB : (4 + r) * NB, :]
            total = jnp.sum(outer, axis=1, keepdims=True)
            rows.append(jnp.sum(total * (hot_last if q + r == 4 else hot), axis=0, keepdims=True))
    out[EXTRA : EXTRA + 1, :] = rows[0] + rows[8]
    for r in range(1, 8):
        out[EXTRA + r : EXTRA + r + 1, :] = rows[r]
    out[EXTRA : EXTRA + 2, 0:32] = pairs[...].astype(F32)
    whole = out[...]
    for copy in range(NZ):
        packed[copy * ROWS : (copy + 1) * ROWS, :] = whole


def column_kernel(*refs):
    out = refs[NZ]
    lane = lanes(8)
    first = jnp.concatenate([ref[0:1, :] for ref in refs[:NZ]], axis=0)
    second = jnp.concatenate([ref[1:2, :] for ref in refs[:NZ]], axis=0)
    total = refs[0][...]
    for ref in refs[1:NZ]:
        total = total + ref[...]
    tile = jnp.where(lane < 32, first, jnp.where(lane < 64, pltpu.roll(second, 32, 1), total))
    for copy in range(NG * NX):
        out[8 * copy : 8 * copy + 8, :] = tile


def group_pairs(rec_t):
    g = lax.axis_index("y") * 2 + lax.axis_index("c")
    lane = lanes(8)
    a = jnp.zeros((8, BLK), F32)
    b = jnp.zeros((8, BLK), F32)
    for x in range(NX):
        part = rec_t[pl.ds(pl.multiple_of(g * 32 + x * 8, 8), 8), :]
        one = jnp.where(lane < 32, part, 0.0)
        two = jnp.where((lane >= 32) & (lane < 64), part, 0.0)
        a = a + (pltpu.roll(one, 32 * x, 1) if x else one)
        b = b + (pltpu.roll(two, (32 * x + 96) % 128, 1) if x != 1 else two)
    return a.astype(jnp.int32), b.astype(jnp.int32)


def list_hits(hit, code, lst, smem, sem):
    rows = hit.shape[0]
    hits = hit.astype(F32)
    hot = jnp.concatenate([hits, jnp.zeros((16 - rows, BLK), F32)], axis=0) if rows < 16 else hits
    hot = hot.astype(BF16)
    sq_row, sq_lane = subs(BLK), lanes(BLK)
    inside = jnp.dot(hot, (sq_row < sq_lane).astype(BF16), preferred_element_type=F32)
    totals = jnp.dot(hot, jnp.ones((BLK, BLK), BF16), preferred_element_type=F32)
    before = jnp.zeros((16, BLK), F32)
    running = jnp.zeros((1, BLK), F32)
    for s in range(rows):
        before = jnp.where(subs(16) == s, running, before)
        running = running + totals[s : s + 1, :]
    count = jnp.max(running).astype(jnp.int32)
    rank = jnp.where(hits > 0.0, (inside + before)[0:rows, :], -1.0)
    code = code.astype(F32)

    def listing(chunk, carry):
        slot = (sq_row + chunk * BLK).astype(F32)
        found = jnp.zeros((BLK, BLK), F32)
        for c in range(rows):
            found = found + jnp.where(rank[c : c + 1, :] == slot, code[c : c + 1, :], 0.0)
        lst[pl.ds(chunk, 1), :] = jnp.sum(found.T, axis=0, keepdims=True).astype(jnp.int32)
        return carry

    listing(0, 0)
    lax.fori_loop(1, (count + BLK - 1) // BLK, listing, 0)
    copy = pltpu.make_async_copy(lst, smem, sem)
    copy.start()
    return copy, count


def send_kernel(turn_no, rec_t, rec_z, send, lst, smem, cnt, sem):
    zz = lax.axis_index("z")
    xx = lax.axis_index("x")
    rnd = turn_no[0]
    ai, bi = group_pairs(rec_t)
    own_a, own_b = ai >> 4, bi >> 4
    xa, xb = own_a & 3, own_b & 3
    to_a = ((own_a >> 2) == zz) & (xa != xx) & (xb == xx)
    to_b = ((own_b >> 2) == zz) & (xb != xx) & (xa == xx)
    code = jnp.where(to_a, xa * 512 + bi, xb * 512 + ai)
    copy, count = list_hits(to_a | to_b, code, lst, smem, sem)
    send[...] = jnp.zeros_like(send)
    for x in range(NX):
        cnt[x] = 0
    copy.wait()

    def deliver(i, carry):
        entry = smem[i >> 7, i & 127]
        f = entry & 511
        x = entry >> 9
        slot = cnt[x] - rnd * CAP
        cnt[x] = cnt[x] + 1

        @pl.when((slot >= 0) & (slot < CAP))
        def _():
            source = (f >> 6) * ROWS + (f & 15)
            target = x * SECT + slot
            send[pl.ds(target, 8, stride=CAP), :] = rec_z[pl.ds(source, 8, stride=NB), :]
            send[pl.ds(target + 8 * CAP, 1), :] = rec_z[pl.ds(source + 8 * NB, 1), :]

        return carry

    lax.fori_loop(0, count, deliver, 0)


def rounds_needed(ai, bi):
    own_a, own_b = ai >> 4, bi >> 4
    owner, column = [], []
    for here, there in ((own_a, own_b), (own_b, own_a)):
        for i in range(8):
            owner.append((subs(32) == here[i : i + 1, :]).astype(BF16))
            column.append((subs(16) == (there[i : i + 1, :] & 3)).astype(BF16))
    owner, column = jnp.concatenate(owner, axis=1), jnp.concatenate(column, axis=1)
    need = lax.dot_general(owner, column, NT, preferred_element_type=F32)
    r32 = lax.broadcasted_iota(jnp.int32, (32, 16), 0)
    c32 = lax.broadcasted_iota(jnp.int32, (32, 16), 1)
    longest = jnp.max(jnp.where((r32 & 3) == c32, 0.0, need)).astype(jnp.int32)
    return (longest + CAP - 1) // CAP


def list_tasks(rec_t, lst, smem, sem):
    me = lax.axis_index("z") * NX + lax.axis_index("x")
    ai, bi = group_pairs(rec_t)
    fa, fb = (ai >> 4) == me, (bi >> 4) == me
    swapped = (bi & 15) * 512 + ai
    hits = jnp.concatenate([(fa | fb).astype(F32), (fa & fb).astype(F32)], axis=0)
    code = jnp.concatenate([jnp.where(fa, (ai & 15) * 512 + bi, swapped), swapped], axis=0)
    return list_hits(hits > 0.0, code, lst, smem, sem)


def place_tasks(rnd, count, local, tasks, smem, cnt):
    xx = lax.axis_index("x")
    for x in range(NX):
        cnt[x] = 0

    def receive(i, carry):
        at_local, at = carry
        entry = smem[i >> 7, i & 127]
        f = entry & 511
        k = (entry >> 9) << 12
        column = (f >> 4) & 3
        here = column == xx
        slot = cnt[column] - rnd * CAP
        cnt[column] = cnt[column] + 1
        local[at_local] = ((f >> 6) * ROWS + (f & 15)) | k
        tasks[at] = (column * SECT + slot) | k
        use = jnp.logical_not(here) & (slot >= 0) & (slot < CAP)
        return at_local + here.astype(jnp.int32), at + use.astype(jnp.int32)

    used_local, used = lax.fori_loop(0, count, receive, (0, 0))
    for u in range(8):
        local[used_local + u] = PAD
        tasks[used + u] = PAD
    tasks[COUNT] = used
    return used_local


def run_tasks(listed, count, blocks, apart, own, sides, acc):
    columns = point_columns()

    def step(i, carry):
        for u in range(UNROLL):
            entry = listed[UNROLL * i + u]
            base = entry & 4095
            k = (entry >> 12) & 15

            def row(r):
                return blocks[pl.ds(base + r * apart, 1), :]

            here = [own[pl.ds(a * NB + k, 1), :] for a in range(3)]
            near = source_pull(row, jnp.where(entry >= PAD, 0, 9), sides[k], here, columns)
            for a in range(3):
                acc[k, a] = acc[k, a] + near[a]
        return carry

    lax.fori_loop(0, (count + UNROLL - 1) // UNROLL, step, 0)


def tasks_kernel(turn_no, rec_t, tasks, lst, smem, cnt, sem, local):
    copy, count = list_tasks(rec_t, lst, smem, sem)
    copy.wait()
    place_tasks(turn_no[0], count, local, tasks, smem, cnt)


def outer_rows(row, symmetric):
    s = subs(16)
    t = [jnp.broadcast_to(row(3 + r), (16, BLK)) for r in range(3)]
    b = [jnp.broadcast_to(row(6 + q), (16, BLK)) for q in range(3)]

    def slow(v):
        return jnp.where(s < 3, v[0], jnp.where(s < 6, v[1], v[2]))

    def fast(v):
        first = (s == 0) | (s == 3) | (s == 6)
        return jnp.where(first, v[0], jnp.where((s == 1) | (s == 4) | (s == 7), v[1], v[2]))

    o = slow(b) * fast(t)
    return o + 0.5 * (fast(b) * slow(t)) if symmetric else o


def other_side(rows, points):
    one, two, three = [x.astype(F32) for x in split(rows)]
    points = jnp.concatenate(points + [jnp.zeros((29, BLK), F32)], axis=0)
    return jnp.concatenate([one, two, one, three, two, one, points], axis=0).T


def own_side(row):
    o = jnp.where(subs(16) < 9, outer_rows(row, False), 0.0)
    one, two, three = split(o)
    return jnp.concatenate([one, one, two, one, two, three, jnp.zeros((32, BLK), BF16)], axis=0)


def own_sides(own, sides):
    for k in range(NB):
        sides[k] = own_side(lambda r: own[r * NB + k : r * NB + k + 1, :])


def spread(turned):
    return [jnp.broadcast_to(turned[:, 96 + a : 97 + a], (BLK, BLK)) for a in range(3)]


def fold(v):
    total = v[0:8, :]
    for i in range(1, BLK // 8):
        total = total + v[8 * i : 8 * i + 8, :]
    return total


def pull(other, there, mine, here, core, drop=None):
    c = jnp.dot(other, mine, preferred_element_type=F32)
    if drop is not None:
        c = jnp.where(subs(BLK) == drop, 0.0, c)
    d = [here[a] - there[a] for a in range(3)]
    inv = lax.rsqrt(d[0] * d[0] + d[1] * d[1] + (d[2] * d[2] + core))
    w = c * (inv * inv * inv)
    return [fold(w * d[a]) for a in range(3)]


def point_columns():
    row = lax.broadcasted_iota(jnp.int32, (BLK, 3 * BLK), 0) - 96
    axis = lax.broadcasted_iota(jnp.int32, (BLK, 3 * BLK), 1) // BLK
    return ((row == axis) | (row == axis + 3) | (row == axis + 6)).astype(BF16)


def source_pull(row, limit, mine, here, columns):
    rows = jnp.where(subs(16) < limit, outer_rows(row, True), 0.0)
    one, two, three = split(rows)
    s = subs(16)
    p = [row(a) for a in range(3)]
    points = jnp.concatenate(p + p + p + [jnp.zeros((7, BLK), F32)], axis=0)
    p1, p2, p3 = [x.astype(F32) for x in split(points)]
    pieces = jnp.where(s < 3, p1, jnp.where(s < 6, p2, p3)).astype(BF16)
    side = jnp.concatenate([one, two, one, three, two, one, pieces, jnp.zeros((16, BLK), BF16)], axis=0).T
    spots = jnp.dot(side, columns, preferred_element_type=F32)
    there = [spots[:, a * BLK : (a + 1) * BLK] for a in range(3)]
    return pull(side, there, mine, here, NEAR_CORE)


def write_forces(acc, forces, so_far=None):
    for k in range(NB):
        cols = slice(k * BLK, (k + 1) * BLK)
        rows = jnp.concatenate([jnp.sum(acc[k, a], axis=0, keepdims=True) for a in range(3)], axis=0)
        forces[:, cols] = rows if so_far is None else so_far[:, cols] + rows


def own_kernel(own, forces, acc):
    columns = point_columns()

    def step(i, carry):
        for u in range(4):
            k = 4 * i + u

            def row(r):
                return own[pl.ds(r * NB + k, 1), :]

            same = source_pull(row, 9, own_side(row), [row(a) for a in range(3)], columns)
            for a in range(3):
                acc[k, a] = same[a]
        return carry

    lax.fori_loop(0, NB // 4, step, 0)
    write_forces(acc, forces)


def far_kernel(
    own, rec_t, rec_z, cells, centers, so_far, forces, rounds, tasks, there, sides, acc, lst, smem, cnt, sem, local
):
    copy, count = list_tasks(rec_t, lst, smem, sem)
    rounds[0] = rounds_needed(*group_pairs(rec_t))
    others = []
    for half in range(2):
        rows = jnp.zeros((8, BLK), F32)
        last = jnp.zeros((8, BLK), F32)
        for i in range(4):
            at = (half * 4 + i) * 32
            tile = rec_t[at : at + 8, :]
            for x in range(1, NX):
                tile = tile + rec_t[at + 8 * x : at + 8 * x + 8, :]
            low = jnp.where((lanes(8) >= 64) & (lanes(8) < 96), tile, 0.0)
            high = jnp.where(lanes(8) >= 96, tile, 0.0)
            rows = rows + (pltpu.roll(low, (32 * i + 64) % 128, 1) if i != 2 else low)
            last = last + (pltpu.roll(high, (32 * i + 32) % 128, 1) if i != 3 else high)
        rows = jnp.concatenate([rows, last[0:1, :], jnp.zeros((7, BLK), F32)], axis=0)
        cols = slice(half * BLK, (half + 1) * BLK)
        turned = other_side(rows, [centers[a : a + 1, cols] for a in range(3)])
        others.append(turned.astype(BF16))
        for a, point in enumerate(spread(turned)):
            there[half, a] = point
    own_sides(own, sides)

    def step(i, carry):
        for u in range(2):
            k = 2 * i + u
            here = [own[pl.ds(a * NB + k, 1), :] for a in range(3)]
            parts = [
                pull(others[h], [there[h, a] for a in range(3)], sides[k], here, FAR_CORE, cells[k] - h * BLK)
                for h in range(2)
            ]
            for a in range(3):
                acc[k, a] = parts[0][a] + parts[1][a]
        return carry

    lax.fori_loop(0, NB // 2, step, 0)
    copy.wait()
    used = place_tasks(0, count, local, tasks, smem, cnt)
    run_tasks(local, used, rec_z, NB, own, sides, acc)
    write_forces(acc, forces, so_far)


def near_kernel(rec_x, tasks, own, so_far, mobility, forces, tops, sides, acc):
    acc[...] = jnp.zeros_like(acc)
    own_sides(own, sides)
    run_tasks(tasks, tasks[COUNT], rec_x, CAP, own, sides, acc)
    write_forces(acc, forces, so_far)
    v = mobility[...] * forces[...]
    speed = jnp.sum(v * v, axis=0, keepdims=True)
    tops[...] = jnp.broadcast_to(jnp.max(speed, axis=1, keepdims=True), tops.shape)


def step_kernel(tops, forces, mobility, out):
    best = jnp.max(jnp.max(tops[...], axis=0, keepdims=True), axis=1, keepdims=True)
    scale = STEP_LIMIT / (jnp.sqrt(best) + 1e-06)
    out[...] = scale * (mobility[...] * forces[...])


def shape(*dims, kind=F32):
    return jax.ShapeDtypeStruct(dims, kind)


def cost(flops):
    return pl.CostEstimate(flops=flops, bytes_accessed=1, transcendentals=0)


def body(segments, pair_blocks, block_cells, mobility, cell_centers):
    small = pltpu.CompilerParams(vmem_limit_bytes=6 * 1024 * 1024)
    seg_count = segments.shape[1]
    devices = 8 * NG * NX
    mob = mobility[None, :]
    packed, own = pl.pallas_call(
        pack_kernel,
        out_shape=(shape(NZ * ROWS, BLK), shape(ROWS, BLK)),
        in_specs=[VMEM, SMEM, VMEM],
        out_specs=(VMEM, VMEM),
        name="pack",
    )(segments, block_cells, pair_blocks.T)
    rec_z = lax.all_to_all(packed.reshape(NZ, ROWS, BLK), "z", 0, 0, tiled=True).reshape(NZ * ROWS, BLK)
    sides = pltpu.VMEM((NB, BLK, BLK), BF16)
    sums = pltpu.VMEM((NB, 3, 8, BLK), F32)
    same = pl.pallas_call(
        own_kernel,
        out_shape=shape(3, seg_count),
        in_specs=[VMEM],
        out_specs=VMEM,
        scratch_shapes=[sums],
        compiler_params=small,
        cost_estimate=cost(10**9),
        name="own",
    )(own)
    rec_z, same = lax.optimization_barrier((rec_z, same))
    column = pl.pallas_call(
        column_kernel,
        out_shape=shape(NG * NX * 8, BLK),
        grid=(1,),
        in_specs=[pl.BlockSpec((8, BLK), lambda i, s=s: ((s * ROWS + EXTRA) // 8, 0)) for s in range(NZ)],
        out_specs=pl.BlockSpec((NG * NX * 8, BLK), lambda i: (0, 0)),
        compiler_params=small,
        name="column",
    )(*([rec_z] * NZ))
    rec_t = lax.all_to_all(column.reshape(NG * NX, 8, BLK), ("y", "c", "x"), 0, 0, tiled=True)
    rec_t = rec_t.reshape(NG * NX * 8, BLK)

    def lists(rows):
        return [
            pltpu.VMEM((rows, BLK), jnp.int32),
            pltpu.SMEM((rows, BLK), jnp.int32),
            pltpu.SMEM((NX,), jnp.int32),
            pltpu.SemaphoreType.DMA,
        ]

    def to_send(number):
        return pl.pallas_call(
            send_kernel,
            out_shape=shape(NX * SECT, BLK),
            in_specs=[SMEM, VMEM, VMEM],
            out_specs=VMEM,
            scratch_shapes=lists(8),
            compiler_params=small,
            name="send",
        )(number, rec_t, rec_z).reshape(NX, SECT, BLK)

    def to_do(number):
        return pl.pallas_call(
            tasks_kernel,
            out_shape=shape(TASKS + 128, kind=jnp.int32),
            in_specs=[SMEM, VMEM],
            out_specs=SMEM,
            scratch_shapes=lists(16) + [pltpu.SMEM((TASKS + 128,), jnp.int32)],
            compiler_params=small,
            cost_estimate=cost(1),
            name="tasks",
        )(number, rec_t)

    def add_near(rec_x, tasks, so_far):
        return pl.pallas_call(
            near_kernel,
            out_shape=(shape(3, seg_count), shape(devices, BLK)),
            in_specs=[VMEM, SMEM, VMEM, VMEM, VMEM],
            out_specs=(VMEM, VMEM),
            scratch_shapes=[sides, sums],
            compiler_params=small,
            name="near",
        )(rec_x, tasks, own, so_far, mob)

    first = jnp.zeros((1,), jnp.int32)
    rec_x = lax.all_to_all(to_send(first), "x", 0, 0, tiled=True)
    home, rounds, tasks = pl.pallas_call(
        far_kernel,
        out_shape=(shape(3, seg_count), shape(1, kind=jnp.int32), shape(TASKS + 128, kind=jnp.int32)),
        in_specs=[VMEM, VMEM, VMEM, SMEM, VMEM, VMEM],
        out_specs=(VMEM, SMEM, SMEM),
        scratch_shapes=[pltpu.VMEM((2, 3, BLK, BLK), F32), sides, sums]
        + lists(16)
        + [pltpu.SMEM((TASKS + 128,), jnp.int32)],
        compiler_params=small,
        cost_estimate=cost(1),
        name="far",
    )(own, rec_t, rec_z, block_cells, cell_centers, same)

    def more(carry):
        left, so_far = carry
        number = left - 1
        send = to_send(number)
        late = to_do(number)
        x = lax.axis_index("x")
        got = jnp.zeros_like(send)
        for k in range(1, NX):
            part = lax.dynamic_index_in_dim(send, (x + k) % NX, 0, keepdims=True)
            part = lax.ppermute(part, "x", [(i, (i + k) % NX) for i in range(NX)])
            got = lax.dynamic_update_slice_in_dim(got, part, (x + NX - k) % NX, 0)
        return number, add_near(got.reshape(NX * SECT, BLK), late, so_far)[0]

    _, home = lax.while_loop(lambda c: c[0][0] > 1, more, (rounds, home))
    forces, tops = add_near(rec_x.reshape(NX * SECT, BLK), tasks, home)
    tops = lax.all_to_all(tops.reshape(devices, 1, BLK), ("y", "c", "z", "x"), 0, 0, tiled=True)
    displacement = pl.pallas_call(
        step_kernel,
        out_shape=shape(3, seg_count),
        in_specs=[VMEM, VMEM, VMEM],
        out_specs=VMEM,
        compiler_params=small,
        name="step",
    )(tops.reshape(devices, BLK), forces, mob)
    return forces, displacement


def solution(mesh):
    names = ("y", "c", "z", "x")
    fine = Mesh(mesh.devices.reshape(NG // 2, 2, NZ, NX), names)
    in_specs = (P(None, names), P(names, None), P(names), P(names), P())
    out_specs = (P(None, names), P(None, names))
    return jax.shard_map(body, mesh=fine, in_specs=in_specs, out_specs=out_specs, check_vma=False)
```

```python
import jax
import jax.numpy as jnp
from jax import lax
from jax.experimental import pallas as pl
from jax.experimental.pallas import tpu as pltpu
from jax.sharding import Mesh
from jax.sharding import PartitionSpec as P

NEAR_CORE = 0.25
FAR_CORE = 1.0
STEP_LIMIT = 0.5
BLK = 128
NB = 16
NZ = 8
NX = 4
NG = 8
EXTRA = 9 * NB
ROWS = EXTRA + 8
CAP = 14
SECT = 9 * CAP + 2
TASKS = 2048
COUNT = TASKS + 64
UNROLL = 4
PAD = 1 << 16
F32 = jnp.float32
BF16 = jnp.bfloat16
VMEM = pl.BlockSpec(memory_space=pltpu.VMEM)
SMEM = pl.BlockSpec(memory_space=pltpu.SMEM)
NT = (((1,), (1,)), ((), ()))


def lanes(rows):
    return lax.broadcasted_iota(jnp.int32, (rows, BLK), 1)


def subs(rows):
    return lax.broadcasted_iota(jnp.int32, (rows, BLK), 0)


def split(x):
    one = x.astype(BF16)
    rest = x - one.astype(F32)
    two = rest.astype(BF16)
    three = (rest - two.astype(F32)).astype(BF16)
    return one, two, three


def pack_kernel(seg, cells, pairs, packed, out, same_cells):
    for k in range(NB):
        cols = slice(k * BLK, (k + 1) * BLK)
        out[pl.ds(k, 8, stride=NB), :] = seg[0:8, cols]
        out[8 * NB + k : 8 * NB + k + 1, :] = seg[8:9, cols]
    row = subs(NB)
    cell = jnp.zeros((NB, BLK), jnp.int32)
    for k in range(NB):
        cell = jnp.where(row == k, cells[k] & 31, cell)
        same_cells[k] = cells[k]
    hot = (lanes(NB) == cell + 64).astype(F32)
    hot_last = (lanes(NB) == cell + 96).astype(F32)
    rows = []
    for q in range(3):
        for r in range(3):
            outer = out[(6 + q) * NB : (7 + q) * NB, :] * out[(3 + r) * NB : (4 + r) * NB, :]
            total = jnp.sum(outer, axis=1, keepdims=True)
            rows.append(jnp.sum(total * (hot_last if q + r == 4 else hot), axis=0, keepdims=True))
    out[EXTRA : EXTRA + 1, :] = rows[0] + rows[8]
    for r in range(1, 8):
        out[EXTRA + r : EXTRA + r + 1, :] = rows[r]
    out[EXTRA : EXTRA + 2, 0:32] = pairs[...].astype(F32)
    whole = out[...]
    for copy in range(NX):
        packed[copy * ROWS : (copy + 1) * ROWS, :] = whole


def row_kernel(*refs):
    out = refs[NX]
    lane = lanes(8)
    rest = [jnp.zeros((8 - NX, BLK), F32)]
    first = jnp.concatenate([ref[0:1, :] for ref in refs[:NX]] + rest, axis=0)
    second = jnp.concatenate([ref[1:2, :] for ref in refs[:NX]] + rest, axis=0)
    total = refs[0][...]
    for ref in refs[1:NX]:
        total = total + ref[...]
    tile = jnp.where(lane < 32, first, jnp.where(lane < 64, pltpu.roll(second, 32, 1), total))
    for copy in range(NZ):
        out[8 * copy : 8 * copy + 8, :] = tile


def group_pairs(rec_t):
    lane = lanes(8)
    a = jnp.zeros((8, BLK), F32)
    b = jnp.zeros((8, BLK), F32)
    for x in range(NX):
        part = rec_t[pl.ds(x, NZ, stride=8), :]
        one = jnp.where(lane < 32, part, 0.0)
        two = jnp.where((lane >= 32) & (lane < 64), part, 0.0)
        a = a + (pltpu.roll(one, 32 * x, 1) if x else one)
        b = b + (pltpu.roll(two, (32 * x + 96) % 128, 1) if x != 1 else two)
    return a.astype(jnp.int32), b.astype(jnp.int32)


def list_hits(hit, code, lst, smem, sem):
    rows = hit.shape[0]
    hits = hit.astype(F32)
    hot = jnp.concatenate([hits, jnp.zeros((16 - rows, BLK), F32)], axis=0) if rows < 16 else hits
    hot = hot.astype(BF16)
    sq_row, sq_lane = subs(BLK), lanes(BLK)
    inside = jnp.dot(hot, (sq_row < sq_lane).astype(BF16), preferred_element_type=F32)
    totals = jnp.dot(hot, jnp.ones((BLK, BLK), BF16), preferred_element_type=F32)
    before = jnp.zeros((16, BLK), F32)
    running = jnp.zeros((1, BLK), F32)
    for s in range(rows):
        before = jnp.where(subs(16) == s, running, before)
        running = running + totals[s : s + 1, :]
    count = jnp.max(running).astype(jnp.int32)
    rank = jnp.where(hits > 0.0, (inside + before)[0:rows, :], -1.0)
    code = code.astype(F32)

    def listing(chunk, carry):
        slot = (sq_row + chunk * BLK).astype(F32)
        found = jnp.zeros((BLK, BLK), F32)
        for c in range(rows):
            found = found + jnp.where(rank[c : c + 1, :] == slot, code[c : c + 1, :], 0.0)
        lst[pl.ds(chunk, 1), :] = jnp.sum(found.T, axis=0, keepdims=True).astype(jnp.int32)
        return carry

    listing(0, 0)
    lax.fori_loop(1, (count + BLK - 1) // BLK, listing, 0)
    copy = pltpu.make_async_copy(lst, smem, sem)
    copy.start()
    return copy, count


def send_kernel(turn_no, rec_t, rec_x, send, start, none, lst, smem, cnt, sem):
    start[0] = 0
    none[COUNT] = 0
    zz = lax.axis_index("z")
    xx = lax.axis_index("x")
    rnd = turn_no[0]
    ai, bi = group_pairs(rec_t)
    za, zb = ai >> 6, bi >> 6
    to_a = (za != zz) & (((ai >> 4) & 3) == xx) & (zb == zz)
    to_b = (zb != zz) & (((bi >> 4) & 3) == xx) & (za == zz)
    code = jnp.where(to_a, za * 512 + bi, zb * 512 + ai)
    copy, count = list_hits((to_a & (ai >= 0)) | (to_b & (bi >= 0)), code, lst, smem, sem)
    send[...] = jnp.zeros_like(send)
    for z in range(NZ):
        cnt[z] = 0
    copy.wait()

    def deliver(i, carry):
        entry = smem[i >> 7, i & 127]
        f = entry & 511
        z = entry >> 9
        slot = cnt[z] - rnd * CAP
        cnt[z] = cnt[z] + 1

        @pl.when((slot >= 0) & (slot < CAP))
        def _():
            source = ((f >> 4) & 3) * ROWS + (f & 15)
            target = z * SECT + slot
            send[pl.ds(target, 8, stride=CAP), :] = rec_x[pl.ds(source, 8, stride=NB), :]
            send[pl.ds(target + 8 * CAP, 1), :] = rec_x[pl.ds(source + 8 * NB, 1), :]

        return carry

    lax.fori_loop(0, count, deliver, 0)


def rounds_needed(ai, bi):
    own_a, own_b = ai >> 4, bi >> 4
    owner, column = [], []
    for here, there in ((own_a, own_b), (own_b, own_a)):
        for i in range(8):
            owner.append((subs(32) == here[i : i + 1, :]).astype(BF16))
            column.append((subs(16) == (there[i : i + 1, :] >> 2)).astype(BF16))
    owner, column = jnp.concatenate(owner, axis=1), jnp.concatenate(column, axis=1)
    need = lax.dot_general(owner, column, NT, preferred_element_type=F32)
    r32 = lax.broadcasted_iota(jnp.int32, (32, 16), 0)
    c32 = lax.broadcasted_iota(jnp.int32, (32, 16), 1)
    longest = jnp.max(jnp.where((r32 >> 2) == c32, 0.0, need)).astype(jnp.int32)
    return (longest + CAP - 1) // CAP


def list_tasks(rec_t, lst, smem, sem):
    me = lax.axis_index("z") * NX + lax.axis_index("x")
    ai, bi = group_pairs(rec_t)
    fa, fb = (ai >> 4) == me, (bi >> 4) == me
    swapped = (bi & 15) * 512 + ai
    hits = jnp.concatenate([(fa | fb).astype(F32), (fa & fb).astype(F32)], axis=0)
    code = jnp.concatenate([jnp.where(fa, (ai & 15) * 512 + bi, swapped), swapped], axis=0)
    return list_hits(hits > 0.0, code, lst, smem, sem)


def place_tasks(rnd, count, local, tasks, smem, cnt):
    zz = lax.axis_index("z")
    for z in range(NZ):
        cnt[z] = 0

    def receive(i, carry):
        at_local, at = carry
        entry = smem[i >> 7, i & 127]
        f = entry & 511
        k = (entry >> 9) << 12
        z = f >> 6
        here = z == zz
        slot = cnt[z] - rnd * CAP
        cnt[z] = cnt[z] + 1
        local[at_local] = (((f >> 4) & 3) * ROWS + (f & 15)) | k
        tasks[at] = (z * SECT + slot) | k
        use = jnp.logical_not(here) & (slot >= 0) & (slot < CAP)
        return at_local + here.astype(jnp.int32), at + use.astype(jnp.int32)

    used_local, used = lax.fori_loop(0, count, receive, (0, 0))
    for u in range(8):
        local[used_local + u] = PAD
        tasks[used + u] = PAD
    tasks[COUNT] = used
    return used_local


def run_tasks(listed, count, blocks, apart, own, sides, acc):
    columns = point_columns()

    def step(i, carry):
        for u in range(UNROLL):
            entry = listed[UNROLL * i + u]
            base = entry & 4095
            k = (entry >> 12) & 15

            def row(r):
                return blocks[pl.ds(base + r * apart, 1), :]

            here = [own[pl.ds(a * NB + k, 1), :] for a in range(3)]
            near = source_pull(row, jnp.where(entry >= PAD, 0, 9), sides[k], here, columns)
            for a in range(3):
                acc[k, a] = acc[k, a] + near[a]
        return carry

    lax.fori_loop(0, (count + UNROLL - 1) // UNROLL, step, 0)


def tasks_kernel(turn_no, rec_t, tasks, lst, smem, cnt, sem, local):
    copy, count = list_tasks(rec_t, lst, smem, sem)
    copy.wait()
    place_tasks(turn_no[0], count, local, tasks, smem, cnt)


def outer_rows(row, symmetric):
    s = subs(16)
    t = [jnp.broadcast_to(row(3 + r), (16, BLK)) for r in range(3)]
    b = [jnp.broadcast_to(row(6 + q), (16, BLK)) for q in range(3)]

    def slow(v):
        return jnp.where(s < 3, v[0], jnp.where(s < 6, v[1], v[2]))

    def fast(v):
        first = (s == 0) | (s == 3) | (s == 6)
        return jnp.where(first, v[0], jnp.where((s == 1) | (s == 4) | (s == 7), v[1], v[2]))

    o = slow(b) * fast(t)
    return o + 0.5 * (fast(b) * slow(t)) if symmetric else o


def other_side(rows, points):
    one, two, three = [x.astype(F32) for x in split(rows)]
    points = jnp.concatenate(points + [jnp.zeros((29, BLK), F32)], axis=0)
    return jnp.concatenate([one, two, one, three, two, one, points], axis=0).T


def own_side(row):
    o = jnp.where(subs(16) < 9, outer_rows(row, False), 0.0)
    one, two, three = split(o)
    return jnp.concatenate([one, one, two, one, two, three, jnp.zeros((32, BLK), BF16)], axis=0)


def own_sides(own, sides):
    for k in range(NB):
        sides[k] = own_side(lambda r: own[r * NB + k : r * NB + k + 1, :])


def spread(turned):
    return [jnp.broadcast_to(turned[:, 96 + a : 97 + a], (BLK, BLK)) for a in range(3)]


def fold(v):
    total = v[0:8, :]
    for i in range(1, BLK // 8):
        total = total + v[8 * i : 8 * i + 8, :]
    return total


def pull(other, there, mine, here, core, drop=None):
    c = jnp.dot(other, mine, preferred_element_type=F32)
    if drop is not None:
        c = jnp.where(subs(BLK) == drop, 0.0, c)
    d = [here[a] - there[a] for a in range(3)]
    inv = lax.rsqrt(d[0] * d[0] + d[1] * d[1] + (d[2] * d[2] + core))
    w = c * (inv * inv * inv)
    return [fold(w * d[a]) for a in range(3)]


def point_columns():
    row = lax.broadcasted_iota(jnp.int32, (BLK, 3 * BLK), 0) - 96
    axis = lax.broadcasted_iota(jnp.int32, (BLK, 3 * BLK), 1) // BLK
    return ((row == axis) | (row == axis + 3) | (row == axis + 6)).astype(BF16)


def source_pull(row, limit, mine, here, columns):
    rows = jnp.where(subs(16) < limit, outer_rows(row, True), 0.0)
    one, two, three = split(rows)
    s = subs(16)
    p = [row(a) for a in range(3)]
    points = jnp.concatenate(p + p + p + [jnp.zeros((7, BLK), F32)], axis=0)
    p1, p2, p3 = [x.astype(F32) for x in split(points)]
    pieces = jnp.where(s < 3, p1, jnp.where(s < 6, p2, p3)).astype(BF16)
    side = jnp.concatenate([one, two, one, three, two, one, pieces, jnp.zeros((16, BLK), BF16)], axis=0).T
    spots = jnp.dot(side, columns, preferred_element_type=F32)
    there = [spots[:, a * BLK : (a + 1) * BLK] for a in range(3)]
    return pull(side, there, mine, here, NEAR_CORE)


def write_forces(acc, forces, so_far=None):
    for k in range(NB):
        cols = slice(k * BLK, (k + 1) * BLK)
        rows = jnp.concatenate([jnp.sum(acc[k, a], axis=0, keepdims=True) for a in range(3)], axis=0)
        forces[:, cols] = rows if so_far is None else so_far[:, cols] + rows


def own_kernel(own, forces, acc):
    columns = point_columns()

    def step(i, carry):
        for u in range(4):
            k = 4 * i + u

            def row(r):
                return own[pl.ds(r * NB + k, 1), :]

            same = source_pull(row, 9, own_side(row), [row(a) for a in range(3)], columns)
            for a in range(3):
                acc[k, a] = same[a]
        return carry

    lax.fori_loop(0, NB // 4, step, 0)
    write_forces(acc, forces)


def row_pairs_kernel(own, rec_t, rec_x, so_far, forces, rounds, tasks, sides, acc, lst, smem, cnt, sem, local):
    copy, count = list_tasks(rec_t, lst, smem, sem)
    rounds[0] = rounds_needed(*group_pairs(rec_t))
    own_sides(own, sides)
    acc[...] = jnp.zeros_like(acc)
    copy.wait()
    used = place_tasks(0, count, local, tasks, smem, cnt)
    run_tasks(local, used, rec_x, NB, own, sides, acc)
    write_forces(acc, forces, so_far)


def far_kernel(own, m0, m1, m2, m3, cells, centers, so_far, forces, there, sides, acc):
    lane = lanes(8)
    parts = []
    for i, ref in enumerate((m0, m1, m2, m3)):
        for h in range(2):
            y = (lax.axis_index("y") + 4 - i) & 3
            c = lax.axis_index("c")
            at = 32 * ((2 * y + (1 - c if h else c)) & 3)
            tile = ref[8 * h : 8 * h + 8, :]
            low = pltpu.roll(jnp.where((lane >= 64) & (lane < 96), tile, 0.0), (at + 64) & 127, 1)
            high = pltpu.roll(jnp.where(lane >= 96, tile, 0.0), (at + 32) & 127, 1)
            parts.append((y >> 1, low, high))
    others = []
    for half in range(2):
        rows = jnp.zeros((8, BLK), F32)
        last = jnp.zeros((8, BLK), F32)
        for which, low, high in parts:
            rows = rows + jnp.where(which == half, low, 0.0)
            last = last + jnp.where(which == half, high, 0.0)
        rows = jnp.concatenate([rows, last[0:1, :], jnp.zeros((7, BLK), F32)], axis=0)
        cols = slice(half * BLK, (half + 1) * BLK)
        turned = other_side(rows, [centers[a : a + 1, cols] for a in range(3)])
        others.append(turned.astype(BF16))
        for a, point in enumerate(spread(turned)):
            there[half, a] = point
    own_sides(own, sides)

    def step(i, carry):
        for u in range(2):
            k = 2 * i + u
            here = [own[pl.ds(a * NB + k, 1), :] for a in range(3)]
            parts = [
                pull(others[h], [there[h, a] for a in range(3)], sides[k], here, FAR_CORE, cells[k] - h * BLK)
                for h in range(2)
            ]
            for a in range(3):
                acc[k, a] = parts[0][a] + parts[1][a]
        return carry

    lax.fori_loop(0, NB // 2, step, 0)
    write_forces(acc, forces, so_far)


def near_kernel(rec_z, tasks, own, so_far, mobility, forces, tops, sides, acc):
    acc[...] = jnp.zeros_like(acc)
    own_sides(own, sides)
    run_tasks(tasks, tasks[COUNT], rec_z, CAP, own, sides, acc)
    write_forces(acc, forces, so_far)
    v = mobility[...] * forces[...]
    speed = jnp.sum(v * v, axis=0, keepdims=True)
    tops[...] = jnp.broadcast_to(jnp.max(speed, axis=1, keepdims=True), tops.shape)


def step_kernel(tops, forces, mobility, out):
    best = jnp.max(jnp.max(tops[...], axis=0, keepdims=True), axis=1, keepdims=True)
    scale = STEP_LIMIT / (jnp.sqrt(best) + 1e-06)
    out[...] = scale * (mobility[...] * forces[...])


def shape(*dims, kind=F32):
    return jax.ShapeDtypeStruct(dims, kind)


def cost(flops):
    return pl.CostEstimate(flops=flops, bytes_accessed=1, transcendentals=0)


def body(segments, pair_blocks, block_cells, mobility, cell_centers):
    small = pltpu.CompilerParams(vmem_limit_bytes=6 * 1024 * 1024)
    seg_count = segments.shape[1]
    devices = 8 * NG * NX
    mob = mobility[None, :]
    packed, own, cells = pl.pallas_call(
        pack_kernel,
        out_shape=(shape(NX * ROWS, BLK), shape(ROWS, BLK), shape(NB, kind=jnp.int32)),
        in_specs=[VMEM, SMEM, VMEM],
        out_specs=(VMEM, VMEM, SMEM),
        name="pack",
    )(segments, block_cells, pair_blocks.T)
    rec_x = lax.all_to_all(packed.reshape(NX, ROWS, BLK), "x", 0, 0, tiled=True).reshape(NX * ROWS, BLK)
    sides = pltpu.VMEM((NB, BLK, BLK), BF16)
    sums = pltpu.VMEM((NB, 3, 8, BLK), F32)
    same = pl.pallas_call(
        own_kernel,
        out_shape=shape(3, seg_count),
        in_specs=[VMEM],
        out_specs=VMEM,
        scratch_shapes=[sums],
        compiler_params=small,
        cost_estimate=cost(10**9),
        name="own",
    )(own)
    rec_x, same = lax.optimization_barrier((rec_x, same))
    row = pl.pallas_call(
        row_kernel,
        out_shape=shape(NZ * 8, BLK),
        grid=(1,),
        in_specs=[pl.BlockSpec((8, BLK), lambda i, s=s: ((s * ROWS + EXTRA) // 8, 0)) for s in range(NX)],
        out_specs=pl.BlockSpec((NZ * 8, BLK), lambda i: (0, 0)),
        compiler_params=small,
        name="row",
    )(*([rec_x] * NX))
    rec_t = lax.all_to_all(row.reshape(NZ, 8, BLK), "z", 0, 0, tiled=True)
    group = jnp.sum(rec_t, axis=0)
    rec_t = rec_t.reshape(NZ * 8, BLK)

    def lists(rows):
        return [
            pltpu.VMEM((rows, BLK), jnp.int32),
            pltpu.SMEM((rows, BLK), jnp.int32),
            pltpu.SMEM((NZ,), jnp.int32),
            pltpu.SemaphoreType.DMA,
        ]

    def to_send(number):
        return pl.pallas_call(
            send_kernel,
            out_shape=(shape(NZ * SECT, BLK), shape(1, kind=jnp.int32), shape(TASKS + 128, kind=jnp.int32)),
            in_specs=[SMEM, VMEM, VMEM],
            out_specs=(VMEM, SMEM, SMEM),
            scratch_shapes=lists(8),
            compiler_params=small,
            name="send",
        )(number, rec_t, rec_x)

    def to_do(number):
        return pl.pallas_call(
            tasks_kernel,
            out_shape=shape(TASKS + 128, kind=jnp.int32),
            in_specs=[SMEM, VMEM],
            out_specs=SMEM,
            scratch_shapes=lists(16) + [pltpu.SMEM((TASKS + 128,), jnp.int32)],
            compiler_params=small,
            cost_estimate=cost(1),
            name="tasks",
        )(number, rec_t)

    def add_near(rec_z, tasks, so_far):
        return pl.pallas_call(
            near_kernel,
            out_shape=(shape(3, seg_count), shape(devices, BLK)),
            in_specs=[VMEM, SMEM, VMEM, VMEM, VMEM],
            out_specs=(VMEM, VMEM),
            scratch_shapes=[sides, sums],
            compiler_params=small,
            name="near",
        )(rec_z, tasks, own, so_far, mob)

    def more(carry):
        left, so_far = carry
        number = left - 1
        send = to_send(number)[0].reshape(NZ, SECT, BLK)
        late = to_do(number)
        z = lax.axis_index("z")
        got = jnp.zeros_like(send)
        for k in range(1, NZ):
            part = lax.dynamic_index_in_dim(send, (z + k) % NZ, 0, keepdims=True)
            part = lax.ppermute(part, "z", [(i, (i + k) % NZ) for i in range(NZ)])
            got = lax.dynamic_update_slice_in_dim(got, part, (z + NZ - k) % NZ, 0)
        return number, add_near(got.reshape(NZ * SECT, BLK), late, so_far)[0]

    def beside(carry):
        turn, so_far, _, moments = carry
        groups = [moments] + [lax.ppermute(moments, "y", [(i, (i + k) % 4) for i in range(4)]) for k in range(1, 4)]
        some, rounds, tasks = pl.pallas_call(
            row_pairs_kernel,
            out_shape=(shape(3, seg_count), shape(1, kind=jnp.int32), shape(TASKS + 128, kind=jnp.int32)),
            in_specs=[VMEM] * 4,
            out_specs=(VMEM, SMEM, SMEM),
            scratch_shapes=[sides, sums] + lists(16) + [pltpu.SMEM((TASKS + 128,), jnp.int32)],
            compiler_params=small,
            cost_estimate=cost(4 * 10**9),
            name="row_pairs",
        )(own, rec_t, rec_x, so_far)
        home = pl.pallas_call(
            far_kernel,
            out_shape=shape(3, seg_count),
            in_specs=[VMEM] * 5 + [SMEM, VMEM, VMEM],
            out_specs=VMEM,
            scratch_shapes=[pltpu.VMEM((2, 3, BLK, BLK), F32), sides, sums],
            compiler_params=small,
            cost_estimate=cost(1),
            name="far",
        )(own, *groups, cells, cell_centers, some)
        _, home = lax.while_loop(lambda c: c[0][0] > 1, more, (rounds, home))
        return turn + 1, home, tasks, groups[1]

    both = jnp.concatenate([group, lax.ppermute(group, "c", [(0, 1), (1, 0)])], axis=0)
    first = jnp.zeros((1,), jnp.int32)
    send, start, no_tasks = to_send(first)
    rec_z = lax.all_to_all(send.reshape(NZ, SECT, BLK), "z", 0, 0, tiled=True)
    _, home, tasks, _ = lax.while_loop(lambda c: c[0][0] < 1, beside, (start, same, no_tasks, both))
    forces, tops = add_near(rec_z.reshape(NZ * SECT, BLK), tasks, home)
    tops = lax.all_to_all(tops.reshape(devices, 1, BLK), ("y", "c", "z", "x"), 0, 0, tiled=True)
    displacement = pl.pallas_call(
        step_kernel,
        out_shape=shape(3, seg_count),
        in_specs=[VMEM, VMEM, VMEM],
        out_specs=VMEM,
        compiler_params=small,
        name="step",
    )(tops.reshape(devices, BLK), forces, mob)
    return forces, displacement


def solution(mesh):
    names = ("y", "c", "z", "x")
    fine = Mesh(mesh.devices.reshape(NG // 2, 2, NZ, NX), names)
    in_specs = (P(None, names), P(names, None), P(names), P(names), P())
    out_specs = (P(None, names), P(None, names))
    return jax.shard_map(body, mesh=fine, in_specs=in_specs, out_specs=out_specs, check_vma=False)
```

```python
import jax
import jax.numpy as jnp
from jax import lax
from jax.experimental import pallas as pl
from jax.experimental.pallas import tpu as pltpu
from jax.sharding import Mesh
from jax.sharding import PartitionSpec as P

NEAR_CORE = 0.25
FAR_CORE = 1.0
STEP_LIMIT = 0.5
BLK = 128
NB = 16
NZ = 8
NX = 4
NG = 8
EXTRA = 9 * NB
ROWS = EXTRA + 8
CAP = 14
SECT = 9 * CAP + 2
TASKS = 2048
COUNT = TASKS + 64
PAD = 1 << 16
F32 = jnp.float32
BF16 = jnp.bfloat16
VMEM = pl.BlockSpec(memory_space=pltpu.VMEM)
SMEM = pl.BlockSpec(memory_space=pltpu.SMEM)
NT = (((1,), (1,)), ((), ()))


def lanes(rows):
    return lax.broadcasted_iota(jnp.int32, (rows, BLK), 1)


def subs(rows):
    return lax.broadcasted_iota(jnp.int32, (rows, BLK), 0)


def split(x):
    one = x.astype(BF16)
    rest = x - one.astype(F32)
    two = rest.astype(BF16)
    three = (rest - two.astype(F32)).astype(BF16)
    return one, two, three


def pack_kernel(seg, cells, pairs, packed, out, same_cells):
    for k in range(NB):
        cols = slice(k * BLK, (k + 1) * BLK)
        out[pl.ds(k, 8, stride=NB), :] = seg[0:8, cols]
        out[8 * NB + k : 8 * NB + k + 1, :] = seg[8:9, cols]
    row = subs(NB)
    cell = jnp.zeros((NB, BLK), jnp.int32)
    for k in range(NB):
        cell = jnp.where(row == k, cells[k] & 31, cell)
        same_cells[k] = cells[k]
    hot = (lanes(NB) == cell + 64).astype(F32)
    hot_last = (lanes(NB) == cell + 96).astype(F32)
    rows = []
    for q in range(3):
        for r in range(3):
            outer = out[(6 + q) * NB : (7 + q) * NB, :] * out[(3 + r) * NB : (4 + r) * NB, :]
            total = jnp.sum(outer, axis=1, keepdims=True)
            rows.append(jnp.sum(total * (hot_last if q + r == 4 else hot), axis=0, keepdims=True))
    out[EXTRA : EXTRA + 1, :] = rows[0] + rows[8]
    for r in range(1, 8):
        out[EXTRA + r : EXTRA + r + 1, :] = rows[r]
    out[EXTRA : EXTRA + 2, 0:32] = pairs[...].astype(F32)
    whole = out[...]
    for copy in range(NX):
        packed[copy * ROWS : (copy + 1) * ROWS, :] = whole


def row_kernel(*refs):
    out = refs[NX]
    lane = lanes(8)
    rest = [jnp.zeros((8 - NX, BLK), F32)]
    first = jnp.concatenate([ref[0:1, :] for ref in refs[:NX]] + rest, axis=0)
    second = jnp.concatenate([ref[1:2, :] for ref in refs[:NX]] + rest, axis=0)
    total = refs[0][...]
    for ref in refs[1:NX]:
        total = total + ref[...]
    tile = jnp.where(lane < 32, first, jnp.where(lane < 64, pltpu.roll(second, 32, 1), total))
    for copy in range(NZ):
        out[8 * copy : 8 * copy + 8, :] = tile


def group_pairs(rec_t):
    lane = lanes(8)
    a = jnp.zeros((8, BLK), F32)
    b = jnp.zeros((8, BLK), F32)
    for x in range(NX):
        part = rec_t[pl.ds(x, NZ, stride=8), :]
        one = jnp.where(lane < 32, part, 0.0)
        two = jnp.where((lane >= 32) & (lane < 64), part, 0.0)
        a = a + (pltpu.roll(one, 32 * x, 1) if x else one)
        b = b + (pltpu.roll(two, (32 * x + 96) % 128, 1) if x != 1 else two)
    return a.astype(jnp.int32), b.astype(jnp.int32)


def list_hits(hit, code, lst, smem, sem):
    rows = hit.shape[0]
    hits = hit.astype(F32)
    hot = jnp.concatenate([hits, jnp.zeros((16 - rows, BLK), F32)], axis=0) if rows < 16 else hits
    hot = hot.astype(BF16)
    sq_row, sq_lane = subs(BLK), lanes(BLK)
    inside = jnp.dot(hot, (sq_row < sq_lane).astype(BF16), preferred_element_type=F32)
    totals = jnp.dot(hot, jnp.ones((BLK, BLK), BF16), preferred_element_type=F32)
    before = jnp.zeros((16, BLK), F32)
    running = jnp.zeros((1, BLK), F32)
    for s in range(rows):
        before = jnp.where(subs(16) == s, running, before)
        running = running + totals[s : s + 1, :]
    count = jnp.max(running).astype(jnp.int32)
    rank = jnp.where(hits > 0.0, (inside + before)[0:rows, :], -1.0)
    code = code.astype(F32)

    def listing(chunk, carry):
        slot = (sq_row + chunk * BLK).astype(F32)
        found = jnp.zeros((BLK, BLK), F32)
        for c in range(rows):
            found = found + jnp.where(rank[c : c + 1, :] == slot, code[c : c + 1, :], 0.0)
        lst[pl.ds(chunk, 1), :] = jnp.sum(found.T, axis=0, keepdims=True).astype(jnp.int32)
        return carry

    listing(0, 0)
    lax.fori_loop(1, (count + BLK - 1) // BLK, listing, 0)
    copy = pltpu.make_async_copy(lst, smem, sem)
    copy.start()
    return copy, count


def send_kernel(turn_no, rec_t, rec_x, send, start, none, lst, smem, cnt, sem):
    start[0] = 0
    none[COUNT] = 0
    zz = lax.axis_index("z")
    xx = lax.axis_index("x")
    rnd = turn_no[0]
    ai, bi = group_pairs(rec_t)
    za, zb = ai >> 6, bi >> 6
    to_a = (za != zz) & (((ai >> 4) & 3) == xx) & (zb == zz)
    to_b = (zb != zz) & (((bi >> 4) & 3) == xx) & (za == zz)
    code = jnp.where(to_a, za * 512 + bi, zb * 512 + ai)
    copy, count = list_hits((to_a & (ai >= 0)) | (to_b & (bi >= 0)), code, lst, smem, sem)
    send[...] = jnp.zeros_like(send)
    for z in range(NZ):
        cnt[z] = 0
    copy.wait()

    def deliver(i, carry):
        entry = smem[i >> 7, i & 127]
        f = entry & 511
        z = entry >> 9
        slot = cnt[z] - rnd * CAP
        cnt[z] = cnt[z] + 1

        @pl.when((slot >= 0) & (slot < CAP))
        def _():
            source = ((f >> 4) & 3) * ROWS + (f & 15)
            target = z * SECT + slot
            send[pl.ds(target, 8, stride=CAP), :] = rec_x[pl.ds(source, 8, stride=NB), :]
            send[pl.ds(target + 8 * CAP, 1), :] = rec_x[pl.ds(source + 8 * NB, 1), :]

        return carry

    lax.fori_loop(0, count, deliver, 0)


def rounds_needed(ai, bi):
    own_a, own_b = ai >> 4, bi >> 4
    owner, column = [], []
    for here, there in ((own_a, own_b), (own_b, own_a)):
        for i in range(8):
            owner.append((subs(32) == here[i : i + 1, :]).astype(BF16))
            column.append((subs(16) == (there[i : i + 1, :] >> 2)).astype(BF16))
    owner, column = jnp.concatenate(owner, axis=1), jnp.concatenate(column, axis=1)
    need = lax.dot_general(owner, column, NT, preferred_element_type=F32)
    r32 = lax.broadcasted_iota(jnp.int32, (32, 16), 0)
    c32 = lax.broadcasted_iota(jnp.int32, (32, 16), 1)
    longest = jnp.max(jnp.where((r32 >> 2) == c32, 0.0, need)).astype(jnp.int32)
    return (longest + CAP - 1) // CAP


def list_tasks(rec_t, lst, smem, sem):
    me = lax.axis_index("z") * NX + lax.axis_index("x")
    ai, bi = group_pairs(rec_t)
    fa, fb = (ai >> 4) == me, (bi >> 4) == me
    swapped = (bi & 15) * 512 + ai
    hits = jnp.concatenate([(fa | fb).astype(F32), (fa & fb).astype(F32)], axis=0)
    code = jnp.concatenate([jnp.where(fa, (ai & 15) * 512 + bi, swapped), swapped], axis=0)
    return list_hits(hits > 0.0, code, lst, smem, sem)


def place_tasks(rnd, count, local, tasks, smem, cnt):
    zz = lax.axis_index("z")
    for z in range(NZ):
        cnt[z] = 0

    def receive(i, carry):
        at_local, at = carry
        entry = smem[i >> 7, i & 127]
        f = entry & 511
        k = (entry >> 9) << 12
        z = f >> 6
        here = z == zz
        slot = cnt[z] - rnd * CAP
        cnt[z] = cnt[z] + 1
        local[at_local] = (((f >> 4) & 3) * ROWS + (f & 15)) | k
        tasks[at] = (z * SECT + slot) | k
        use = jnp.logical_not(here) & (slot >= 0) & (slot < CAP)
        return at_local + here.astype(jnp.int32), at + use.astype(jnp.int32)

    used_local, used = lax.fori_loop(0, count, receive, (0, 0))
    for u in range(8):
        local[used_local + u] = PAD
        tasks[used + u] = PAD
    tasks[COUNT] = used
    return used_local


def run_tasks(listed, count, unroll, blocks, apart, own, sides, acc):
    columns = point_columns()

    def step(i, carry):
        for u in range(unroll):
            entry = listed[unroll * i + u]
            base = entry & 4095
            k = (entry >> 12) & 15

            def row(r):
                return blocks[pl.ds(base + r * apart, 1), :]

            here = [own[pl.ds(a * NB + k, 1), :] for a in range(3)]
            near = source_pull(row, jnp.where(entry >= PAD, 0, 9), sides[k], here, columns)
            for a in range(3):
                acc[k, a] = acc[k, a] + near[a]
        return carry

    lax.fori_loop(0, (count + unroll - 1) // unroll, step, 0)


def tasks_kernel(turn_no, rec_t, tasks, lst, smem, cnt, sem, local):
    copy, count = list_tasks(rec_t, lst, smem, sem)
    copy.wait()
    place_tasks(turn_no[0], count, local, tasks, smem, cnt)


def outer_rows(row, symmetric):
    s = subs(16)
    t = [jnp.broadcast_to(row(3 + r), (16, BLK)) for r in range(3)]
    b = [jnp.broadcast_to(row(6 + q), (16, BLK)) for q in range(3)]

    def slow(v):
        return jnp.where(s < 3, v[0], jnp.where(s < 6, v[1], v[2]))

    def fast(v):
        first = (s == 0) | (s == 3) | (s == 6)
        return jnp.where(first, v[0], jnp.where((s == 1) | (s == 4) | (s == 7), v[1], v[2]))

    o = slow(b) * fast(t)
    return o + 0.5 * (fast(b) * slow(t)) if symmetric else o


def other_side(rows, points):
    one, two, three = [x.astype(F32) for x in split(rows)]
    points = jnp.concatenate(points + [jnp.zeros((29, BLK), F32)], axis=0)
    return jnp.concatenate([one, two, one, three, two, one, points], axis=0).T


def own_side(row):
    o = jnp.where(subs(16) < 9, outer_rows(row, False), 0.0)
    one, two, three = split(o)
    return jnp.concatenate([one, one, two, one, two, three, jnp.zeros((32, BLK), BF16)], axis=0)


def own_sides(own, sides):
    for k in range(NB):
        sides[k] = own_side(lambda r: own[r * NB + k : r * NB + k + 1, :])


def spread(turned):
    return [jnp.broadcast_to(turned[:, 96 + a : 97 + a], (BLK, BLK)) for a in range(3)]


def fold(v):
    total = v[0:8, :]
    for i in range(1, BLK // 8):
        total = total + v[8 * i : 8 * i + 8, :]
    return total


def pull(other, there, mine, here, core, drop=None):
    c = jnp.dot(other, mine, preferred_element_type=F32)
    if drop is not None:
        c = jnp.where(subs(BLK) == drop, 0.0, c)
    d = [here[a] - there[a] for a in range(3)]
    inv = lax.rsqrt(d[0] * d[0] + d[1] * d[1] + (d[2] * d[2] + core))
    w = c * (inv * inv * inv)
    return [fold(w * d[a]) for a in range(3)]


def point_columns():
    row = lax.broadcasted_iota(jnp.int32, (BLK, 3 * BLK), 0) - 96
    axis = lax.broadcasted_iota(jnp.int32, (BLK, 3 * BLK), 1) // BLK
    return ((row == axis) | (row == axis + 3) | (row == axis + 6)).astype(BF16)


def source_pull(row, limit, mine, here, columns):
    rows = jnp.where(subs(16) < limit, outer_rows(row, True), 0.0)
    one, two, three = split(rows)
    s = subs(16)
    p = [row(a) for a in range(3)]
    points = jnp.concatenate(p + p + p + [jnp.zeros((7, BLK), F32)], axis=0)
    p1, p2, p3 = [x.astype(F32) for x in split(points)]
    pieces = jnp.where(s < 3, p1, jnp.where(s < 6, p2, p3)).astype(BF16)
    side = jnp.concatenate([one, two, one, three, two, one, pieces, jnp.zeros((16, BLK), BF16)], axis=0).T
    spots = jnp.dot(side, columns, preferred_element_type=F32)
    there = [spots[:, a * BLK : (a + 1) * BLK] for a in range(3)]
    return pull(side, there, mine, here, NEAR_CORE)


def write_forces(acc, forces, so_far=None):
    for k in range(NB):
        cols = slice(k * BLK, (k + 1) * BLK)
        rows = jnp.concatenate([jnp.sum(acc[k, a], axis=0, keepdims=True) for a in range(3)], axis=0)
        forces[:, cols] = rows if so_far is None else so_far[:, cols] + rows


def own_kernel(own, forces, acc):
    columns = point_columns()

    def step(i, carry):
        for u in range(4):
            k = 4 * i + u

            def row(r):
                return own[pl.ds(r * NB + k, 1), :]

            same = source_pull(row, 9, own_side(row), [row(a) for a in range(3)], columns)
            for a in range(3):
                acc[k, a] = same[a]
        return carry

    lax.fori_loop(0, NB // 4, step, 0)
    write_forces(acc, forces)


def row_pairs_kernel(own, rec_t, rec_x, so_far, forces, rounds, tasks, sides, acc, lst, smem, cnt, sem, local):
    copy, count = list_tasks(rec_t, lst, smem, sem)
    rounds[0] = rounds_needed(*group_pairs(rec_t))
    own_sides(own, sides)
    acc[...] = jnp.zeros_like(acc)
    copy.wait()
    used = place_tasks(0, count, local, tasks, smem, cnt)
    run_tasks(local, used, 4, rec_x, NB, own, sides, acc)
    write_forces(acc, forces, so_far)


def far_kernel(own, m0, m1, m2, m3, cells, centers, so_far, forces, there, sides, acc):
    lane = lanes(8)
    parts = []
    for i, ref in enumerate((m0, m1, m2, m3)):
        for h in range(2):
            y = (lax.axis_index("y") + 4 - i) & 3
            c = lax.axis_index("c")
            at = 32 * ((2 * y + (1 - c if h else c)) & 3)
            tile = ref[8 * h : 8 * h + 8, :]
            low = pltpu.roll(jnp.where((lane >= 64) & (lane < 96), tile, 0.0), (at + 64) & 127, 1)
            high = pltpu.roll(jnp.where(lane >= 96, tile, 0.0), (at + 32) & 127, 1)
            parts.append((y >> 1, low, high))
    others = []
    for half in range(2):
        rows = jnp.zeros((8, BLK), F32)
        last = jnp.zeros((8, BLK), F32)
        for which, low, high in parts:
            rows = rows + jnp.where(which == half, low, 0.0)
            last = last + jnp.where(which == half, high, 0.0)
        rows = jnp.concatenate([rows, last[0:1, :], jnp.zeros((7, BLK), F32)], axis=0)
        cols = slice(half * BLK, (half + 1) * BLK)
        turned = other_side(rows, [centers[a : a + 1, cols] for a in range(3)])
        others.append(turned.astype(BF16))
        for a, point in enumerate(spread(turned)):
            there[half, a] = point
    own_sides(own, sides)

    def step(i, carry):
        for u in range(2):
            k = 2 * i + u
            here = [own[pl.ds(a * NB + k, 1), :] for a in range(3)]
            parts = [
                pull(others[h], [there[h, a] for a in range(3)], sides[k], here, FAR_CORE, cells[k] - h * BLK)
                for h in range(2)
            ]
            for a in range(3):
                acc[k, a] = parts[0][a] + parts[1][a]
        return carry

    lax.fori_loop(0, NB // 2, step, 0)
    write_forces(acc, forces, so_far)


def near_kernel(rec_z, tasks, own, so_far, mobility, forces, tops, sides, acc):
    acc[...] = jnp.zeros_like(acc)
    own_sides(own, sides)
    run_tasks(tasks, tasks[COUNT], 8, rec_z, CAP, own, sides, acc)
    write_forces(acc, forces, so_far)
    v = mobility[...] * forces[...]
    speed = jnp.sum(v * v, axis=0, keepdims=True)
    tops[...] = jnp.broadcast_to(jnp.max(speed, axis=1, keepdims=True), tops.shape)


def step_kernel(tops, forces, mobility, out):
    best = jnp.max(jnp.max(tops[...], axis=0, keepdims=True), axis=1, keepdims=True)
    scale = STEP_LIMIT / (jnp.sqrt(best) + 1e-06)
    out[...] = scale * (mobility[...] * forces[...])


def shape(*dims, kind=F32):
    return jax.ShapeDtypeStruct(dims, kind)


def cost(flops):
    return pl.CostEstimate(flops=flops, bytes_accessed=1, transcendentals=0)


def body(segments, pair_blocks, block_cells, mobility, cell_centers):
    small = pltpu.CompilerParams(vmem_limit_bytes=6 * 1024 * 1024)
    seg_count = segments.shape[1]
    devices = 8 * NG * NX
    mob = mobility[None, :]
    packed, own, cells = pl.pallas_call(
        pack_kernel,
        out_shape=(shape(NX * ROWS, BLK), shape(ROWS, BLK), shape(NB, kind=jnp.int32)),
        in_specs=[VMEM, SMEM, VMEM],
        out_specs=(VMEM, VMEM, SMEM),
        name="pack",
    )(segments, block_cells, pair_blocks.T)
    rec_x = lax.all_to_all(packed.reshape(NX, ROWS, BLK), "x", 0, 0, tiled=True).reshape(NX * ROWS, BLK)
    sides = pltpu.VMEM((NB, BLK, BLK), BF16)
    sums = pltpu.VMEM((NB, 3, 8, BLK), F32)
    same = pl.pallas_call(
        own_kernel,
        out_shape=shape(3, seg_count),
        in_specs=[VMEM],
        out_specs=VMEM,
        scratch_shapes=[sums],
        compiler_params=small,
        cost_estimate=cost(10**9),
        name="own",
    )(own)
    rec_x, same = lax.optimization_barrier((rec_x, same))
    row = pl.pallas_call(
        row_kernel,
        out_shape=shape(NZ * 8, BLK),
        grid=(1,),
        in_specs=[pl.BlockSpec((8, BLK), lambda i, s=s: ((s * ROWS + EXTRA) // 8, 0)) for s in range(NX)],
        out_specs=pl.BlockSpec((NZ * 8, BLK), lambda i: (0, 0)),
        compiler_params=small,
        name="row",
    )(*([rec_x] * NX))
    rec_t = lax.all_to_all(row.reshape(NZ, 8, BLK), "z", 0, 0, tiled=True)
    group = jnp.sum(rec_t, axis=0)
    rec_t = rec_t.reshape(NZ * 8, BLK)

    def lists(rows):
        return [
            pltpu.VMEM((rows, BLK), jnp.int32),
            pltpu.SMEM((rows, BLK), jnp.int32),
            pltpu.SMEM((NZ,), jnp.int32),
            pltpu.SemaphoreType.DMA,
        ]

    def to_send(number):
        return pl.pallas_call(
            send_kernel,
            out_shape=(shape(NZ * SECT, BLK), shape(1, kind=jnp.int32), shape(TASKS + 128, kind=jnp.int32)),
            in_specs=[SMEM, VMEM, VMEM],
            out_specs=(VMEM, SMEM, SMEM),
            scratch_shapes=lists(8),
            compiler_params=small,
            name="send",
        )(number, rec_t, rec_x)

    def to_do(number):
        return pl.pallas_call(
            tasks_kernel,
            out_shape=shape(TASKS + 128, kind=jnp.int32),
            in_specs=[SMEM, VMEM],
            out_specs=SMEM,
            scratch_shapes=lists(16) + [pltpu.SMEM((TASKS + 128,), jnp.int32)],
            compiler_params=small,
            cost_estimate=cost(1),
            name="tasks",
        )(number, rec_t)

    def add_near(rec_z, tasks, so_far):
        return pl.pallas_call(
            near_kernel,
            out_shape=(shape(3, seg_count), shape(devices, BLK)),
            in_specs=[VMEM, SMEM, VMEM, VMEM, VMEM],
            out_specs=(VMEM, VMEM),
            scratch_shapes=[sides, sums],
            compiler_params=small,
            name="near",
        )(rec_z, tasks, own, so_far, mob)

    def more(carry):
        left, so_far = carry
        number = left - 1
        send = to_send(number)[0].reshape(NZ, SECT, BLK)
        late = to_do(number)
        z = lax.axis_index("z")
        got = jnp.zeros_like(send)
        for k in range(1, NZ):
            part = lax.dynamic_index_in_dim(send, (z + k) % NZ, 0, keepdims=True)
            part = lax.ppermute(part, "z", [(i, (i + k) % NZ) for i in range(NZ)])
            got = lax.dynamic_update_slice_in_dim(got, part, (z + NZ - k) % NZ, 0)
        return number, add_near(got.reshape(NZ * SECT, BLK), late, so_far)[0]

    def beside(carry):
        turn, so_far, _, moments = carry
        groups = [moments] + [lax.ppermute(moments, "y", [(i, (i + k) % 4) for i in range(4)]) for k in range(1, 4)]
        some, rounds, tasks = pl.pallas_call(
            row_pairs_kernel,
            out_shape=(shape(3, seg_count), shape(1, kind=jnp.int32), shape(TASKS + 128, kind=jnp.int32)),
            in_specs=[VMEM] * 4,
            out_specs=(VMEM, SMEM, SMEM),
            scratch_shapes=[sides, sums] + lists(16) + [pltpu.SMEM((TASKS + 128,), jnp.int32)],
            compiler_params=small,
            cost_estimate=cost(4 * 10**9),
            name="row_pairs",
        )(own, rec_t, rec_x, so_far)
        home = pl.pallas_call(
            far_kernel,
            out_shape=shape(3, seg_count),
            in_specs=[VMEM] * 5 + [SMEM, VMEM, VMEM],
            out_specs=VMEM,
            scratch_shapes=[pltpu.VMEM((2, 3, BLK, BLK), F32), sides, sums],
            compiler_params=small,
            cost_estimate=cost(1),
            name="far",
        )(own, *groups, cells, cell_centers, some)
        _, home = lax.while_loop(lambda c: c[0][0] > 1, more, (rounds, home))
        return turn + 1, home, tasks, groups[1]

    both = jnp.concatenate([group, lax.ppermute(group, "c", [(0, 1), (1, 0)])], axis=0)
    first = jnp.zeros((1,), jnp.int32)
    send, start, no_tasks = to_send(first)
    rec_z = lax.all_to_all(send.reshape(NZ, SECT, BLK), "z", 0, 0, tiled=True)
    _, home, tasks, _ = lax.while_loop(lambda c: c[0][0] < 1, beside, (start, same, no_tasks, both))
    forces, tops = add_near(rec_z.reshape(NZ * SECT, BLK), tasks, home)
    tops = lax.all_to_all(tops.reshape(devices, 1, BLK), ("y", "c", "z", "x"), 0, 0, tiled=True)
    displacement = pl.pallas_call(
        step_kernel,
        out_shape=shape(3, seg_count),
        in_specs=[VMEM, VMEM, VMEM],
        out_specs=VMEM,
        compiler_params=small,
        name="step",
    )(tops.reshape(devices, BLK), forces, mob)
    return forces, displacement


def solution(mesh):
    names = ("y", "c", "z", "x")
    fine = Mesh(mesh.devices.reshape(NG // 2, 2, NZ, NX), names)
    in_specs = (P(None, names), P(names, None), P(names), P(names), P())
    out_specs = (P(None, names), P(None, names))
    return jax.shard_map(body, mesh=fine, in_specs=in_specs, out_specs=out_specs, check_vma=False)
```

```python
import jax
import jax.numpy as jnp
from jax import lax
from jax.experimental import pallas as pl
from jax.experimental.pallas import tpu as pltpu
from jax.sharding import Mesh
from jax.sharding import PartitionSpec as P

NEAR_CORE = 0.25
FAR_CORE = 1.0
STEP_LIMIT = 0.5
BLK = 128
NB = 16
NZ = 8
NX = 4
NG = 8
EXTRA = 9 * NB
ROWS = EXTRA + 8
CAP = 14
SECT = 9 * CAP + 2
TASKS = 2048
COUNT = TASKS + 64
PAD = 1 << 16
F32 = jnp.float32
BF16 = jnp.bfloat16
VMEM = pl.BlockSpec(memory_space=pltpu.VMEM)
SMEM = pl.BlockSpec(memory_space=pltpu.SMEM)
NT = (((1,), (1,)), ((), ()))


def lanes(rows):
    return lax.broadcasted_iota(jnp.int32, (rows, BLK), 1)


def subs(rows):
    return lax.broadcasted_iota(jnp.int32, (rows, BLK), 0)


def split(x):
    one = x.astype(BF16)
    rest = x - one.astype(F32)
    two = rest.astype(BF16)
    three = (rest - two.astype(F32)).astype(BF16)
    return one, two, three


def pack_kernel(seg, cells, pairs, packed, out, same_cells):
    for k in range(NB):
        cols = slice(k * BLK, (k + 1) * BLK)
        out[pl.ds(k, 8, stride=NB), :] = seg[0:8, cols]
        out[8 * NB + k : 8 * NB + k + 1, :] = seg[8:9, cols]
    row = subs(NB)
    cell = jnp.zeros((NB, BLK), jnp.int32)
    for k in range(NB):
        cell = jnp.where(row == k, cells[k] & 31, cell)
        same_cells[k] = cells[k]
    hot = (lanes(NB) == cell + 64).astype(F32)
    hot_last = (lanes(NB) == cell + 96).astype(F32)
    rows = []
    for q in range(3):
        for r in range(3):
            outer = out[(6 + q) * NB : (7 + q) * NB, :] * out[(3 + r) * NB : (4 + r) * NB, :]
            total = jnp.sum(outer, axis=1, keepdims=True)
            rows.append(jnp.sum(total * (hot_last if q + r == 4 else hot), axis=0, keepdims=True))
    out[EXTRA : EXTRA + 1, :] = rows[0] + rows[8]
    for r in range(1, 8):
        out[EXTRA + r : EXTRA + r + 1, :] = rows[r]
    out[EXTRA : EXTRA + 2, 0:32] = pairs[...].astype(F32)
    whole = out[...]
    for copy in range(NX):
        packed[copy * ROWS : (copy + 1) * ROWS, :] = whole


def row_kernel(*refs):
    out = refs[NX]
    lane = lanes(8)
    rest = [jnp.zeros((8 - NX, BLK), F32)]
    first = jnp.concatenate([ref[0:1, :] for ref in refs[:NX]] + rest, axis=0)
    second = jnp.concatenate([ref[1:2, :] for ref in refs[:NX]] + rest, axis=0)
    total = refs[0][...]
    for ref in refs[1:NX]:
        total = total + ref[...]
    tile = jnp.where(lane < 32, first, jnp.where(lane < 64, pltpu.roll(second, 32, 1), total))
    for copy in range(NZ):
        out[8 * copy : 8 * copy + 8, :] = tile


def group_pairs(rec_t):
    lane = lanes(8)
    a = jnp.zeros((8, BLK), F32)
    b = jnp.zeros((8, BLK), F32)
    for x in range(NX):
        part = rec_t[pl.ds(x, NZ, stride=8), :]
        one = jnp.where(lane < 32, part, 0.0)
        two = jnp.where((lane >= 32) & (lane < 64), part, 0.0)
        a = a + (pltpu.roll(one, 32 * x, 1) if x else one)
        b = b + (pltpu.roll(two, (32 * x + 96) % 128, 1) if x != 1 else two)
    return a.astype(jnp.int32), b.astype(jnp.int32)


def list_hits(hit, code, lst, smem, sem):
    rows = hit.shape[0]
    hits = hit.astype(F32)
    hot = jnp.concatenate([hits, jnp.zeros((16 - rows, BLK), F32)], axis=0) if rows < 16 else hits
    hot = hot.astype(BF16)
    sq_row, sq_lane = subs(BLK), lanes(BLK)
    inside = jnp.dot(hot, (sq_row < sq_lane).astype(BF16), preferred_element_type=F32)
    totals = jnp.dot(hot, jnp.ones((BLK, BLK), BF16), preferred_element_type=F32)
    before = jnp.zeros((16, BLK), F32)
    running = jnp.zeros((1, BLK), F32)
    for s in range(rows):
        before = jnp.where(subs(16) == s, running, before)
        running = running + totals[s : s + 1, :]
    count = jnp.max(running).astype(jnp.int32)
    rank = jnp.where(hits > 0.0, (inside + before)[0:rows, :], -1.0)
    code = code.astype(F32)

    def listing(chunk, carry):
        slot = (sq_row + chunk * BLK).astype(F32)
        found = jnp.zeros((BLK, BLK), F32)
        for c in range(rows):
            found = found + jnp.where(rank[c : c + 1, :] == slot, code[c : c + 1, :], 0.0)
        lst[pl.ds(chunk, 1), :] = jnp.sum(found.T, axis=0, keepdims=True).astype(jnp.int32)
        return carry

    listing(0, 0)
    lax.fori_loop(1, (count + BLK - 1) // BLK, listing, 0)
    copy = pltpu.make_async_copy(lst, smem, sem)
    copy.start()
    return copy, count


def send_kernel(turn_no, rec_t, rec_x, send, start, none, lst, smem, cnt, sem):
    start[0] = 0
    none[COUNT] = 0
    zz = lax.axis_index("z")
    xx = lax.axis_index("x")
    rnd = turn_no[0]
    ai, bi = group_pairs(rec_t)
    za, zb = ai >> 6, bi >> 6
    to_a = (za != zz) & (((ai >> 4) & 3) == xx) & (zb == zz)
    to_b = (zb != zz) & (((bi >> 4) & 3) == xx) & (za == zz)
    code = jnp.where(to_a, za * 512 + bi, zb * 512 + ai)
    copy, count = list_hits((to_a & (ai >= 0)) | (to_b & (bi >= 0)), code, lst, smem, sem)
    send[...] = jnp.zeros_like(send)
    for z in range(NZ):
        cnt[z] = 0
    copy.wait()

    def deliver(i, carry):
        entry = smem[i >> 7, i & 127]
        f = entry & 511
        z = entry >> 9
        slot = cnt[z] - rnd * CAP
        cnt[z] = cnt[z] + 1

        @pl.when((slot >= 0) & (slot < CAP))
        def _():
            source = ((f >> 4) & 3) * ROWS + (f & 15)
            target = z * SECT + slot
            send[pl.ds(target, 8, stride=CAP), :] = rec_x[pl.ds(source, 8, stride=NB), :]
            send[pl.ds(target + 8 * CAP, 1), :] = rec_x[pl.ds(source + 8 * NB, 1), :]

        return carry

    lax.fori_loop(0, count, deliver, 0)


def rounds_needed(ai, bi):
    own_a, own_b = ai >> 4, bi >> 4
    owner, column = [], []
    for here, there in ((own_a, own_b), (own_b, own_a)):
        for i in range(8):
            owner.append((subs(32) == here[i : i + 1, :]).astype(BF16))
            column.append((subs(16) == (there[i : i + 1, :] >> 2)).astype(BF16))
    owner, column = jnp.concatenate(owner, axis=1), jnp.concatenate(column, axis=1)
    need = lax.dot_general(owner, column, NT, preferred_element_type=F32)
    r32 = lax.broadcasted_iota(jnp.int32, (32, 16), 0)
    c32 = lax.broadcasted_iota(jnp.int32, (32, 16), 1)
    longest = jnp.max(jnp.where((r32 >> 2) == c32, 0.0, need)).astype(jnp.int32)
    return (longest + CAP - 1) // CAP


def list_tasks(rec_t, lst, smem, sem):
    me = lax.axis_index("z") * NX + lax.axis_index("x")
    ai, bi = group_pairs(rec_t)
    fa, fb = (ai >> 4) == me, (bi >> 4) == me
    swapped = (bi & 15) * 512 + ai
    hits = jnp.concatenate([(fa | fb).astype(F32), (fa & fb).astype(F32)], axis=0)
    code = jnp.concatenate([jnp.where(fa, (ai & 15) * 512 + bi, swapped), swapped], axis=0)
    return list_hits(hits > 0.0, code, lst, smem, sem)


def place_tasks(rnd, count, local, tasks, smem, cnt):
    zz = lax.axis_index("z")
    for z in range(NZ):
        cnt[z] = 0

    def receive(i, carry):
        at_local, at = carry
        entry = smem[i >> 7, i & 127]
        f = entry & 511
        k = (entry >> 9) << 12
        z = f >> 6
        here = z == zz
        slot = cnt[z] - rnd * CAP
        cnt[z] = cnt[z] + 1
        local[at_local] = (((f >> 4) & 3) * ROWS + (f & 15)) | k
        tasks[at] = (z * SECT + slot) | k
        use = jnp.logical_not(here) & (slot >= 0) & (slot < CAP)
        return at_local + here.astype(jnp.int32), at + use.astype(jnp.int32)

    used_local, used = lax.fori_loop(0, count, receive, (0, 0))
    for u in range(8):
        local[used_local + u] = PAD
        tasks[used + u] = PAD
    tasks[COUNT] = used
    return used_local


def run_tasks(listed, count, unroll, blocks, apart, own, sides, acc):
    columns = point_columns()

    def step(i, carry):
        for u in range(unroll):
            entry = listed[unroll * i + u]
            base = entry & 4095
            k = (entry >> 12) & 15

            def row(r):
                return blocks[pl.ds(base + r * apart, 1), :]

            here = [own[pl.ds(a * NB + k, 1), :] for a in range(3)]
            near = source_pull(row, jnp.where(entry >= PAD, 0, 9), sides[k], here, columns)
            for a in range(3):
                acc[k, a] = acc[k, a] + near[a]
        return carry

    lax.fori_loop(0, (count + unroll - 1) // unroll, step, 0)


def tasks_kernel(turn_no, rec_t, tasks, lst, smem, cnt, sem, local):
    copy, count = list_tasks(rec_t, lst, smem, sem)
    copy.wait()
    place_tasks(turn_no[0], count, local, tasks, smem, cnt)


def outer_rows(row, symmetric):
    s = subs(16)
    t = [jnp.broadcast_to(row(3 + r), (16, BLK)) for r in range(3)]
    b = [jnp.broadcast_to(row(6 + q), (16, BLK)) for q in range(3)]

    def slow(v):
        return jnp.where(s < 3, v[0], jnp.where(s < 6, v[1], v[2]))

    def fast(v):
        first = (s == 0) | (s == 3) | (s == 6)
        return jnp.where(first, v[0], jnp.where((s == 1) | (s == 4) | (s == 7), v[1], v[2]))

    o = slow(b) * fast(t)
    return o + 0.5 * (fast(b) * slow(t)) if symmetric else o


def other_side(rows, points):
    one, two, three = [x.astype(F32) for x in split(rows)]
    points = jnp.concatenate(points + [jnp.zeros((29, BLK), F32)], axis=0)
    return jnp.concatenate([one, two, one, three, two, one, points], axis=0).T


def own_side(row):
    o = jnp.where(subs(16) < 9, outer_rows(row, False), 0.0)
    one, two, three = split(o)
    return jnp.concatenate([one, one, two, one, two, three, jnp.zeros((32, BLK), BF16)], axis=0)


def own_sides(own, sides):
    for k in range(NB):
        sides[k] = own_side(lambda r: own[r * NB + k : r * NB + k + 1, :])


def spread(turned):
    return [jnp.broadcast_to(turned[:, 96 + a : 97 + a], (BLK, BLK)) for a in range(3)]


def fold(v):
    total = v[0:8, :]
    for i in range(1, BLK // 8):
        total = total + v[8 * i : 8 * i + 8, :]
    return total


def pull(other, there, mine, here, core, drop=None):
    c = jnp.dot(other, mine, preferred_element_type=F32)
    if drop is not None:
        c = jnp.where(subs(BLK) == drop, 0.0, c)
    d = [here[a] - there[a] for a in range(3)]
    inv = lax.rsqrt(d[0] * d[0] + d[1] * d[1] + (d[2] * d[2] + core))
    w = c * (inv * inv * inv)
    return [fold(w * d[a]) for a in range(3)]


def point_columns():
    row = lax.broadcasted_iota(jnp.int32, (BLK, 3 * BLK), 0) - 96
    axis = lax.broadcasted_iota(jnp.int32, (BLK, 3 * BLK), 1) // BLK
    return ((row == axis) | (row == axis + 3) | (row == axis + 6)).astype(BF16)


def source_pull(row, limit, mine, here, columns):
    rows = jnp.where(subs(16) < limit, outer_rows(row, True), 0.0)
    one, two, three = split(rows)
    s = subs(16)
    p = [row(a) for a in range(3)]
    points = jnp.concatenate(p + p + p + [jnp.zeros((7, BLK), F32)], axis=0)
    p1, p2, p3 = [x.astype(F32) for x in split(points)]
    pieces = jnp.where(s < 3, p1, jnp.where(s < 6, p2, p3)).astype(BF16)
    side = jnp.concatenate([one, two, one, three, two, one, pieces, jnp.zeros((16, BLK), BF16)], axis=0).T
    spots = jnp.dot(side, columns, preferred_element_type=F32)
    there = [spots[:, a * BLK : (a + 1) * BLK] for a in range(3)]
    return pull(side, there, mine, here, NEAR_CORE)


def write_forces(acc, forces, so_far=None):
    for k in range(NB):
        cols = slice(k * BLK, (k + 1) * BLK)
        rows = jnp.concatenate([jnp.sum(acc[k, a], axis=0, keepdims=True) for a in range(3)], axis=0)
        forces[:, cols] = rows if so_far is None else so_far[:, cols] + rows


def own_kernel(own, forces, acc):
    columns = point_columns()

    def step(i, carry):
        for u in range(4):
            k = 4 * i + u

            def row(r):
                return own[pl.ds(r * NB + k, 1), :]

            same = source_pull(row, 9, own_side(row), [row(a) for a in range(3)], columns)
            for a in range(3):
                acc[k, a] = same[a]
        return carry

    lax.fori_loop(0, NB // 4, step, 0)
    write_forces(acc, forces)


def row_pairs_kernel(own, rec_t, rec_x, so_far, forces, rounds, tasks, sides, acc, lst, smem, cnt, sem, local):
    copy, count = list_tasks(rec_t, lst, smem, sem)
    rounds[0] = rounds_needed(*group_pairs(rec_t))
    own_sides(own, sides)
    acc[...] = jnp.zeros_like(acc)
    copy.wait()
    used = place_tasks(0, count, local, tasks, smem, cnt)
    run_tasks(local, used, 4, rec_x, NB, own, sides, acc)
    write_forces(acc, forces, so_far)


def far_kernel(own, m0, m1, m2, m3, cells, centers, so_far, forces, there, sides, acc):
    lane = lanes(8)
    parts = []
    for i, ref in enumerate((m0, m1, m2, m3)):
        for h in range(2):
            y = (lax.axis_index("y") + 4 - i) & 3
            c = lax.axis_index("c")
            at = 32 * ((2 * y + (1 - c if h else c)) & 3)
            tile = ref[8 * h : 8 * h + 8, :]
            low = pltpu.roll(jnp.where((lane >= 64) & (lane < 96), tile, 0.0), (at + 64) & 127, 1)
            high = pltpu.roll(jnp.where(lane >= 96, tile, 0.0), (at + 32) & 127, 1)
            parts.append((y >> 1, low, high))
    others = []
    for half in range(2):
        rows = jnp.zeros((8, BLK), F32)
        last = jnp.zeros((8, BLK), F32)
        for which, low, high in parts:
            rows = rows + jnp.where(which == half, low, 0.0)
            last = last + jnp.where(which == half, high, 0.0)
        rows = jnp.concatenate([rows, last[0:1, :], jnp.zeros((7, BLK), F32)], axis=0)
        cols = slice(half * BLK, (half + 1) * BLK)
        turned = other_side(rows, [centers[a : a + 1, cols] for a in range(3)])
        others.append(turned.astype(BF16))
        for a, point in enumerate(spread(turned)):
            there[half, a] = point
    own_sides(own, sides)

    def step(i, carry):
        for u in range(4):
            k = 4 * i + u
            here = [own[pl.ds(a * NB + k, 1), :] for a in range(3)]
            parts = [
                pull(others[h], [there[h, a] for a in range(3)], sides[k], here, FAR_CORE, cells[k] - h * BLK)
                for h in range(2)
            ]
            for a in range(3):
                acc[k, a] = parts[0][a] + parts[1][a]
        return carry

    lax.fori_loop(0, NB // 4, step, 0)
    write_forces(acc, forces, so_far)


def near_kernel(rec_z, tasks, own, so_far, mobility, forces, tops, sides, acc):
    acc[...] = jnp.zeros_like(acc)
    own_sides(own, sides)
    run_tasks(tasks, tasks[COUNT], 8, rec_z, CAP, own, sides, acc)
    write_forces(acc, forces, so_far)
    v = mobility[...] * forces[...]
    speed = jnp.sum(v * v, axis=0, keepdims=True)
    tops[...] = jnp.broadcast_to(jnp.max(speed, axis=1, keepdims=True), tops.shape)


def step_kernel(tops, forces, mobility, out):
    best = jnp.max(jnp.max(tops[...], axis=0, keepdims=True), axis=1, keepdims=True)
    scale = STEP_LIMIT / (jnp.sqrt(best) + 1e-06)
    out[...] = scale * (mobility[...] * forces[...])


def shape(*dims, kind=F32):
    return jax.ShapeDtypeStruct(dims, kind)


def cost(flops):
    return pl.CostEstimate(flops=flops, bytes_accessed=1, transcendentals=0)


def body(segments, pair_blocks, block_cells, mobility, cell_centers):
    small = pltpu.CompilerParams(vmem_limit_bytes=6 * 1024 * 1024)
    seg_count = segments.shape[1]
    devices = 8 * NG * NX
    mob = mobility[None, :]
    packed, own, cells = pl.pallas_call(
        pack_kernel,
        out_shape=(shape(NX * ROWS, BLK), shape(ROWS, BLK), shape(NB, kind=jnp.int32)),
        in_specs=[VMEM, SMEM, VMEM],
        out_specs=(VMEM, VMEM, SMEM),
        name="pack",
    )(segments, block_cells, pair_blocks.T)
    rec_x = lax.all_to_all(packed.reshape(NX, ROWS, BLK), "x", 0, 0, tiled=True).reshape(NX * ROWS, BLK)
    sides = pltpu.VMEM((NB, BLK, BLK), BF16)
    sums = pltpu.VMEM((NB, 3, 8, BLK), F32)
    same = pl.pallas_call(
        own_kernel,
        out_shape=shape(3, seg_count),
        in_specs=[VMEM],
        out_specs=VMEM,
        scratch_shapes=[sums],
        compiler_params=small,
        cost_estimate=cost(10**9),
        name="own",
    )(own)
    rec_x, same = lax.optimization_barrier((rec_x, same))
    row = pl.pallas_call(
        row_kernel,
        out_shape=shape(NZ * 8, BLK),
        grid=(1,),
        in_specs=[pl.BlockSpec((8, BLK), lambda i, s=s: ((s * ROWS + EXTRA) // 8, 0)) for s in range(NX)],
        out_specs=pl.BlockSpec((NZ * 8, BLK), lambda i: (0, 0)),
        compiler_params=small,
        name="row",
    )(*([rec_x] * NX))
    rec_t = lax.all_to_all(row.reshape(NZ, 8, BLK), "z", 0, 0, tiled=True)
    group = jnp.sum(rec_t, axis=0)
    rec_t = rec_t.reshape(NZ * 8, BLK)

    def lists(rows):
        return [
            pltpu.VMEM((rows, BLK), jnp.int32),
            pltpu.SMEM((rows, BLK), jnp.int32),
            pltpu.SMEM((NZ,), jnp.int32),
            pltpu.SemaphoreType.DMA,
        ]

    def to_send(number):
        return pl.pallas_call(
            send_kernel,
            out_shape=(shape(NZ * SECT, BLK), shape(1, kind=jnp.int32), shape(TASKS + 128, kind=jnp.int32)),
            in_specs=[SMEM, VMEM, VMEM],
            out_specs=(VMEM, SMEM, SMEM),
            scratch_shapes=lists(8),
            compiler_params=small,
            name="send",
        )(number, rec_t, rec_x)

    def to_do(number):
        return pl.pallas_call(
            tasks_kernel,
            out_shape=shape(TASKS + 128, kind=jnp.int32),
            in_specs=[SMEM, VMEM],
            out_specs=SMEM,
            scratch_shapes=lists(16) + [pltpu.SMEM((TASKS + 128,), jnp.int32)],
            compiler_params=small,
            cost_estimate=cost(1),
            name="tasks",
        )(number, rec_t)

    def add_near(rec_z, tasks, so_far):
        return pl.pallas_call(
            near_kernel,
            out_shape=(shape(3, seg_count), shape(devices, BLK)),
            in_specs=[VMEM, SMEM, VMEM, VMEM, VMEM],
            out_specs=(VMEM, VMEM),
            scratch_shapes=[sides, sums],
            compiler_params=small,
            name="near",
        )(rec_z, tasks, own, so_far, mob)

    def more(carry):
        left, so_far = carry
        number = left - 1
        send = to_send(number)[0].reshape(NZ, SECT, BLK)
        late = to_do(number)
        z = lax.axis_index("z")
        got = jnp.zeros_like(send)
        for k in range(1, NZ):
            part = lax.dynamic_index_in_dim(send, (z + k) % NZ, 0, keepdims=True)
            part = lax.ppermute(part, "z", [(i, (i + k) % NZ) for i in range(NZ)])
            got = lax.dynamic_update_slice_in_dim(got, part, (z + NZ - k) % NZ, 0)
        return number, add_near(got.reshape(NZ * SECT, BLK), late, so_far)[0]

    def beside(carry):
        turn, so_far, _, moments = carry
        groups = [moments] + [lax.ppermute(moments, "y", [(i, (i + k) % 4) for i in range(4)]) for k in range(1, 4)]
        some, rounds, tasks = pl.pallas_call(
            row_pairs_kernel,
            out_shape=(shape(3, seg_count), shape(1, kind=jnp.int32), shape(TASKS + 128, kind=jnp.int32)),
            in_specs=[VMEM] * 4,
            out_specs=(VMEM, SMEM, SMEM),
            scratch_shapes=[sides, sums] + lists(16) + [pltpu.SMEM((TASKS + 128,), jnp.int32)],
            compiler_params=small,
            cost_estimate=cost(4 * 10**9),
            name="row_pairs",
        )(own, rec_t, rec_x, so_far)
        home = pl.pallas_call(
            far_kernel,
            out_shape=shape(3, seg_count),
            in_specs=[VMEM] * 5 + [SMEM, VMEM, VMEM],
            out_specs=VMEM,
            scratch_shapes=[pltpu.VMEM((2, 3, BLK, BLK), F32), sides, sums],
            compiler_params=small,
            cost_estimate=cost(1),
            name="far",
        )(own, *groups, cells, cell_centers, some)
        _, home = lax.while_loop(lambda c: c[0][0] > 1, more, (rounds, home))
        return turn + 1, home, tasks, groups[1]

    both = jnp.concatenate([group, lax.ppermute(group, "c", [(0, 1), (1, 0)])], axis=0)
    first = jnp.zeros((1,), jnp.int32)
    send, start, no_tasks = to_send(first)
    rec_z = lax.all_to_all(send.reshape(NZ, SECT, BLK), "z", 0, 0, tiled=True)
    _, home, tasks, _ = lax.while_loop(lambda c: c[0][0] < 1, beside, (start, same, no_tasks, both))
    forces, tops = add_near(rec_z.reshape(NZ * SECT, BLK), tasks, home)
    tops = lax.all_to_all(tops.reshape(devices, 1, BLK), ("y", "c", "z", "x"), 0, 0, tiled=True)
    displacement = pl.pallas_call(
        step_kernel,
        out_shape=shape(3, seg_count),
        in_specs=[VMEM, VMEM, VMEM],
        out_specs=VMEM,
        compiler_params=small,
        name="step",
    )(tops.reshape(devices, BLK), forces, mob)
    return forces, displacement


def solution(mesh):
    names = ("y", "c", "z", "x")
    fine = Mesh(mesh.devices.reshape(NG // 2, 2, NZ, NX), names)
    in_specs = (P(None, names), P(names, None), P(names), P(names), P())
    out_specs = (P(None, names), P(None, names))
    return jax.shard_map(body, mesh=fine, in_specs=in_specs, out_specs=out_specs, check_vma=False)
```

```python
import jax
import jax.numpy as jnp
from jax import lax
from jax.experimental import pallas as pl
from jax.experimental.pallas import tpu as pltpu
from jax.sharding import Mesh
from jax.sharding import PartitionSpec as P

NEAR_CORE = 0.25
FAR_CORE = 1.0
STEP_LIMIT = 0.5
BLK = 128
NB = 16
NZ = 8
NX = 4
NG = 8
EXTRA = 9 * NB
ROWS = EXTRA + 8
CAP = 13
SECT = 9 * CAP + 3
TASKS = 2048
COUNT = TASKS + 64
PAD = 1 << 16
F32 = jnp.float32
BF16 = jnp.bfloat16
VMEM = pl.BlockSpec(memory_space=pltpu.VMEM)
SMEM = pl.BlockSpec(memory_space=pltpu.SMEM)
NT = (((1,), (1,)), ((), ()))


def lanes(rows):
    return lax.broadcasted_iota(jnp.int32, (rows, BLK), 1)


def subs(rows):
    return lax.broadcasted_iota(jnp.int32, (rows, BLK), 0)


def split(x):
    one = x.astype(BF16)
    rest = x - one.astype(F32)
    two = rest.astype(BF16)
    three = (rest - two.astype(F32)).astype(BF16)
    return one, two, three


def pack_kernel(seg, cells, pairs, packed, out, same_cells):
    for k in range(NB):
        cols = slice(k * BLK, (k + 1) * BLK)
        out[pl.ds(k, 8, stride=NB), :] = seg[0:8, cols]
        out[8 * NB + k : 8 * NB + k + 1, :] = seg[8:9, cols]
    row = subs(NB)
    cell = jnp.zeros((NB, BLK), jnp.int32)
    for k in range(NB):
        cell = jnp.where(row == k, cells[k] & 31, cell)
        same_cells[k] = cells[k]
    hot = (lanes(NB) == cell + 64).astype(F32)
    hot_last = (lanes(NB) == cell + 96).astype(F32)
    rows = []
    for q in range(3):
        for r in range(3):
            outer = out[(6 + q) * NB : (7 + q) * NB, :] * out[(3 + r) * NB : (4 + r) * NB, :]
            total = jnp.sum(outer, axis=1, keepdims=True)
            rows.append(jnp.sum(total * (hot_last if q + r == 4 else hot), axis=0, keepdims=True))
    out[EXTRA : EXTRA + 1, :] = rows[0] + rows[8]
    for r in range(1, 8):
        out[EXTRA + r : EXTRA + r + 1, :] = rows[r]
    out[EXTRA : EXTRA + 2, 0:32] = pairs[...].astype(F32)
    whole = out[...]
    for copy in range(NX):
        packed[copy * ROWS : (copy + 1) * ROWS, :] = whole


def row_kernel(*refs):
    out = refs[NX]
    lane = lanes(8)
    rest = [jnp.zeros((8 - NX, BLK), F32)]
    first = jnp.concatenate([ref[0:1, :] for ref in refs[:NX]] + rest, axis=0)
    second = jnp.concatenate([ref[1:2, :] for ref in refs[:NX]] + rest, axis=0)
    total = refs[0][...]
    for ref in refs[1:NX]:
        total = total + ref[...]
    tile = jnp.where(lane < 32, first, jnp.where(lane < 64, pltpu.roll(second, 32, 1), total))
    for copy in range(NZ):
        out[8 * copy : 8 * copy + 8, :] = tile


def group_pairs(rec_t):
    lane = lanes(8)
    a = jnp.zeros((8, BLK), F32)
    b = jnp.zeros((8, BLK), F32)
    for x in range(NX):
        part = rec_t[pl.ds(x, NZ, stride=8), :]
        one = jnp.where(lane < 32, part, 0.0)
        two = jnp.where((lane >= 32) & (lane < 64), part, 0.0)
        a = a + (pltpu.roll(one, 32 * x, 1) if x else one)
        b = b + (pltpu.roll(two, (32 * x + 96) % 128, 1) if x != 1 else two)
    return a.astype(jnp.int32), b.astype(jnp.int32)


def list_hits(hit, code, lst, smem, sem):
    rows = hit.shape[0]
    hits = hit.astype(F32)
    hot = jnp.concatenate([hits, jnp.zeros((16 - rows, BLK), F32)], axis=0) if rows < 16 else hits
    hot = hot.astype(BF16)
    sq_row, sq_lane = subs(BLK), lanes(BLK)
    inside = jnp.dot(hot, (sq_row < sq_lane).astype(BF16), preferred_element_type=F32)
    totals = jnp.dot(hot, jnp.ones((BLK, BLK), BF16), preferred_element_type=F32)
    before = jnp.zeros((16, BLK), F32)
    running = jnp.zeros((1, BLK), F32)
    for s in range(rows):
        before = jnp.where(subs(16) == s, running, before)
        running = running + totals[s : s + 1, :]
    count = jnp.max(running).astype(jnp.int32)
    rank = jnp.where(hits > 0.0, (inside + before)[0:rows, :], -1.0)
    code = code.astype(F32)

    def listing(chunk, carry):
        slot = (sq_row + chunk * BLK).astype(F32)
        found = jnp.zeros((BLK, BLK), F32)
        for c in range(rows):
            found = found + jnp.where(rank[c : c + 1, :] == slot, code[c : c + 1, :], 0.0)
        lst[pl.ds(chunk, 1), :] = jnp.sum(found.T, axis=0, keepdims=True).astype(jnp.int32)
        return carry

    listing(0, 0)
    lax.fori_loop(1, (count + BLK - 1) // BLK, listing, 0)
    copy = pltpu.make_async_copy(lst, smem, sem)
    copy.start()
    return copy, count


def send_kernel(turn_no, rec_t, rec_x, send, start, none, lst, smem, cnt, sem):
    start[0] = 0
    none[COUNT] = 0
    zz = lax.axis_index("z")
    xx = lax.axis_index("x")
    rnd = turn_no[0]
    ai, bi = group_pairs(rec_t)
    za, zb = ai >> 6, bi >> 6
    to_a = (za != zz) & (((ai >> 4) & 3) == xx) & (zb == zz)
    to_b = (zb != zz) & (((bi >> 4) & 3) == xx) & (za == zz)
    code = jnp.where(to_a, za * 512 + bi, zb * 512 + ai)
    copy, count = list_hits((to_a & (ai >= 0)) | (to_b & (bi >= 0)), code, lst, smem, sem)
    send[...] = jnp.zeros_like(send)
    for z in range(NZ):
        cnt[z] = 0
    copy.wait()

    def deliver(i, carry):
        entry = smem[i >> 7, i & 127]
        f = entry & 511
        z = entry >> 9
        slot = cnt[z] - rnd * CAP
        cnt[z] = cnt[z] + 1

        @pl.when((slot >= 0) & (slot < CAP))
        def _():
            source = ((f >> 4) & 3) * ROWS + (f & 15)
            target = z * SECT + slot
            send[pl.ds(target, 8, stride=CAP), :] = rec_x[pl.ds(source, 8, stride=NB), :]
            send[pl.ds(target + 8 * CAP, 1), :] = rec_x[pl.ds(source + 8 * NB, 1), :]

        return carry

    lax.fori_loop(0, count, deliver, 0)


def rounds_needed(ai, bi):
    own_a, own_b = ai >> 4, bi >> 4
    owner, column = [], []
    for here, there in ((own_a, own_b), (own_b, own_a)):
        for i in range(8):
            owner.append((subs(32) == here[i : i + 1, :]).astype(BF16))
            column.append((subs(16) == (there[i : i + 1, :] >> 2)).astype(BF16))
    owner, column = jnp.concatenate(owner, axis=1), jnp.concatenate(column, axis=1)
    need = lax.dot_general(owner, column, NT, preferred_element_type=F32)
    r32 = lax.broadcasted_iota(jnp.int32, (32, 16), 0)
    c32 = lax.broadcasted_iota(jnp.int32, (32, 16), 1)
    longest = jnp.max(jnp.where((r32 >> 2) == c32, 0.0, need)).astype(jnp.int32)
    return (longest + CAP - 1) // CAP


def list_tasks(rec_t, lst, smem, sem):
    me = lax.axis_index("z") * NX + lax.axis_index("x")
    ai, bi = group_pairs(rec_t)
    fa, fb = (ai >> 4) == me, (bi >> 4) == me
    swapped = (bi & 15) * 512 + ai
    hits = jnp.concatenate([(fa | fb).astype(F32), (fa & fb).astype(F32)], axis=0)
    code = jnp.concatenate([jnp.where(fa, (ai & 15) * 512 + bi, swapped), swapped], axis=0)
    return list_hits(hits > 0.0, code, lst, smem, sem)


def place_tasks(rnd, count, local, tasks, smem, cnt):
    zz = lax.axis_index("z")
    for z in range(NZ):
        cnt[z] = 0

    def receive(i, carry):
        at_local, at = carry
        entry = smem[i >> 7, i & 127]
        f = entry & 511
        k = (entry >> 9) << 12
        z = f >> 6
        here = z == zz
        slot = cnt[z] - rnd * CAP
        cnt[z] = cnt[z] + 1
        local[at_local] = (((f >> 4) & 3) * ROWS + (f & 15)) | k
        tasks[at] = (z * SECT + slot) | k
        use = jnp.logical_not(here) & (slot >= 0) & (slot < CAP)
        return at_local + here.astype(jnp.int32), at + use.astype(jnp.int32)

    used_local, used = lax.fori_loop(0, count, receive, (0, 0))
    for u in range(8):
        local[used_local + u] = PAD
        tasks[used + u] = PAD
    tasks[COUNT] = used
    return used_local


def run_tasks(listed, count, unroll, blocks, apart, own, sides, acc):
    columns = point_columns()

    def step(i, carry):
        for u in range(unroll):
            entry = listed[unroll * i + u]
            base = entry & 4095
            k = (entry >> 12) & 15

            def row(r):
                return blocks[pl.ds(base + r * apart, 1), :]

            here = [own[pl.ds(a * NB + k, 1), :] for a in range(3)]
            near = source_pull(row, jnp.where(entry >= PAD, 0, 9), sides[k], here, columns)
            for a in range(3):
                acc[k, a] = acc[k, a] + near[a]
        return carry

    lax.fori_loop(0, (count + unroll - 1) // unroll, step, 0)


def tasks_kernel(turn_no, rec_t, tasks, lst, smem, cnt, sem, local):
    copy, count = list_tasks(rec_t, lst, smem, sem)
    copy.wait()
    place_tasks(turn_no[0], count, local, tasks, smem, cnt)


def outer_rows(row, symmetric):
    s = subs(16)
    t = [jnp.broadcast_to(row(3 + r), (16, BLK)) for r in range(3)]
    b = [jnp.broadcast_to(row(6 + q), (16, BLK)) for q in range(3)]

    def slow(v):
        return jnp.where(s < 3, v[0], jnp.where(s < 6, v[1], v[2]))

    def fast(v):
        first = (s == 0) | (s == 3) | (s == 6)
        return jnp.where(first, v[0], jnp.where((s == 1) | (s == 4) | (s == 7), v[1], v[2]))

    o = slow(b) * fast(t)
    return o + 0.5 * (fast(b) * slow(t)) if symmetric else o


def other_side(rows, points):
    one, two, three = [x.astype(F32) for x in split(rows)]
    points = jnp.concatenate(points + [jnp.zeros((29, BLK), F32)], axis=0)
    return jnp.concatenate([one, two, one, three, two, one, points], axis=0).T


def own_side(row):
    o = jnp.where(subs(16) < 9, outer_rows(row, False), 0.0)
    one, two, three = split(o)
    return jnp.concatenate([one, one, two, one, two, three, jnp.zeros((32, BLK), BF16)], axis=0)


def own_sides(own, sides):
    for k in range(NB):
        sides[k] = own_side(lambda r: own[r * NB + k : r * NB + k + 1, :])


def spread(turned):
    return [jnp.broadcast_to(turned[:, 96 + a : 97 + a], (BLK, BLK)) for a in range(3)]


def fold(v):
    total = v[0:8, :]
    for i in range(1, BLK // 8):
        total = total + v[8 * i : 8 * i + 8, :]
    return total


def pull(other, there, mine, here, core, drop=None):
    c = jnp.dot(other, mine, preferred_element_type=F32)
    if drop is not None:
        c = jnp.where(subs(BLK) == drop, 0.0, c)
    d = [here[a] - there[a] for a in range(3)]
    inv = lax.rsqrt(d[0] * d[0] + d[1] * d[1] + (d[2] * d[2] + core))
    w = c * (inv * inv * inv)
    return [fold(w * d[a]) for a in range(3)]


def point_columns():
    row = lax.broadcasted_iota(jnp.int32, (BLK, 3 * BLK), 0) - 96
    axis = lax.broadcasted_iota(jnp.int32, (BLK, 3 * BLK), 1) // BLK
    return ((row == axis) | (row == axis + 3) | (row == axis + 6)).astype(BF16)


def source_pull(row, limit, mine, here, columns):
    rows = jnp.where(subs(16) < limit, outer_rows(row, True), 0.0)
    one, two, three = split(rows)
    s = subs(16)
    p = [row(a) for a in range(3)]
    points = jnp.concatenate(p + p + p + [jnp.zeros((7, BLK), F32)], axis=0)
    p1, p2, p3 = [x.astype(F32) for x in split(points)]
    pieces = jnp.where(s < 3, p1, jnp.where(s < 6, p2, p3)).astype(BF16)
    side = jnp.concatenate([one, two, one, three, two, one, pieces, jnp.zeros((16, BLK), BF16)], axis=0).T
    spots = jnp.dot(side, columns, preferred_element_type=F32)
    there = [spots[:, a * BLK : (a + 1) * BLK] for a in range(3)]
    return pull(side, there, mine, here, NEAR_CORE)


def write_forces(acc, forces, so_far=None):
    for k in range(NB):
        cols = slice(k * BLK, (k + 1) * BLK)
        rows = jnp.concatenate([jnp.sum(acc[k, a], axis=0, keepdims=True) for a in range(3)], axis=0)
        forces[:, cols] = rows if so_far is None else so_far[:, cols] + rows


def own_kernel(own, forces, acc):
    columns = point_columns()

    def step(i, carry):
        for u in range(4):
            k = 4 * i + u

            def row(r):
                return own[pl.ds(r * NB + k, 1), :]

            same = source_pull(row, 9, own_side(row), [row(a) for a in range(3)], columns)
            for a in range(3):
                acc[k, a] = same[a]
        return carry

    lax.fori_loop(0, NB // 4, step, 0)
    write_forces(acc, forces)


def row_pairs_kernel(own, rec_t, rec_x, so_far, forces, rounds, tasks, sides, acc, lst, smem, cnt, sem, local):
    copy, count = list_tasks(rec_t, lst, smem, sem)
    rounds[0] = rounds_needed(*group_pairs(rec_t))
    own_sides(own, sides)
    acc[...] = jnp.zeros_like(acc)
    copy.wait()
    used = place_tasks(0, count, local, tasks, smem, cnt)
    run_tasks(local, used, 4, rec_x, NB, own, sides, acc)
    write_forces(acc, forces, so_far)


def far_kernel(own, m0, m1, m2, m3, cells, centers, so_far, forces, there, sides, acc):
    lane = lanes(8)
    parts = []
    for i, ref in enumerate((m0, m1, m2, m3)):
        for h in range(2):
            y = (lax.axis_index("y") + 4 - i) & 3
            c = lax.axis_index("c")
            at = 32 * ((2 * y + (1 - c if h else c)) & 3)
            tile = ref[8 * h : 8 * h + 8, :]
            low = pltpu.roll(jnp.where((lane >= 64) & (lane < 96), tile, 0.0), (at + 64) & 127, 1)
            high = pltpu.roll(jnp.where(lane >= 96, tile, 0.0), (at + 32) & 127, 1)
            parts.append((y >> 1, low, high))
    others = []
    for half in range(2):
        rows = jnp.zeros((8, BLK), F32)
        last = jnp.zeros((8, BLK), F32)
        for which, low, high in parts:
            rows = rows + jnp.where(which == half, low, 0.0)
            last = last + jnp.where(which == half, high, 0.0)
        rows = jnp.concatenate([rows, last[0:1, :], jnp.zeros((7, BLK), F32)], axis=0)
        cols = slice(half * BLK, (half + 1) * BLK)
        turned = other_side(rows, [centers[a : a + 1, cols] for a in range(3)])
        others.append(turned.astype(BF16))
        for a, point in enumerate(spread(turned)):
            there[half, a] = point
    own_sides(own, sides)

    def step(i, carry):
        for u in range(4):
            k = 4 * i + u
            here = [own[pl.ds(a * NB + k, 1), :] for a in range(3)]
            parts = [
                pull(others[h], [there[h, a] for a in range(3)], sides[k], here, FAR_CORE, cells[k] - h * BLK)
                for h in range(2)
            ]
            for a in range(3):
                acc[k, a] = parts[0][a] + parts[1][a]
        return carry

    lax.fori_loop(0, NB // 4, step, 0)
    write_forces(acc, forces, so_far)


def near_kernel(rec_z, tasks, own, so_far, mobility, forces, tops, sides, acc):
    acc[...] = jnp.zeros_like(acc)
    own_sides(own, sides)
    run_tasks(tasks, tasks[COUNT], 8, rec_z, CAP, own, sides, acc)
    write_forces(acc, forces, so_far)
    v = mobility[...] * forces[...]
    speed = jnp.sum(v * v, axis=0, keepdims=True)
    tops[...] = jnp.broadcast_to(jnp.max(speed, axis=1, keepdims=True), tops.shape)


def step_kernel(tops, forces, mobility, out):
    best = jnp.max(jnp.max(tops[...], axis=0, keepdims=True), axis=1, keepdims=True)
    scale = STEP_LIMIT / (jnp.sqrt(best) + 1e-06)
    out[...] = scale * (mobility[...] * forces[...])


def shape(*dims, kind=F32):
    return jax.ShapeDtypeStruct(dims, kind)


def cost(flops):
    return pl.CostEstimate(flops=flops, bytes_accessed=1, transcendentals=0)


def body(segments, pair_blocks, block_cells, mobility, cell_centers):
    small = pltpu.CompilerParams(vmem_limit_bytes=6 * 1024 * 1024)
    seg_count = segments.shape[1]
    devices = 8 * NG * NX
    mob = mobility[None, :]
    packed, own, cells = pl.pallas_call(
        pack_kernel,
        out_shape=(shape(NX * ROWS, BLK), shape(ROWS, BLK), shape(NB, kind=jnp.int32)),
        in_specs=[VMEM, SMEM, VMEM],
        out_specs=(VMEM, VMEM, SMEM),
        name="pack",
    )(segments, block_cells, pair_blocks.T)
    rec_x = lax.all_to_all(packed.reshape(NX, ROWS, BLK), "x", 0, 0, tiled=True).reshape(NX * ROWS, BLK)
    sides = pltpu.VMEM((NB, BLK, BLK), BF16)
    sums = pltpu.VMEM((NB, 3, 8, BLK), F32)
    same = pl.pallas_call(
        own_kernel,
        out_shape=shape(3, seg_count),
        in_specs=[VMEM],
        out_specs=VMEM,
        scratch_shapes=[sums],
        compiler_params=small,
        cost_estimate=cost(10**9),
        name="own",
    )(own)
    rec_x, same = lax.optimization_barrier((rec_x, same))
    row = pl.pallas_call(
        row_kernel,
        out_shape=shape(NZ * 8, BLK),
        grid=(1,),
        in_specs=[pl.BlockSpec((8, BLK), lambda i, s=s: ((s * ROWS + EXTRA) // 8, 0)) for s in range(NX)],
        out_specs=pl.BlockSpec((NZ * 8, BLK), lambda i: (0, 0)),
        compiler_params=small,
        name="row",
    )(*([rec_x] * NX))
    rec_t = lax.all_to_all(row.reshape(NZ, 8, BLK), "z", 0, 0, tiled=True)
    group = jnp.sum(rec_t, axis=0)
    rec_t = rec_t.reshape(NZ * 8, BLK)

    def lists(rows):
        return [
            pltpu.VMEM((rows, BLK), jnp.int32),
            pltpu.SMEM((rows, BLK), jnp.int32),
            pltpu.SMEM((NZ,), jnp.int32),
            pltpu.SemaphoreType.DMA,
        ]

    def to_send(number):
        return pl.pallas_call(
            send_kernel,
            out_shape=(shape(NZ * SECT, BLK), shape(1, kind=jnp.int32), shape(TASKS + 128, kind=jnp.int32)),
            in_specs=[SMEM, VMEM, VMEM],
            out_specs=(VMEM, SMEM, SMEM),
            scratch_shapes=lists(8),
            compiler_params=small,
            name="send",
        )(number, rec_t, rec_x)

    def to_do(number):
        return pl.pallas_call(
            tasks_kernel,
            out_shape=shape(TASKS + 128, kind=jnp.int32),
            in_specs=[SMEM, VMEM],
            out_specs=SMEM,
            scratch_shapes=lists(16) + [pltpu.SMEM((TASKS + 128,), jnp.int32)],
            compiler_params=small,
            cost_estimate=cost(1),
            name="tasks",
        )(number, rec_t)

    def add_near(rec_z, tasks, so_far):
        return pl.pallas_call(
            near_kernel,
            out_shape=(shape(3, seg_count), shape(devices, BLK)),
            in_specs=[VMEM, SMEM, VMEM, VMEM, VMEM],
            out_specs=(VMEM, VMEM),
            scratch_shapes=[sides, sums],
            compiler_params=small,
            name="near",
        )(rec_z, tasks, own, so_far, mob)

    def more(carry):
        left, so_far = carry
        number = left - 1
        send = to_send(number)[0].reshape(NZ, SECT, BLK)
        late = to_do(number)
        z = lax.axis_index("z")
        got = jnp.zeros_like(send)
        for k in range(1, NZ):
            part = lax.dynamic_index_in_dim(send, (z + k) % NZ, 0, keepdims=True)
            part = lax.ppermute(part, "z", [(i, (i + k) % NZ) for i in range(NZ)])
            got = lax.dynamic_update_slice_in_dim(got, part, (z + NZ - k) % NZ, 0)
        return number, add_near(got.reshape(NZ * SECT, BLK), late, so_far)[0]

    def beside(carry):
        turn, so_far, _, moments = carry
        groups = [moments] + [lax.ppermute(moments, "y", [(i, (i + k) % 4) for i in range(4)]) for k in range(1, 4)]
        some, rounds, tasks = pl.pallas_call(
            row_pairs_kernel,
            out_shape=(shape(3, seg_count), shape(1, kind=jnp.int32), shape(TASKS + 128, kind=jnp.int32)),
            in_specs=[VMEM] * 4,
            out_specs=(VMEM, SMEM, SMEM),
            scratch_shapes=[sides, sums] + lists(16) + [pltpu.SMEM((TASKS + 128,), jnp.int32)],
            compiler_params=small,
            cost_estimate=cost(4 * 10**9),
            name="row_pairs",
        )(own, rec_t, rec_x, so_far)
        home = pl.pallas_call(
            far_kernel,
            out_shape=shape(3, seg_count),
            in_specs=[VMEM] * 5 + [SMEM, VMEM, VMEM],
            out_specs=VMEM,
            scratch_shapes=[pltpu.VMEM((2, 3, BLK, BLK), F32), sides, sums],
            compiler_params=small,
            cost_estimate=cost(1),
            name="far",
        )(own, *groups, cells, cell_centers, some)
        _, home = lax.while_loop(lambda c: c[0][0] > 1, more, (rounds, home))
        return turn + 1, home, tasks, groups[1]

    both = jnp.concatenate([group, lax.ppermute(group, "c", [(0, 1), (1, 0)])], axis=0)
    first = jnp.zeros((1,), jnp.int32)
    send, start, no_tasks = to_send(first)
    rec_z = lax.all_to_all(send.reshape(NZ, SECT, BLK), "z", 0, 0, tiled=True)
    _, home, tasks, _ = lax.while_loop(lambda c: c[0][0] < 1, beside, (start, same, no_tasks, both))
    forces, tops = add_near(rec_z.reshape(NZ * SECT, BLK), tasks, home)
    tops = lax.all_to_all(tops.reshape(devices, 1, BLK), ("y", "c", "z", "x"), 0, 0, tiled=True)
    displacement = pl.pallas_call(
        step_kernel,
        out_shape=shape(3, seg_count),
        in_specs=[VMEM, VMEM, VMEM],
        out_specs=VMEM,
        compiler_params=small,
        name="step",
    )(tops.reshape(devices, BLK), forces, mob)
    return forces, displacement


def solution(mesh):
    names = ("y", "c", "z", "x")
    fine = Mesh(mesh.devices.reshape(NG // 2, 2, NZ, NX), names)
    in_specs = (P(None, names), P(names, None), P(names), P(names), P())
    out_specs = (P(None, names), P(None, names))
    return jax.shard_map(body, mesh=fine, in_specs=in_specs, out_specs=out_specs, check_vma=False)
```
